32 devices in a mesh: gx: 8 (over y, x, core), gy: 4 (over z).
Axes of the slice: x: 2, y: 2, z: 4, core: 2. Of those that a mesh axis runs over, the one named last changes fastest.
Arguments:
- source: float32 [64, 64, 256], P('gx', 'gy'), may hold values from -6 to 6
- initial: float32 [64, 64, 256], P('gx', 'gy'), may hold values from -6 to 6
- absorption: float32 [64, 64, 256], P('gx', 'gy'), may hold values from 0.01 to 0.2
- beta_x: float32 [64, 64, 256], P('gx', 'gy'), may hold values from 0.4 to 2.5
- beta_y: float32 [64, 64, 256], P('gx', 'gy'), may hold values from 0.4 to 2.5
- beta_z: float32 [64, 64, 256], P('gx', 'gy'), may hold values from 0.4 to 2.5
Outputs:
- solution: float32 [64, 64, 256], P('gx', 'gy')
The draws below stay inside these ranges and needn't reach their ends.
All inputs are finite; a program needn't handle non-finite values.
Results may differ from the reference program's by a relative error of at most 0.00002.
Values sent between devices are 32-bit elements; how exact they have to be, the bound alone decides.
No kernel may reach another device: no remote copies, remote signals or barrier semaphores. Data moves between devices by JAX's collectives and lax.ppermute only.
A program may use at most 64 MiB of HBM per device.

```python
import math
import jax
import jax.numpy as jnp

NZ = 256
SWEEPS = 4
COARSE_SWEEPS = 8
NX = 64
NY = 64


def log_spread(key, low, high):
    values = jnp.exp(jax.random.uniform(key, (NX, NY, NZ), jnp.float32, math.log(low), math.log(high)))
    return jnp.clip(values, low, high)


def draw_absorption(key, part):
    own_key = jax.random.fold_in(key, 101)
    return log_spread(own_key, 0.01, 0.2)


def draw_beta_x(key, part):
    own_key = jax.random.fold_in(key, 202)
    return log_spread(own_key, 0.4, 2.5)


def draw_beta_y(key, part):
    own_key = jax.random.fold_in(key, 303)
    return log_spread(own_key, 0.4, 2.5)


def draw_beta_z(key, part):
    own_key = jax.random.fold_in(key, 404)
    return log_spread(own_key, 0.4, 2.5)


def steps_of(key, dims, split, low, high):
    def one(dim, parts):
        heights = jax.random.uniform(jax.random.fold_in(jax.random.fold_in(key, 6), dim), (parts,), jnp.float32, low / len(split), high / len(split))
        return jnp.repeat(jnp.exp(heights), dims[dim] // parts).reshape((-1,) + (1,) * (len(dims) - dim - 1))

    gain = one(*split[0])
    for cut in split[1:]:
        gain = gain * one(*cut)
    return gain


def noise(rng, shape, scale, limit, cuts=(), kind=jnp.bfloat16):
    entries = jax.random.normal(rng, shape, jnp.float32) * scale
    if len(cuts) > 0:
        entries = steps_of(rng, shape, cuts, -0.22, 0.18) * entries
    return jnp.clip(entries, min=-limit, max=limit).astype(kind)


def setup_inputs(seed: int = 0) -> dict:
    key_list = jax.random.split(jax.random.key(seed), 7)
    return {
        "source": noise(key_list[0], (NX, NY, NZ), 1.0, 6.0, ((0, 8), (1, 4)), jnp.float32),
        "initial": noise(key_list[1], (NX, NY, NZ), 1.0, 6.0, ((0, 8), (1, 4)), jnp.float32),
        "absorption": draw_absorption(jax.random.fold_in(key_list[6], 71), 0),
        "beta_x": draw_beta_x(jax.random.fold_in(key_list[6], 71), 0),
        "beta_y": draw_beta_y(jax.random.fold_in(key_list[6], 71), 0),
        "beta_z": draw_beta_z(jax.random.fold_in(key_list[6], 71), 0),
    }


def restrict_cells(field):
    size_x, size_y, size_z = field.shape
    return field.reshape(size_x // 2, 2, size_y // 2, 2, size_z // 2, 2).mean(axis=(1, 3, 5))


def restrict_faces(face_x, face_y, face_z):
    lower_x = face_x[0::2]
    size_x, size_y, size_z = lower_x.shape
    coarse_x = lower_x.reshape(size_x, size_y // 2, 2, size_z // 2, 2).mean(axis=(2, 4))
    lower_y = face_y[:, 0::2]
    size_x, size_y, size_z = lower_y.shape
    coarse_y = lower_y.reshape(size_x // 2, 2, size_y, size_z // 2, 2).mean(axis=(1, 4))
    lower_z = face_z[:, :, 0::2]
    size_x, size_y, size_z = lower_z.shape
    coarse_z = lower_z.reshape(size_x // 2, 2, size_y // 2, 2, size_z).mean(axis=(1, 3))
    return coarse_x, coarse_y, coarse_z


def prolong_cells(field):
    return jnp.repeat(jnp.repeat(jnp.repeat(field, 2, axis=0), 2, axis=1), 2, axis=2)


def level_coeffs(absorb, face_xl, face_yl, face_zl, stencil_scale):
    face_xh = jnp.roll(face_xl, -1, axis=0)
    face_yh = jnp.roll(face_yl, -1, axis=1)
    face_zh = jnp.concatenate([face_zl[:, :, 1:], jnp.zeros_like(face_zl[:, :, :1])], axis=2)
    diagonal = absorb + stencil_scale * (face_xl + face_xh + face_yl + face_yh + face_zl + face_zh)
    return (absorb, face_xl, face_xh, face_yl, face_yh, face_zl, face_zh, diagonal, stencil_scale)


def rolled(field):
    return (jnp.roll(field, 1, axis=0), jnp.roll(field, -1, axis=0),
            jnp.roll(field, 1, axis=1), jnp.roll(field, -1, axis=1))


def apply_operator(field, coeffs, lower_x, upper_x, lower_y, upper_y):
    absorb, face_xl, face_xh, face_yl, face_yh, face_zl, face_zh, diagonal, stencil_scale = coeffs
    zeros_plane = jnp.zeros_like(field[:, :, :1])
    lower_z = jnp.concatenate([zeros_plane, field[:, :, :-1]], axis=2)
    upper_z = jnp.concatenate([field[:, :, 1:], zeros_plane], axis=2)
    flux = (face_xl * (field - lower_x) + face_xh * (field - upper_x)
            + face_yl * (field - lower_y) + face_yh * (field - upper_y)
            + face_zl * (field - lower_z) + face_zh * (field - upper_z))
    return absorb * field + stencil_scale * flux


def chebyshev_weights(sweeps):
    cheb_theta = 1.125
    cheb_delta = 0.875
    cheb_sigma = cheb_theta / cheb_delta
    rho_old = 1.0 / cheb_sigma
    weights = [(0.0, 1.0 / cheb_theta)]
    for sweep in range(1, sweeps):
        rho_new = 1.0 / (2.0 * cheb_sigma - rho_old)
        weights.append((rho_new * rho_old, 2.0 * rho_new / cheb_delta))
        rho_old = rho_new
    return weights


def chebyshev_smooth(iterate, target, coeffs, sweeps, zero_start):
    update = jnp.zeros_like(target)
    for sweep, pair in enumerate(chebyshev_weights(sweeps)):
        if sweep == 0 and zero_start:
            remain = target
        else:
            remain = target - apply_operator(iterate, coeffs, *rolled(iterate))
        update = pair[0] * update + pair[1] * remain / coeffs[7]
        iterate = iterate + update
    return iterate


def reference(source, initial, absorption, beta_x, beta_y, beta_z):
    coeffs_fine = level_coeffs(absorption, beta_x, beta_y, beta_z, 1.0)
    absorb_mid = restrict_cells(absorption)
    face_mid = restrict_faces(beta_x, beta_y, beta_z)
    coeffs_mid = level_coeffs(absorb_mid, face_mid[0], face_mid[1], face_mid[2], 0.25)
    absorb_low = restrict_cells(absorb_mid)
    face_low = restrict_faces(face_mid[0], face_mid[1], face_mid[2])
    coeffs_low = level_coeffs(absorb_low, face_low[0], face_low[1], face_low[2], 0.0625)

    fine_iter = chebyshev_smooth(initial, source, coeffs_fine, SWEEPS, False)
    fine_rest = source - apply_operator(fine_iter, coeffs_fine, *rolled(fine_iter))
    source_mid = restrict_cells(fine_rest)
    mid_iter = chebyshev_smooth(jnp.zeros_like(source_mid), source_mid, coeffs_mid, SWEEPS, True)
    mid_rest = source_mid - apply_operator(mid_iter, coeffs_mid, *rolled(mid_iter))
    source_low = restrict_cells(mid_rest)
    low_iter = chebyshev_smooth(jnp.zeros_like(source_low), source_low, coeffs_low, COARSE_SWEEPS, True)
    mid_iter = mid_iter + prolong_cells(low_iter)
    mid_iter = chebyshev_smooth(mid_iter, source_mid, coeffs_mid, SWEEPS, False)
    fine_iter = fine_iter + prolong_cells(mid_iter)
    return chebyshev_smooth(fine_iter, source, coeffs_fine, SWEEPS, False)
```

```python
import functools

import jax
import jax.numpy as jnp
from jax import lax
from jax.experimental import pallas as pl
from jax.experimental.pallas import tpu as pltpu
from jax.sharding import PartitionSpec as P

SWEEPS = 4
COARSE_SWEEPS = 8
F32 = jnp.float32
TILE = (8, 128)
PAD = 8
FINE = 5
MID = 6


def chebyshev_weights(sweeps):
    cheb_theta = 1.125
    cheb_delta = 0.875
    cheb_sigma = cheb_theta / cheb_delta
    rho_old = 1.0 / cheb_sigma
    weights = [(0.0, 1.0 / cheb_theta)]
    for sweep in range(1, sweeps):
        rho_new = 1.0 / (2.0 * cheb_sigma - rho_old)
        weights.append((rho_new * rho_old, 2.0 * rho_new / cheb_delta))
        rho_old = rho_new
    return weights


def iota(shape, axis):
    return lax.broadcasted_iota(jnp.int32, shape, axis)


def selector(rows, columns, hit):
    return jnp.where(hit(iota((rows, columns), 0), iota((rows, columns), 1)), 1.0, 0.0).astype(F32)


def pair_sum(size):
    return selector(size, size // 2, lambda k, m: k // 2 == m)


def pair_copy(size):
    return selector(size, 2 * size, lambda k, m: k == m // 2)


def dot(left, right):
    return lax.dot(left, right, precision=lax.Precision.HIGHEST, preferred_element_type=F32)


def roll(value, shift, axis):
    return pltpu.roll(value, shift % value.shape[axis], axis)


class Writer:
    def __init__(self, ref):
        self.ref, self.at = ref, 0

    def put(self, value):
        rows, columns = value.shape
        for r in range(0, rows, TILE[0]):
            for c in range(0, columns, TILE[1]):
                self.ref[self.at] = value[r : r + TILE[0], c : c + TILE[1]]
                self.at += 1


class Reader:
    def __init__(self, ref, at=0):
        self.ref, self.at = ref, at

    def get(self, rows, columns):
        lines = []
        for _ in range(rows // TILE[0]):
            parts = []
            for _ in range(columns // TILE[1]):
                parts.append(self.ref[self.at])
                self.at += 1
            lines.append(parts[0] if len(parts) == 1 else jnp.concatenate(parts, axis=1))
        return lines[0] if len(lines) == 1 else jnp.concatenate(lines, axis=0)


UP_PLANES = (5, 4, 4, 4, 4, 4)
DOWN_PLANES = (5, 4, 4, 5, 4, 4)
UP_CORNER = (4, 3, 3, 3, 4, 3)
DOWN_CORNER = (4, 3, 3, 4, 4, 3)


def tiles_of(rows, columns):
    return (rows // TILE[0]) * (columns // TILE[1])


def is_upper(width):
    return iota((TILE[0], width), 0) < TILE[0] // 2


def shifted(value, axis, step):
    count = lax.axis_size(axis)
    return lax.ppermute(value, axis, [(i, (i + step) % count) for i in range(count)])


def pack_kernel(
    ini, src, absorb, face_x, face_y, face_z, up_x, down_x, up_y, down_y, mid, low, rows_mid
):
    fields = (ini, src, absorb, face_x, face_y, face_z)
    size_x, size_y, size_z = ini.shape
    half = size_y // 2
    blocks = range(0, size_x, 2)

    def both_planes(ref):
        return [ref[plane] + ref[plane + 1] for plane in blocks]

    stacked = both_planes(absorb) + [face_x[plane] for plane in blocks] + both_planes(face_y)
    summed = dot(jnp.concatenate(stacked, axis=0), pair_sum(size_z))
    picked = dot(
        jnp.concatenate(both_planes(face_z), axis=0),
        selector(size_z, size_z // 2, lambda k, m: k == 2 * m),
    )
    count = summed.shape[0]
    rows_mid[:count] = summed
    rows_mid[count:] = picked
    out = Writer(mid)
    for array, (factor, sides) in enumerate(((0.125, 2), (0.25, 2), (0.25, 1), (0.25, 2))):
        lines = (size_x // 2) * half
        start = 2 * array * lines
        total = rows_mid[pl.ds(start, lines, 2), :]
        if sides == 2:
            total = total + rows_mid[pl.ds(start + 1, lines, 2), :]
        out.put(total * factor)

    mid_x, mid_z = size_x // 2, size_z // 2
    both = (0, 1)
    low_z = mid_z // 2

    def coarser(array, planes, sides):
        lines = []
        for block in range(mid_x // 2):
            total = None
            for plane in planes:
                for side in sides:
                    at = array * mid_x + 2 * block + plane
                    part = mid[at, pl.ds(side, half // 2, 2), :]
                    total = part if total is None else total + part
            lines.append(total)
        return jnp.concatenate(lines, axis=0)

    left = selector(mid_z, mid_z, lambda k, m: k // 2 == m)
    right = selector(mid_z, mid_z, lambda k, m: k // 2 == m - low_z)
    evens = selector(mid_z, mid_z, lambda k, m: k == 2 * m)
    low[0] = dot(coarser(0, both, both) * 0.125, right)
    low[1] = dot(coarser(1, (0,), both) * 0.25, left) + dot(coarser(2, both, (0,)) * 0.25, right)
    low[2] = dot(coarser(3, both, both) * 0.25, evens)

    tops, bottoms = Writer(up_x), Writer(down_x)
    for ref, count in zip(fields, UP_PLANES):
        for plane in range(size_x - count, size_x):
            tops.put(ref[plane])
    for ref, count in zip(fields, DOWN_PLANES):
        for plane in range(count):
            bottoms.put(ref[plane])

    upper = is_upper(size_z)
    tops_y, bottoms_y = Writer(up_y), Writer(down_y)
    for ref in fields:
        for pair in range(0, size_x, 2):
            one, two = ref[pair], ref[pair + 1]
            tops_y.put(jnp.where(upper, roll(one[size_y - 8 :], 4, 0), two[size_y - 8 :]))
            bottoms_y.put(jnp.where(upper, one[:8], roll(two[:8], 4, 0)))
    tops_y.put(ini[:, size_y - 5, :])
    bottoms_y.put(ini[:, 4, :])
    bottoms_y.put(face_y[:, 4, :])
    for writer in (tops, bottoms, tops_y, bottoms_y):
        for tile in range(mid.shape[0]):
            writer.put(mid[tile])


def corner_of(low_y, high_y, plane, upper, first_tile=0):
    width = upper.shape[1]
    at = first_tile + (plane // 2) * tiles_of(8, width)
    low = Reader(low_y, at).get(8, width)
    high = Reader(high_y, at).get(8, width)
    if plane % 2 == 0:
        return jnp.where(upper, low, roll(high, 4, 0))
    return jnp.where(upper, roll(low, 4, 0), high)


def corner_kernel(size_x, size_z, low_y, high_y, up, down):
    upper = is_upper(size_z)
    per_field = (size_x // 2) * tiles_of(8, size_z)
    tops, bottoms = Writer(up), Writer(down)
    for field in range(6):
        for plane in range(size_x - UP_CORNER[field], size_x):
            tops.put(corner_of(low_y, high_y, plane, upper, field * per_field))
        for plane in range(DOWN_CORNER[field]):
            bottoms.put(corner_of(low_y, high_y, plane, upper, field * per_field))
    mid_tiles = 4 * (size_x // 2)
    for writer in (tops, bottoms):
        for ref in (low_y, high_y):
            for tile in range(ref.shape[0] - mid_tiles, ref.shape[0]):
                writer.put(ref[tile])


def scale_coeffs(scale, absorb, face_x, face_y, face_z, coeffs, diagonal, planes):
    rows, lanes = absorb.shape[1:]
    lane = iota((rows, lanes), 1)

    def body(i, carry):
        xl, xh = face_x[i], face_x[i + 1]
        yl, zl = face_y[i], face_z[i]
        yh = roll(yl, -1, 0)
        zh = jnp.where(lane == lanes - 1, 0.0, roll(zl, -1, 1))
        diag = absorb[i] + scale * (xl + xh + yl + yh + zl + zh)
        inverse = 1.0 / diag
        scaled = scale * inverse
        coeffs[0, i] = scaled * xl
        coeffs[1, i] = scaled * xh
        coeffs[2, i] = scaled * yl
        coeffs[3, i] = scaled * yh
        coeffs[4, i] = jnp.where(lane == 0, 0.0, scaled * zl)
        coeffs[5, i] = scaled * zh
        coeffs[6, i] = inverse
        if diagonal is not None:
            diagonal[i] = diag
        return carry

    lax.fori_loop(*planes, body, 0)


def scaled_remain(coeffs, target, i, below, here, above):
    total = target[i] - here
    total = total + coeffs[0, i] * below + coeffs[1, i] * above
    total = total + coeffs[2, i] * roll(here, 1, 0) + coeffs[3, i] * roll(here, -1, 0)
    return total + coeffs[4, i] * roll(here, 1, 1) + coeffs[5, i] * roll(here, -1, 1)


def sweep_window(iterate, update, coeffs, target, planes, pair, first, unroll=1):
    start, stop = planes

    def body(i, carry):
        below, here = carry
        above = iterate[i + 1]
        step = pair[1] * scaled_remain(coeffs, target, i, below, here, above)
        if not first:
            step = step + pair[0] * update[i]
        update[i] = step
        iterate[i] = here + step
        return here, above

    lax.fori_loop(start, stop, body, (iterate[start - 1], iterate[start]), unroll=unroll)


def assemble_fine(window, own, low_x, high_x, low_y, high_y, low_c, high_c, up, down, up_c, down_c, starts):
    size_x, size_y, size_z = own.shape
    for plane in range(size_x):
        window[FINE + plane, PAD : PAD + size_y] = own[plane]
    reader = Reader(low_x, starts[0])
    for plane in range(up):
        window[FINE - up + plane, PAD : PAD + size_y] = reader.get(size_y, size_z)
    reader = Reader(high_x, starts[1])
    for plane in range(down):
        window[FINE + size_x + plane, PAD : PAD + size_y] = reader.get(size_y, size_z)
    high = PAD + size_y
    low_reader, high_reader = Reader(low_y, starts[2]), Reader(high_y, starts[3])
    for pair in range(0, size_x, 2):
        tile = low_reader.get(8, size_z)
        window[FINE + pair, 0:8] = roll(tile, 4, 0)
        window[FINE + pair + 1, 0:8] = tile
        tile = high_reader.get(8, size_z)
        window[FINE + pair, high : high + 8] = tile
        window[FINE + pair + 1, high : high + 8] = roll(tile, 4, 0)
    for ref, start, first, count in (
        (low_c, starts[4], FINE - up_c, up_c),
        (high_c, starts[5], FINE + size_x, down_c),
    ):
        reader = Reader(ref, start)
        for plane in range(count):
            tile = roll(reader.get(8, size_z), 4, 0)
            window[first + plane, 0:8] = tile
            window[first + plane, high : high + 8] = tile


def fine_kernel(
    ini, src, absorb, face_x, face_y, face_z, low_x, high_x, low_y, high_y, low_c, high_c,
    iterate_out, coeffs, target, mid_target, up_x, down_x, up_y, down_y,
    windows, update, diagonal, rest,
):
    own = (ini, src, absorb, face_x, face_y, face_z)
    size_x, size_y, size_z = ini.shape
    plane_tiles, strip_tiles = tiles_of(size_y, size_z), tiles_of(8, size_z)
    starts = [0] * 6
    for field in range(6):
        assemble_fine(
            windows.at[field], own[field], low_x, high_x, low_y, high_y, low_c, high_c,
            UP_PLANES[field], DOWN_PLANES[field], UP_CORNER[field], DOWN_CORNER[field], tuple(starts),
        )
        starts[0] += UP_PLANES[field] * plane_tiles
        starts[1] += DOWN_PLANES[field] * plane_tiles
        starts[2] += (size_x // 2) * strip_tiles
        starts[3] += (size_x // 2) * strip_tiles
        starts[4] += UP_CORNER[field] * strip_tiles
        starts[5] += DOWN_CORNER[field] * strip_tiles
    low_line = Reader(low_y, starts[2]).get(8, size_z)
    high_reader = Reader(high_y, starts[3])
    high_line = high_reader.get(8, size_z)
    face_line = high_reader.get(8, size_z)
    high = PAD + size_y
    for plane in range(size_x):
        windows[0, FINE + plane, 3:4] = low_line[plane : plane + 1]
        windows[0, FINE + plane, high + 4 : high + 5] = high_line[plane : plane + 1]
        windows[4, FINE + plane, high + 4 : high + 5] = face_line[plane : plane + 1]

    iterate = windows.at[0]
    last = size_x + 2 * FINE - 1
    scale_coeffs(1.0, windows.at[2], windows.at[3], windows.at[4], windows.at[5], coeffs, diagonal, (1, last))

    def scale_target(i, carry):
        target[i] = windows[1, i] * coeffs[6, i]
        return carry

    lax.fori_loop(1, last, scale_target, 0)
    for sweep, pair in enumerate(chebyshev_weights(SWEEPS)):
        sweep_window(
            iterate, update, coeffs, target, (1 + sweep, last - sweep), pair, sweep == 0
        )
    mid_x, mid_y = size_x // 2, size_y // 2
    lines = []
    for block in range(mid_x):
        total = None
        for plane in (FINE + 2 * block, FINE + 2 * block + 1):
            remain = scaled_remain(coeffs, target, plane, iterate[plane - 1], iterate[plane], iterate[plane + 1])
            remain = (remain * diagonal[plane])[PAD : PAD + size_y]
            total = remain if total is None else total + remain
        lines.append(total)
    rest[...] = dot(jnp.concatenate(lines, axis=0), pair_sum(size_z))
    count = mid_x * mid_y
    coarse = (rest[pl.ds(0, count, 2), :] + rest[pl.ds(1, count, 2), :]) * 0.125
    for block in range(mid_x):
        mid_target[block] = coarse[block * mid_y : (block + 1) * mid_y]
    for plane in range(size_x):
        iterate_out[plane] = iterate[FINE + plane, PAD : PAD + size_y]

    tops, bottoms = Writer(up_x), Writer(down_x)
    for plane in range(size_x - 4, size_x):
        tops.put(iterate_out[plane])
    for plane in range(4):
        bottoms.put(iterate_out[plane])
    upper = is_upper(size_z)
    tops_y, bottoms_y = Writer(up_y), Writer(down_y)
    for pair in range(0, size_x, 2):
        one, two = iterate_out[pair], iterate_out[pair + 1]
        tops_y.put(jnp.where(upper, roll(one[size_y - 8 :], 4, 0), two[size_y - 8 :]))
        bottoms_y.put(jnp.where(upper, one[:8], roll(two[:8], 4, 0)))
    for writer in (tops, bottoms, tops_y, bottoms_y):
        writer.put(coarse)
    mids = 4 * mid_x
    near_low = [(low_c, low_c.shape[0] - 2 * mids), (low_x, low_x.shape[0] - mids), (low_c, low_c.shape[0] - mids)]
    near_high = [(high_c, high_c.shape[0] - 2 * mids), (high_x, high_x.shape[0] - mids), (high_c, high_c.shape[0] - mids)]
    for array in range(4):
        for ref, start in near_low:
            tops.put(ref[start + array * mid_x + mid_x - 1])
        for ref, start in near_high:
            bottoms.put(ref[start + array * mid_x])
    for ref, start in near_high:
        bottoms.put(ref[start + mid_x + 1])


def corner_two_kernel(size_x, size_z, low_y, high_y, up, down):
    upper = is_upper(size_z)
    tops, bottoms = Writer(up), Writer(down)
    for plane in range(size_x - 3, size_x):
        tops.put(corner_of(low_y, high_y, plane, upper))
    for plane in range(3):
        bottoms.put(corner_of(low_y, high_y, plane, upper))
    for writer in (tops, bottoms):
        for ref in (low_y, high_y):
            for tile in range(ref.shape[0] - size_x // 2, ref.shape[0]):
                writer.put(ref[tile])


def mid_kernel(
    count_x, count_y, mid, low, low_x, high_x, low_y, high_y, low_c, high_c,
    mid_target, low_x2, high_x2, low_y2, high_y2, low_c2, high_c2,
    window, target, slots,
    coeffs, diagonal, scaled, iterate, update, rest,
):
    mid_x, mid_y, mid_z = mid_target.shape
    mids = 4 * mid_x
    first = MID - mid_x
    blocks = {
        (0, 0): (low_c, low_c.shape[0] - 2 * mids), (0, 1): (low_x, low_x.shape[0] - mids),
        (0, 2): (low_c, low_c.shape[0] - mids), (1, 0): (low_y, low_y.shape[0] - mids),
        (1, 1): (mid, 0), (1, 2): (high_y, high_y.shape[0] - mids),
        (2, 0): (high_c, high_c.shape[0] - 2 * mids), (2, 1): (high_x, high_x.shape[0] - mids),
        (2, 2): (high_c, high_c.shape[0] - mids),
    }
    for (bx, by), (ref, start) in blocks.items():
        for array in range(4):
            for plane in range(mid_x):
                window[array, first + bx * mid_x + plane, by * mid_y : (by + 1) * mid_y] = ref[
                    start + array * mid_x + plane
                ]
    far = 3 * mid_x + first
    fine_tiles = 4 * tiles_of(2 * mid_y, 2 * mid_z)
    own_planes = fine_tiles + mid_x
    for array in range(4):
        for by in range(3):
            rows = slice(by * mid_y, (by + 1) * mid_y)
            window[array, first - 1, rows] = low_x2[own_planes + 3 * array + by]
            window[array, far, rows] = high_x2[own_planes + 3 * array + by]
    for by in range(3):
        window[1, far + 1, by * mid_y : (by + 1) * mid_y] = high_x2[own_planes + 12 + by]

    blocks = {
        (0, 0): (low_c2, low_c2.shape[0] - 2 * mid_x), (0, 1): (low_x2, fine_tiles),
        (0, 2): (low_c2, low_c2.shape[0] - mid_x), (1, 0): (low_y2, low_y2.shape[0] - mid_x),
        (1, 2): (high_y2, high_y2.shape[0] - mid_x),
        (2, 0): (high_c2, high_c2.shape[0] - 2 * mid_x), (2, 1): (high_x2, fine_tiles),
        (2, 2): (high_c2, high_c2.shape[0] - mid_x),
    }
    for plane in range(mid_x):
        target[MID + plane, mid_y : 2 * mid_y] = mid_target[plane]
    for (bx, by), (ref, start) in blocks.items():
        for plane in range(mid_x):
            target[first + bx * mid_x + plane, by * mid_y : (by + 1) * mid_y] = ref[start + plane]

    scale_coeffs(0.25, window.at[0], window.at[1], window.at[2], window.at[3], coeffs, diagonal, (first, far))
    weights = chebyshev_weights(SWEEPS)

    def start_sweep(i, carry):
        goal = target[i] * coeffs[6, i]
        scaled[i] = goal
        update[i] = weights[0][1] * goal
        iterate[i] = weights[0][1] * goal
        return carry

    lax.fori_loop(first, far, start_sweep, 0)
    for sweep in range(1, SWEEPS):
        sweep_window(iterate, update, coeffs, scaled, (first + sweep, far - sweep), weights[sweep], False)
    low_x_size = mid_x // 2
    for block in range(low_x_size):
        total = None
        for plane in (MID + 2 * block, MID + 2 * block + 1):
            remain = scaled_remain(coeffs, scaled, plane, iterate[plane - 1], iterate[plane], iterate[plane + 1])
            remain = (remain * diagonal[plane])[mid_y : 2 * mid_y]
            total = remain if total is None else total + remain
        rest[block * mid_y : (block + 1) * mid_y] = total
    count = low_x_size * mid_y // 2
    summed = rest[pl.ds(0, count, 2), :] + rest[pl.ds(1, count, 2), :]
    coarse = dot(summed * 0.125, selector(mid_z, mid_z, lambda k, m: k // 2 == m))
    halves = (
        [coarse + low[0], low[1], low[2], mid_target[0], mid_target[mid_x - 1]],
        [iterate[MID + plane, mid_y : 2 * mid_y] for plane in range(mid_x)],
    )

    def fill(i, carry):
        for side in range(2):
            for j in range(count_y):
                for tile, value in enumerate(halves[side]):
                    slots[(2 * i + side) * count_y + j, tile] = value
        return carry

    lax.fori_loop(0, count_x // 2, fill, 0)


def solve_low(count_x, count_y, half, fields, coeffs, target, iterate, update):
    size_x, size_y, lanes = target.shape
    low_x, low_y = size_x // count_x, size_y // count_y
    low_z = lanes // 2

    def place(i, carry):
        for j in range(count_y):
            for kind in range(3):
                tile = half(0, i * count_y + j, kind)
                for plane in range(low_x):
                    fields[kind, i * low_x + plane, j * low_y : (j + 1) * low_y] = tile[
                        plane * low_y : (plane + 1) * low_y
                    ]
        return carry

    lax.fori_loop(0, count_x, place, 0)
    lane = iota((size_y, lanes), 1)
    inside = lane < low_z
    scale = 0.0625
    weights = chebyshev_weights(COARSE_SWEEPS)

    def prepare(i, carry):
        after = jnp.where(i == size_x - 1, 0, i + 1)
        first, second, third = fields[0, i], fields[1, i], fields[2, i]
        xl, xh = second, fields[1, after]
        yl = roll(second, low_z, 1)
        yh = roll(yl, -1, 0)
        zl = third
        zh = jnp.where(lane == low_z - 1, 0.0, roll(third, -1, 1))
        diag = roll(first, low_z, 1) + scale * (xl + xh + yl + yh + zl + zh)
        inverse = jnp.where(inside, 1.0 / diag, 0.0)
        scaled = scale * inverse
        coeffs[0, i] = scaled * xl
        coeffs[1, i] = scaled * xh
        coeffs[2, i] = scaled * yl
        coeffs[3, i] = scaled * yh
        coeffs[4, i] = jnp.where(lane == 0, 0.0, scaled * zl)
        coeffs[5, i] = scaled * zh
        goal = first * inverse
        target[i] = goal
        update[i] = weights[0][1] * goal
        iterate[i] = weights[0][1] * goal
        return carry

    lax.fori_loop(0, size_x, prepare, 0)
    for pair in weights[1:]:
        start = iterate[0]

        def body(i, carry, pair=pair, start=start):
            below, here = carry
            after = jnp.where(i == size_x - 1, 0, i + 1)
            above = jnp.where(i == size_x - 1, start, iterate[after])
            step = pair[1] * scaled_remain(coeffs, target, i, below, here, above) + pair[0] * update[i]
            update[i] = step
            iterate[i] = here + step
            return here, above

        lax.fori_loop(0, size_x, body, (iterate[size_x - 1], start), unroll=4)


def last_kernel(
    count_x, count_y, place, own_half, other_half, window, mid_target, coeffs, target, iterate_own,
    low_x2, high_x2, low_y2, high_y2, low_c2, high_c2,
    out,
    low_fields, low_coeffs, low_target, low_iterate, low_update,
    mid_coeffs, mid_scaled, mid_iterate, mid_update, spread_mid,
    iterate, update, spread,
):
    size_x, size_y, size_z = iterate_own.shape
    mid_x, mid_y, mid_z = size_x // 2, size_y // 2, size_z // 2
    me_x, me_y = place[0], place[1]
    even = me_x % 2 == 0

    def half(which, device, tile):
        one, two = own_half[device, tile], other_half[device, tile]
        return jnp.where(even, one, two) if which == 0 else jnp.where(even, two, one)

    solve_low(count_x, count_y, half, low_fields, low_coeffs, low_target, low_iterate, low_update)

    def device(dx, dy):
        return lax.rem(me_x + dx + count_x, count_x) * count_y + lax.rem(me_y + dy + count_y, count_y)

    first, far = MID - mid_x, MID + 2 * mid_x
    for dy in (-1, 0, 1):
        rows = slice((dy + 1) * mid_y, (dy + 2) * mid_y)
        for dx in (-1, 0, 1):
            for plane in range(mid_x):
                mid_iterate[MID + dx * mid_x + plane, rows] = half(1, device(dx, dy), plane)
        for plane in range(first):
            mid_iterate[plane, rows] = half(1, device(-2, dy), mid_x - first + plane)
            mid_iterate[far + plane, rows] = half(1, device(2, dy), plane)
    low_size_x, low_size_y = low_target.shape[:2]
    low_planes, low_rows = (mid_x + 2 * MID) // 2, 16
    low_y = mid_y // 2
    turn = lax.rem(low_size_y - me_y * low_y + low_y, low_size_y)
    picked = []
    for plane in range(low_planes):
        at = lax.rem(me_x * (mid_x // 2) - MID // 2 + plane + low_size_x, low_size_x)
        picked.append(pltpu.roll(low_iterate[at], turn, 0)[:low_rows])
    wide = dot(jnp.concatenate(picked, axis=0), selector(mid_z, mid_z, lambda k, m: k == m // 2))
    count = low_planes * low_rows
    spread_mid[pl.ds(0, count, 2), :] = wide
    spread_mid[pl.ds(1, count, 2), :] = wide
    for plane in range(low_planes):
        part = spread_mid[plane * 2 * low_rows : plane * 2 * low_rows + 3 * mid_y]
        mid_iterate[2 * plane] += part
        mid_iterate[2 * plane + 1] += part

    scale_coeffs(0.25, window.at[0], window.at[1], window.at[2], window.at[3], mid_coeffs, None, (first - 1, far + 1))

    def scale_target(i, carry):
        mid_scaled[i] = mid_target[i] * mid_coeffs[6, i]
        return carry

    lax.fori_loop(first, far, scale_target, 0)
    for dy in (-1, 0, 1):
        rows = slice((dy + 1) * mid_y, (dy + 2) * mid_y)
        mid_scaled[first - 1, rows] = half(0, device(-2, dy), 4) * mid_coeffs[6, first - 1, rows]
        mid_scaled[far, rows] = half(0, device(2, dy), 3) * mid_coeffs[6, far, rows]
    for sweep, pair in enumerate(chebyshev_weights(SWEEPS)):
        sweep_window(
            mid_iterate, mid_update, mid_coeffs, mid_scaled, (first - 1 + sweep, far + 1 - sweep), pair, sweep == 0
        )

    fine_low = FINE - 4
    assemble_fine(
        iterate, iterate_own, low_x2, high_x2, low_y2, high_y2, low_c2, high_c2, 4, 4, 3, 3, (0,) * 6
    )
    planes = mid_x + 4
    rows = mid_y + 8
    picked = [roll(mid_iterate[MID - 2 + plane], -4, 0)[:rows] for plane in range(planes)]
    wide = dot(jnp.concatenate(picked, axis=0), pair_copy(mid_z))
    count = planes * rows
    for side in range(2):
        lanes = slice(side * mid_z, (side + 1) * mid_z)
        spread[side, pl.ds(0, count, 2), :] = wide[:, lanes]
        spread[side, pl.ds(1, count, 2), :] = wide[:, lanes]
    for plane in range(planes):
        lines = slice(plane * 2 * rows, (plane + 1) * 2 * rows)
        part = jnp.concatenate([spread[0, lines], spread[1, lines]], axis=1)
        iterate[fine_low + 2 * plane] += part
        iterate[fine_low + 2 * plane + 1] += part
    last = size_x + 2 * FINE - 2
    for sweep, pair in enumerate(chebyshev_weights(SWEEPS)):
        sweep_window(
            iterate, update, coeffs, target, (2 + sweep, last - sweep), pair, sweep == 0
        )
    for plane in range(size_x):
        out[plane] = iterate[FINE + plane, PAD : PAD + size_y]


def call(kernel, inputs, outs, scratch=(), scalars=0):
    spaces = [pltpu.SMEM] * scalars + [pltpu.VMEM] * (len(inputs) - scalars)
    return pl.pallas_call(
        kernel,
        out_shape=[jax.ShapeDtypeStruct(shape, F32) for shape in outs],
        in_specs=[pl.BlockSpec(memory_space=space) for space in spaces],
        out_specs=[pl.BlockSpec(memory_space=pltpu.VMEM)] * len(outs),
        scratch_shapes=[pltpu.VMEM(shape, F32) for shape in scratch],
        compiler_params=pltpu.CompilerParams(vmem_limit_bytes=60 * 1024 * 1024),
    )(*inputs)


def local(source, initial, absorption, beta_x, beta_y, beta_z):
    size_x, size_y, size_z = source.shape
    mid_x, mid_y, mid_z = size_x // 2, size_y // 2, size_z // 2
    low_x, low_y = mid_x // 2, mid_y // 2
    count_x, count_y = lax.axis_size("gx"), lax.axis_size("gy")
    devices = count_x * count_y
    plane, strip = tiles_of(size_y, size_z), tiles_of(8, size_z)
    mids = 4 * mid_x

    def tiles(count):
        return (count,) + TILE

    own = (initial, source, absorption, beta_x, beta_y, beta_z)
    pairs = size_x // 2
    up_x, down_x, up_y, down_y, mid, low = call(
        pack_kernel,
        own,
        [
            tiles(sum(UP_PLANES) * plane + mids),
            tiles(sum(DOWN_PLANES) * plane + mids),
            tiles((6 * pairs + 1) * strip + mids),
            tiles((6 * pairs + 2) * strip + mids),
            tiles(mids),
            tiles(3),
        ],
        [(4 * mid_x * size_y, mid_z)],
    )
    low_x1, high_x1 = shifted(up_x, "gx", 1), shifted(down_x, "gx", -1)
    low_y1, high_y1 = shifted(up_y, "gy", 1), shifted(down_y, "gy", -1)
    up_c, down_c = call(
        functools.partial(corner_kernel, size_x, size_z),
        (low_y1, high_y1),
        [tiles(sum(UP_CORNER) * strip + 2 * mids), tiles(sum(DOWN_CORNER) * strip + 2 * mids)],
    )
    low_c1, high_c1 = shifted(up_c, "gx", 1), shifted(down_c, "gx", -1)

    wide = (size_x + 2 * FINE, size_y + 2 * PAD, size_z)
    iterate, coeffs, target, mid_target, up_x, down_x, up_y, down_y = call(
        fine_kernel,
        own + (low_x1, high_x1, low_y1, high_y1, low_c1, high_c1),
        [
            source.shape,
            (7,) + wide,
            wide,
            (mid_x, mid_y, mid_z),
            tiles(4 * plane + mid_x + 12),
            tiles(4 * plane + mid_x + 15),
            tiles(pairs * strip + mid_x),
            tiles(pairs * strip + mid_x),
        ],
        [(6,) + wide, wide, wide, (mid_x * size_y, mid_z)],
    )
    low_x2, high_x2 = shifted(up_x, "gx", 1), shifted(down_x, "gx", -1)
    low_y2, high_y2 = shifted(up_y, "gy", 1), shifted(down_y, "gy", -1)
    up_c, down_c = call(
        functools.partial(corner_two_kernel, size_x, size_z),
        (low_y2, high_y2),
        [tiles(3 * strip + 2 * mid_x)] * 2,
    )
    low_c2, high_c2 = shifted(up_c, "gx", 1), shifted(down_c, "gx", -1)

    mid_wide = (mid_x + 2 * MID, 3 * mid_y, mid_z)
    window, mid_goal, slots = call(
        functools.partial(mid_kernel, count_x, count_y),
        (mid, low, low_x1, high_x1, low_y1, high_y1, low_c1, high_c1)
        + (mid_target, low_x2, high_x2, low_y2, high_y2, low_c2, high_c2),
        [(4,) + mid_wide, mid_wide, (devices, 5) + TILE],
        [(7,) + mid_wide] + [mid_wide] * 4 + [(low_x * mid_y, mid_z)],
    )
    own_half = lax.all_to_all(slots, ("gx", "gy"), 0, 0)
    other_half = lax.ppermute(own_half, "gx", [(i, i ^ 1) for i in range(count_x)])

    place = jnp.stack([lax.axis_index("gx"), lax.axis_index("gy")]).astype(jnp.int32)
    low_wide = (low_x * count_x, low_y * count_y, mid_z)
    low_planes = mid_wide[0] // 2
    (result,) = call(
        functools.partial(last_kernel, count_x, count_y),
        (place, own_half, other_half, window, mid_goal, coeffs, target, iterate)
        + (low_x2, high_x2, low_y2, high_y2, low_c2, high_c2),
        [source.shape],
        [(3,) + low_wide, (6,) + low_wide, low_wide, low_wide, low_wide]
        + [(7,) + mid_wide, mid_wide, mid_wide, mid_wide, (low_planes * 32, mid_z)]
        + [wide, wide, (2, (mid_x + 4) * 2 * (mid_y + 8), mid_z)],
        scalars=1,
    )
    return result


def solution(mesh):
    spec = P("gx", "gy", None)
    return jax.shard_map(
        local, mesh=mesh, in_specs=(spec,) * 6, out_specs=spec, check_vma=False
    )
```

```python
import functools
import math

import jax
import jax.numpy as jnp
from jax import lax
from jax.experimental import pallas as pl
from jax.experimental.pallas import tpu as pltpu
from jax.sharding import PartitionSpec as P

SWEEPS = 4
COARSE_SWEEPS = 8
F32 = jnp.float32
TILE = (8, 128)
PAD = 8
FINE = 5
MID = 6


def chebyshev_weights(sweeps):
    cheb_theta = 1.125
    cheb_delta = 0.875
    cheb_sigma = cheb_theta / cheb_delta
    rho_old = 1.0 / cheb_sigma
    weights = [(0.0, 1.0 / cheb_theta)]
    for sweep in range(1, sweeps):
        rho_new = 1.0 / (2.0 * cheb_sigma - rho_old)
        weights.append((rho_new * rho_old, 2.0 * rho_new / cheb_delta))
        rho_old = rho_new
    return weights


def iota(shape, axis):
    return lax.broadcasted_iota(jnp.int32, shape, axis)


def selector(rows, columns, hit):
    return jnp.where(hit(iota((rows, columns), 0), iota((rows, columns), 1)), 1.0, 0.0).astype(F32)


def pair_sum(size):
    return selector(size, size // 2, lambda k, m: k // 2 == m)


def pair_copy(size):
    return selector(size, 2 * size, lambda k, m: k == m // 2)


def dot(left, right):
    return lax.dot(left, right, precision=lax.Precision.HIGHEST, preferred_element_type=F32)


def roll(value, shift, axis):
    return pltpu.roll(value, shift % value.shape[axis], axis)


def each(start, stop, body, carry=0):
    if stop - start > 20:
        return lax.fori_loop(start, stop, body, carry, unroll=2)
    for i in range(start, stop):
        carry = body(i, carry)
    return carry


class Writer:
    def __init__(self, ref):
        self.ref, self.at = ref, 0

    def put(self, value):
        rows, columns = value.shape
        for r in range(0, rows, TILE[0]):
            for c in range(0, columns, TILE[1]):
                self.ref[self.at] = value[r : r + TILE[0], c : c + TILE[1]]
                self.at += 1


class Reader:
    def __init__(self, ref, at=0):
        self.ref, self.at = ref, at

    def get(self, rows, columns):
        lines = []
        for _ in range(rows // TILE[0]):
            parts = []
            for _ in range(columns // TILE[1]):
                parts.append(self.ref[self.at])
                self.at += 1
            lines.append(parts[0] if len(parts) == 1 else jnp.concatenate(parts, axis=1))
        return lines[0] if len(lines) == 1 else jnp.concatenate(lines, axis=0)


UP_PLANES = (5, 4, 4, 4, 4, 4)
DOWN_PLANES = (5, 4, 4, 5, 4, 4)
UP_CORNER = (4, 3, 3, 3, 4, 3)
DOWN_CORNER = (4, 3, 3, 4, 4, 3)


def tiles_of(rows, columns):
    return (rows // TILE[0]) * (columns // TILE[1])


def is_upper(width):
    return iota((TILE[0], width), 0) < TILE[0] // 2


def shifted(value, axis, step):
    count = lax.axis_size(axis)
    return lax.ppermute(value, axis, [(i, (i + step) % count) for i in range(count)])


def pack_kernel(
    ini_in, src_in, absorb_in, face_x_in, face_y_in, face_z_in,
    up_x, down_x, up_y, down_y, mid, low, own, rows_mid, sems,
):
    copies = []
    for field, ref in enumerate((ini_in, src_in, absorb_in, face_x_in, face_y_in, face_z_in)):
        copies.append(pltpu.make_async_copy(ref, own.at[field], sems.at[field]))
        copies[-1].start()
    for copy in copies:
        copy.wait()
    fields = tuple(own.at[field] for field in range(6))
    ini, src, absorb, face_x, face_y, face_z = fields
    size_x, size_y, size_z = ini.shape
    half = size_y // 2
    blocks = range(0, size_x, 2)

    def both_planes(ref):
        return [ref[plane] + ref[plane + 1] for plane in blocks]

    stacked = both_planes(absorb) + [face_x[plane] for plane in blocks] + both_planes(face_y)
    summed = dot(jnp.concatenate(stacked, axis=0), pair_sum(size_z))
    picked = dot(
        jnp.concatenate(both_planes(face_z), axis=0),
        selector(size_z, size_z // 2, lambda k, m: k == 2 * m),
    )
    count = summed.shape[0]
    rows_mid[:count] = summed
    rows_mid[count:] = picked
    out = Writer(mid)
    for array, (factor, sides) in enumerate(((0.125, 2), (0.25, 2), (0.25, 1), (0.25, 2))):
        lines = (size_x // 2) * half
        start = 2 * array * lines
        total = rows_mid[pl.ds(start, lines, 2), :]
        if sides == 2:
            total = total + rows_mid[pl.ds(start + 1, lines, 2), :]
        out.put(total * factor)

    mid_x, mid_z = size_x // 2, size_z // 2
    both = (0, 1)
    low_z = mid_z // 2

    def coarser(array, planes, sides):
        lines = []
        for block in range(mid_x // 2):
            total = None
            for plane in planes:
                for side in sides:
                    at = array * mid_x + 2 * block + plane
                    part = mid[at, pl.ds(side, half // 2, 2), :]
                    total = part if total is None else total + part
            lines.append(total)
        return jnp.concatenate(lines, axis=0)

    left = selector(mid_z, mid_z, lambda k, m: k // 2 == m)
    right = selector(mid_z, mid_z, lambda k, m: k // 2 == m - low_z)
    evens = selector(mid_z, mid_z, lambda k, m: k == 2 * m)
    low[0] = dot(coarser(0, both, both) * 0.125, right)
    low[1] = dot(coarser(1, (0,), both) * 0.25, left) + dot(coarser(2, both, (0,)) * 0.25, right)
    low[2] = dot(coarser(3, both, both) * 0.25, evens)

    tops, bottoms = Writer(up_x), Writer(down_x)
    for ref, count in zip(fields, UP_PLANES):
        for plane in range(size_x - count, size_x):
            tops.put(ref[plane])
    for ref, count in zip(fields, DOWN_PLANES):
        for plane in range(count):
            bottoms.put(ref[plane])

    upper = is_upper(size_z)
    tops_y, bottoms_y = Writer(up_y), Writer(down_y)
    for ref in fields:
        for pair in range(0, size_x, 2):
            one, two = ref[pair], ref[pair + 1]
            tops_y.put(jnp.where(upper, roll(one[size_y - 8 :], 4, 0), two[size_y - 8 :]))
            bottoms_y.put(jnp.where(upper, one[:8], roll(two[:8], 4, 0)))
    tops_y.put(ini[:, size_y - 5, :])
    bottoms_y.put(ini[:, 4, :])
    bottoms_y.put(face_y[:, 4, :])
    for writer in (tops, bottoms, tops_y, bottoms_y):
        for tile in range(mid.shape[0]):
            writer.put(mid[tile])


def corner_of(low_y, high_y, plane, upper, first_tile=0):
    width = upper.shape[1]
    at = first_tile + (plane // 2) * tiles_of(8, width)
    low = Reader(low_y, at).get(8, width)
    high = Reader(high_y, at).get(8, width)
    if plane % 2 == 0:
        return jnp.where(upper, low, roll(high, 4, 0))
    return jnp.where(upper, roll(low, 4, 0), high)


def corner_kernel(size_x, size_z, low_y, high_y, up, down):
    upper = is_upper(size_z)
    per_field = (size_x // 2) * tiles_of(8, size_z)
    tops, bottoms = Writer(up), Writer(down)
    for field in range(6):
        for plane in range(size_x - UP_CORNER[field], size_x):
            tops.put(corner_of(low_y, high_y, plane, upper, field * per_field))
        for plane in range(DOWN_CORNER[field]):
            bottoms.put(corner_of(low_y, high_y, plane, upper, field * per_field))
    mid_x = size_x // 2
    sides = [(ref, ref.shape[0] - 4 * mid_x) for ref in (low_y, high_y)]
    upper = is_upper(TILE[1])
    for writer, first, step in ((tops, mid_x - 1, -1), (bottoms, 0, 1)):
        for array in range(4):
            for q in range(2):
                for ref, start in sides:
                    writer.put(ref[start + array * mid_x + first + q * step])
        for array in range(4):
            for q in range(2, 4):
                one, two = (roll(ref[start + array * mid_x + first + q * step], 4, 0) for ref, start in sides)
                writer.put(jnp.where(upper, one, two))


MID_CORNER = 24


def whole_corner(ref, array, q, side):
    return ref[ref.shape[0] - MID_CORNER + (array * 2 + q) * 2 + side]


def part_corner(ref, array, q):
    return ref[ref.shape[0] - MID_CORNER + 16 + array * 2 + q - 2]


def scale_coeffs(scale, absorb, face_x, face_y, face_z, coeffs, diagonal, planes):
    rows, lanes = absorb.shape[1:]
    lane = iota((rows, lanes), 1)

    def body(i, carry):
        xl, xh = face_x[i], face_x[i + 1]
        yl, zl = face_y[i], face_z[i]
        yh = roll(yl, -1, 0)
        zh = jnp.where(lane == lanes - 1, 0.0, roll(zl, -1, 1))
        diag = absorb[i] + scale * (xl + xh + yl + yh + zl + zh)
        inverse = 1.0 / diag
        scaled = scale * inverse
        coeffs[0, i] = scaled * xl
        coeffs[1, i] = scaled * xh
        coeffs[2, i] = scaled * yl
        coeffs[3, i] = scaled * yh
        coeffs[4, i] = jnp.where(lane == 0, 0.0, scaled * zl)
        coeffs[5, i] = scaled * zh
        coeffs[7, i] = inverse
        if diagonal is not None:
            diagonal[i] = diag
        return carry

    each(*planes, body)


def scaled_remain(coeffs, i, below, here, above):
    total = coeffs[6, i] - here
    total = total + coeffs[0, i] * below + coeffs[1, i] * above
    total = total + coeffs[2, i] * roll(here, 1, 0) + coeffs[3, i] * roll(here, -1, 0)
    return total + coeffs[4, i] * roll(here, 1, 1) + coeffs[5, i] * roll(here, -1, 1)


def sweep_window(iterate, update, coeffs, planes, pair, first):
    start, stop = planes

    def body(i, carry):
        below, here = carry
        above = iterate[i + 1]
        step = pair[1] * scaled_remain(coeffs, i, below, here, above)
        if not first:
            step = step + pair[0] * update[i]
        update[i] = step
        iterate[i] = here + step
        return here, above

    each(start, stop, body, (iterate[start - 1], iterate[start]))


def assemble_fine(window, own, low_x, high_x, low_y, high_y, low_c, high_c, up, down, up_c, down_c, starts):
    size_x, size_y, size_z = own.shape
    for plane in range(size_x):
        window[FINE + plane, PAD : PAD + size_y] = own[plane]
    reader = Reader(low_x, starts[0])
    for plane in range(up):
        window[FINE - up + plane, PAD : PAD + size_y] = reader.get(size_y, size_z)
    reader = Reader(high_x, starts[1])
    for plane in range(down):
        window[FINE + size_x + plane, PAD : PAD + size_y] = reader.get(size_y, size_z)
    high = PAD + size_y
    low_reader, high_reader = Reader(low_y, starts[2]), Reader(high_y, starts[3])
    for pair in range(0, size_x, 2):
        tile = low_reader.get(8, size_z)
        window[FINE + pair, 0:8] = roll(tile, 4, 0)
        window[FINE + pair + 1, 0:8] = tile
        tile = high_reader.get(8, size_z)
        window[FINE + pair, high : high + 8] = tile
        window[FINE + pair + 1, high : high + 8] = roll(tile, 4, 0)
    for ref, start, first, count in (
        (low_c, starts[4], FINE - up_c, up_c),
        (high_c, starts[5], FINE + size_x, down_c),
    ):
        reader = Reader(ref, start)
        for plane in range(count):
            tile = roll(reader.get(8, size_z), 4, 0)
            window[first + plane, 0:8] = tile
            window[first + plane, high : high + 8] = tile


def fine_kernel(
    own, low_x, high_x, low_y, high_y, low_c, high_c,
    iterate_out, coeffs_out, mid_target, up_x, down_x, up_y, down_y,
    windows, coeffs, update, diagonal, rest, sem,
):
    size_x, size_y, size_z = own.shape[1:]
    plane_tiles, strip_tiles = tiles_of(size_y, size_z), tiles_of(8, size_z)
    starts = [0] * 6
    for field in range(6):
        assemble_fine(
            windows.at[field], own.at[field], low_x, high_x, low_y, high_y, low_c, high_c,
            UP_PLANES[field], DOWN_PLANES[field], UP_CORNER[field], DOWN_CORNER[field], tuple(starts),
        )
        starts[0] += UP_PLANES[field] * plane_tiles
        starts[1] += DOWN_PLANES[field] * plane_tiles
        starts[2] += (size_x // 2) * strip_tiles
        starts[3] += (size_x // 2) * strip_tiles
        starts[4] += UP_CORNER[field] * strip_tiles
        starts[5] += DOWN_CORNER[field] * strip_tiles
    low_line = Reader(low_y, starts[2]).get(8, size_z)
    high_reader = Reader(high_y, starts[3])
    high_line = high_reader.get(8, size_z)
    face_line = high_reader.get(8, size_z)
    high = PAD + size_y
    for plane in range(size_x):
        windows[0, FINE + plane, 3:4] = low_line[plane : plane + 1]
        windows[0, FINE + plane, high + 4 : high + 5] = high_line[plane : plane + 1]
        windows[4, FINE + plane, high + 4 : high + 5] = face_line[plane : plane + 1]

    iterate = windows.at[0]
    last = size_x + 2 * FINE - 1
    scale_coeffs(1.0, windows.at[2], windows.at[3], windows.at[4], windows.at[5], coeffs, diagonal, (1, last))

    for plane in range(1, last):
        coeffs[6, plane] = windows[1, plane] * coeffs[7, plane]
    keep = pltpu.make_async_copy(coeffs.at[:7, 2 : last - 1], coeffs_out, sem)
    keep.start()
    for sweep, pair in enumerate(chebyshev_weights(SWEEPS)):
        sweep_window(
            iterate, update, coeffs, (1 + sweep, last - sweep), pair, sweep == 0
        )
    mid_x, mid_y = size_x // 2, size_y // 2
    lines = []
    for block in range(mid_x):
        total = None
        for plane in (FINE + 2 * block, FINE + 2 * block + 1):
            remain = scaled_remain(coeffs, plane, iterate[plane - 1], iterate[plane], iterate[plane + 1])
            remain = (remain * diagonal[plane])[PAD : PAD + size_y]
            total = remain if total is None else total + remain
        lines.append(total)
    rest[...] = dot(jnp.concatenate(lines, axis=0), pair_sum(size_z))
    count = mid_x * mid_y
    coarse = (rest[pl.ds(0, count, 2), :] + rest[pl.ds(1, count, 2), :]) * 0.125
    for block in range(mid_x):
        mid_target[block] = coarse[block * mid_y : (block + 1) * mid_y]
    for plane in range(size_x):
        iterate_out[plane] = iterate[FINE + plane, PAD : PAD + size_y]

    tops, bottoms = Writer(up_x), Writer(down_x)
    for plane in range(size_x - 4, size_x):
        tops.put(iterate_out[plane])
    for plane in range(4):
        bottoms.put(iterate_out[plane])
    upper = is_upper(size_z)
    tops_y, bottoms_y = Writer(up_y), Writer(down_y)
    for pair in range(0, size_x, 2):
        one, two = iterate_out[pair], iterate_out[pair + 1]
        tops_y.put(jnp.where(upper, roll(one[size_y - 8 :], 4, 0), two[size_y - 8 :]))
        bottoms_y.put(jnp.where(upper, one[:8], roll(two[:8], 4, 0)))
    for writer in (tops, bottoms, tops_y, bottoms_y):
        writer.put(coarse)
    low_start, high_start = (ref.shape[0] - 4 * mid_x for ref in (low_x, high_x))
    for array in range(4):
        tops.put(whole_corner(low_c, array, 0, 0))
        tops.put(low_x[low_start + array * mid_x + mid_x - 1])
        tops.put(whole_corner(low_c, array, 0, 1))
        bottoms.put(whole_corner(high_c, array, 0, 0))
        bottoms.put(high_x[high_start + array * mid_x])
        bottoms.put(whole_corner(high_c, array, 0, 1))
    bottoms.put(whole_corner(high_c, 1, 1, 0))
    bottoms.put(high_x[high_start + mid_x + 1])
    bottoms.put(whole_corner(high_c, 1, 1, 1))
    keep.wait()


def corner_two_kernel(size_x, size_z, low_y, high_y, up, down):
    upper = is_upper(size_z)
    tops, bottoms = Writer(up), Writer(down)
    for plane in range(size_x - 3, size_x):
        tops.put(corner_of(low_y, high_y, plane, upper))
    for plane in range(3):
        bottoms.put(corner_of(low_y, high_y, plane, upper))
    for writer in (tops, bottoms):
        for ref in (low_y, high_y):
            for tile in range(ref.shape[0] - size_x // 2, ref.shape[0]):
                writer.put(ref[tile])


def mid_kernel(
    count_x, count_y, place, mid, low, low_x, high_x, low_y, high_y, low_c, high_c,
    mid_target, low_x2, high_x2, low_y2, high_y2, low_c2, high_c2,
    window, target, slots,
    coeffs, diagonal, iterate, update, rest,
):
    mid_x, mid_y, mid_z = mid_target.shape
    mids = 4 * mid_x
    first = MID - mid_x
    blocks = {
        (0, 1): (low_x, low_x.shape[0] - mids), (1, 0): (low_y, low_y.shape[0] - mids),
        (1, 1): (mid, 0), (1, 2): (high_y, high_y.shape[0] - mids),
        (2, 1): (high_x, high_x.shape[0] - mids),
    }
    for (bx, by), (ref, start) in blocks.items():
        for array in range(4):
            for plane in range(mid_x):
                window[array, first + bx * mid_x + plane, by * mid_y : (by + 1) * mid_y] = ref[
                    start + array * mid_x + plane
                ]
    for ref, start, step in ((low_c, MID - 1, -1), (high_c, MID + mid_x, 1)):
        for array in range(4):
            for q in range(mid_x):
                if q < 2:
                    one, two = whole_corner(ref, array, q, 0), whole_corner(ref, array, q, 1)
                else:
                    one = two = roll(part_corner(ref, array, q), 4, 0)
                window[array, start + q * step, :mid_y] = one
                window[array, start + q * step, 2 * mid_y :] = two
    far = 3 * mid_x + first
    fine_tiles = 4 * tiles_of(2 * mid_y, 2 * mid_z)
    own_planes = fine_tiles + mid_x
    for array in range(4):
        for by in range(3):
            rows = slice(by * mid_y, (by + 1) * mid_y)
            window[array, first - 1, rows] = low_x2[own_planes + 3 * array + by]
            window[array, far, rows] = high_x2[own_planes + 3 * array + by]
    for by in range(3):
        window[1, far + 1, by * mid_y : (by + 1) * mid_y] = high_x2[own_planes + 12 + by]

    blocks = {
        (0, 0): (low_c2, low_c2.shape[0] - 2 * mid_x), (0, 1): (low_x2, fine_tiles),
        (0, 2): (low_c2, low_c2.shape[0] - mid_x), (1, 0): (low_y2, low_y2.shape[0] - mid_x),
        (1, 2): (high_y2, high_y2.shape[0] - mid_x),
        (2, 0): (high_c2, high_c2.shape[0] - 2 * mid_x), (2, 1): (high_x2, fine_tiles),
        (2, 2): (high_c2, high_c2.shape[0] - mid_x),
    }
    for plane in range(mid_x):
        target[MID + plane, mid_y : 2 * mid_y] = mid_target[plane]
    for (bx, by), (ref, start) in blocks.items():
        for plane in range(mid_x):
            target[first + bx * mid_x + plane, by * mid_y : (by + 1) * mid_y] = ref[start + plane]

    scale_coeffs(0.25, window.at[0], window.at[1], window.at[2], window.at[3], coeffs, diagonal, (first, far))
    weights = chebyshev_weights(SWEEPS)

    def start_sweep(i, carry):
        goal = target[i] * coeffs[7, i]
        coeffs[6, i] = goal
        update[i] = weights[0][1] * goal
        iterate[i] = weights[0][1] * goal
        return carry

    each(first, far, start_sweep)
    for sweep in range(1, SWEEPS):
        sweep_window(iterate, update, coeffs, (first + sweep, far - sweep), weights[sweep], False)
    low_x_size = mid_x // 2
    for block in range(low_x_size):
        total = None
        for plane in (MID + 2 * block, MID + 2 * block + 1):
            remain = scaled_remain(coeffs, plane, iterate[plane - 1], iterate[plane], iterate[plane + 1])
            remain = (remain * diagonal[plane])[mid_y : 2 * mid_y]
            total = remain if total is None else total + remain
        rest[block * mid_y : (block + 1) * mid_y] = total
    count = low_x_size * mid_y // 2
    summed = rest[pl.ds(0, count, 2), :] + rest[pl.ds(1, count, 2), :]
    coarse = dot(summed * 0.125, selector(mid_z, mid_z, lambda k, m: k // 2 == m))
    low_tiles = (coarse + low[0], low[1], low[2])
    iterates = [iterate[MID + plane, mid_y : 2 * mid_y] for plane in range(mid_x)]
    pairs = count_x // 2
    following = lax.rem(place[0] // 2 + 1, pairs)

    def fill(i, carry):
        edge = jnp.where(i == following, mid_target[mid_x - 1], mid_target[0])
        for j in range(count_y):
            for tile, value in enumerate(low_tiles + (edge,)):
                slots[2 * i * count_y + j, tile] = value
            for tile, value in enumerate(iterates):
                slots[(2 * i + 1) * count_y + j, tile] = value
        return carry

    each(0, pairs, fill)


def solve_low(count_x, count_y, half, fields, coeffs, iterate, update):
    size_x, size_y, lanes = iterate.shape
    low_x, low_y = size_x // count_x, size_y // count_y
    low_z = lanes // 2

    def place(i, carry):
        for j in range(count_y):
            for kind in range(3):
                tile = half(0, i * count_y + j, kind)
                for plane in range(low_x):
                    fields[kind, i * low_x + plane, j * low_y : (j + 1) * low_y] = tile[
                        plane * low_y : (plane + 1) * low_y
                    ]
        return carry

    each(0, count_x, place)
    lane = iota((size_y, lanes), 1)
    inside = lane < low_z
    scale = 0.0625
    weights = chebyshev_weights(COARSE_SWEEPS)

    def following(i):
        if isinstance(i, int):
            return (i + 1) % size_x
        return jnp.where(i == size_x - 1, 0, i + 1)

    def prepare(i, carry):
        first, second, third = fields[0, i], fields[1, i], fields[2, i]
        xl, xh = second, fields[1, following(i)]
        yl = roll(second, low_z, 1)
        yh = roll(yl, -1, 0)
        zl = third
        zh = jnp.where(lane == low_z - 1, 0.0, roll(third, -1, 1))
        diag = roll(first, low_z, 1) + scale * (xl + xh + yl + yh + zl + zh)
        inverse = jnp.where(inside, 1.0 / diag, 0.0)
        scaled = scale * inverse
        coeffs[0, i] = scaled * xl
        coeffs[1, i] = scaled * xh
        coeffs[2, i] = scaled * yl
        coeffs[3, i] = scaled * yh
        coeffs[4, i] = jnp.where(lane == 0, 0.0, scaled * zl)
        coeffs[5, i] = scaled * zh
        goal = first * inverse
        coeffs[6, i] = goal
        update[i] = weights[0][1] * goal
        iterate[i] = weights[0][1] * goal
        return carry

    each(0, size_x, prepare)
    for pair in weights[1:]:
        start = iterate[0]

        def body(i, carry, pair=pair, start=start):
            below, here = carry
            if isinstance(i, int):
                above = start if i == size_x - 1 else iterate[i + 1]
            else:
                above = jnp.where(i == size_x - 1, start, iterate[following(i)])
            step = pair[1] * scaled_remain(coeffs, i, below, here, above) + pair[0] * update[i]
            update[i] = step
            iterate[i] = here + step
            return here, above

        each(0, size_x, body, (iterate[size_x - 1], start))


def last_kernel(
    count_x, count_y, place, own_half, other_half, window, mid_target, coeffs_in, iterate_own,
    low_x2, high_x2, low_y2, high_y2, low_c2, high_c2,
    out,
    low_fields, low_coeffs, low_iterate, low_update,
    mid_coeffs, mid_iterate, mid_update, spread_mid,
    coeffs, iterate, update, spread, sem,
):
    size_x, size_y, size_z = iterate_own.shape
    mid_x, mid_y, mid_z = size_x // 2, size_y // 2, size_z // 2
    last = size_x + 2 * FINE - 2
    fetch = pltpu.make_async_copy(coeffs_in, coeffs.at[:, 2:last], sem)
    fetch.start()
    me_x, me_y = place[0], place[1]
    even = me_x % 2 == 0

    def half(which, device, tile):
        one, two = own_half[device, tile], other_half[device, tile]
        return jnp.where(even, one, two) if which == 0 else jnp.where(even, two, one)

    solve_low(count_x, count_y, half, low_fields, low_coeffs, low_iterate, low_update)

    def device(dx, dy):
        return lax.rem(me_x + dx + count_x, count_x) * count_y + lax.rem(me_y + dy + count_y, count_y)

    first, far = MID - mid_x, MID + 2 * mid_x
    for dy in (-1, 0, 1):
        rows = slice((dy + 1) * mid_y, (dy + 2) * mid_y)
        for dx in (-1, 0, 1):
            for plane in range(mid_x):
                mid_iterate[MID + dx * mid_x + plane, rows] = half(1, device(dx, dy), plane)
        for plane in range(first):
            mid_iterate[plane, rows] = half(1, device(-2, dy), mid_x - first + plane)
            mid_iterate[far + plane, rows] = half(1, device(2, dy), plane)
    low_size_x, low_size_y = low_iterate.shape[:2]
    low_planes, low_rows = (mid_x + 2 * MID) // 2, 16
    low_y = mid_y // 2
    turn = lax.rem(low_size_y - me_y * low_y + low_y, low_size_y)
    picked = []
    for plane in range(low_planes):
        at = lax.rem(me_x * (mid_x // 2) - MID // 2 + plane + low_size_x, low_size_x)
        picked.append(pltpu.roll(low_iterate[at], turn, 0)[:low_rows])
    wide = dot(jnp.concatenate(picked, axis=0), selector(mid_z, mid_z, lambda k, m: k == m // 2))
    count = low_planes * low_rows
    spread_mid[pl.ds(0, count, 2), :] = wide
    spread_mid[pl.ds(1, count, 2), :] = wide
    for plane in range(low_planes):
        part = spread_mid[plane * 2 * low_rows : plane * 2 * low_rows + 3 * mid_y]
        mid_iterate[2 * plane] += part
        mid_iterate[2 * plane + 1] += part

    scale_coeffs(0.25, window.at[0], window.at[1], window.at[2], window.at[3], mid_coeffs, None, (first - 1, far + 1))

    for plane in range(first, far):
        mid_coeffs[6, plane] = mid_target[plane] * mid_coeffs[7, plane]
    for dy in (-1, 0, 1):
        rows = slice((dy + 1) * mid_y, (dy + 2) * mid_y)
        for plane, dx in ((first - 1, -2), (far, 2)):
            mid_coeffs[6, plane, rows] = half(0, device(dx, dy), 3) * mid_coeffs[7, plane, rows]
    for sweep, pair in enumerate(chebyshev_weights(SWEEPS)):
        sweep_window(
            mid_iterate, mid_update, mid_coeffs, (first - 1 + sweep, far + 1 - sweep), pair, sweep == 0
        )

    fine_low = FINE - 4
    assemble_fine(
        iterate, iterate_own, low_x2, high_x2, low_y2, high_y2, low_c2, high_c2, 4, 4, 3, 3, (0,) * 6
    )
    planes = mid_x + 4
    rows = mid_y + 8
    picked = [roll(mid_iterate[MID - 2 + plane], -4, 0)[:rows] for plane in range(planes)]
    wide = dot(jnp.concatenate(picked, axis=0), pair_copy(mid_z))
    count = planes * rows
    for side in range(2):
        lanes = slice(side * mid_z, (side + 1) * mid_z)
        spread[side, pl.ds(0, count, 2), :] = wide[:, lanes]
        spread[side, pl.ds(1, count, 2), :] = wide[:, lanes]
    for plane in range(planes):
        lines = slice(plane * 2 * rows, (plane + 1) * 2 * rows)
        part = jnp.concatenate([spread[0, lines], spread[1, lines]], axis=1)
        iterate[fine_low + 2 * plane] += part
        iterate[fine_low + 2 * plane + 1] += part
    fetch.wait()
    for sweep, pair in enumerate(chebyshev_weights(SWEEPS)):
        sweep_window(
            iterate, update, coeffs, (2 + sweep, last - sweep), pair, sweep == 0
        )
    for plane in range(size_x):
        out[plane] = iterate[FINE + plane, PAD : PAD + size_y]


def call(kernel, inputs, outs, scratch=(), scalars=0, far_in=(), far_out=(), sems=0):
    def place(i):
        return pltpu.SMEM if i < scalars else pltpu.HBM if i in far_in else pltpu.VMEM

    near = [x.shape for i, x in enumerate(inputs) if i >= scalars and i not in far_in]
    near += [shape for i, shape in enumerate(outs) if i not in far_out] + list(scratch)
    used = 4 * sum(math.prod(shape) for shape in near)
    inputs = [pltpu.with_memory_space_constraint(x, pltpu.HBM) if i in far_in else x for i, x in enumerate(inputs)]
    return pl.pallas_call(
        kernel,
        out_shape=[
            pltpu.HBM(shape, F32) if i in far_out else jax.ShapeDtypeStruct(shape, F32)
            for i, shape in enumerate(outs)
        ],
        in_specs=[pl.BlockSpec(memory_space=place(i)) for i in range(len(inputs))],
        out_specs=[
            pl.BlockSpec(memory_space=pltpu.HBM if i in far_out else pltpu.VMEM) for i in range(len(outs))
        ],
        scratch_shapes=[pltpu.VMEM(shape, F32) for shape in scratch]
        + ([pltpu.SemaphoreType.DMA((sems,))] if sems > 1 else [pltpu.SemaphoreType.DMA] * sems),
        cost_estimate=pl.CostEstimate(flops=1000, bytes_accessed=1000, transcendentals=0),
        compiler_params=pltpu.CompilerParams(vmem_limit_bytes=used + used // 4 + 2 * 1024 * 1024),
    )(*inputs)


def local(source, initial, absorption, beta_x, beta_y, beta_z):
    size_x, size_y, size_z = source.shape
    mid_x, mid_y, mid_z = size_x // 2, size_y // 2, size_z // 2
    low_x, low_y = mid_x // 2, mid_y // 2
    count_x, count_y = lax.axis_size("gx"), lax.axis_size("gy")
    devices = count_x * count_y
    plane, strip = tiles_of(size_y, size_z), tiles_of(8, size_z)
    mids = 4 * mid_x

    def tiles(count):
        return (count,) + TILE

    place = jnp.stack([lax.axis_index("gx"), lax.axis_index("gy")]).astype(jnp.int32)
    pairs = size_x // 2
    up_x, down_x, up_y, down_y, mid, low, own = call(
        pack_kernel,
        (initial, source, absorption, beta_x, beta_y, beta_z),
        [
            tiles(sum(UP_PLANES) * plane + mids),
            tiles(sum(DOWN_PLANES) * plane + mids),
            tiles((6 * pairs + 1) * strip + mids),
            tiles((6 * pairs + 2) * strip + mids),
            tiles(mids),
            tiles(3),
            (6,) + source.shape,
        ],
        [(4 * mid_x * size_y, mid_z)],
        far_in=range(6),
        sems=6,
    )
    low_x1, high_x1 = shifted(up_x, "gx", 1), shifted(down_x, "gx", -1)
    low_y1, high_y1 = shifted(up_y, "gy", 1), shifted(down_y, "gy", -1)
    up_c, down_c = call(
        functools.partial(corner_kernel, size_x, size_z),
        (low_y1, high_y1),
        [tiles(sum(UP_CORNER) * strip + MID_CORNER), tiles(sum(DOWN_CORNER) * strip + MID_CORNER)],
    )
    low_c1, high_c1 = shifted(up_c, "gx", 1), shifted(down_c, "gx", -1)

    wide = (size_x + 2 * FINE, size_y + 2 * PAD, size_z)
    iterate, coeffs, mid_target, up_x, down_x, up_y, down_y = call(
        fine_kernel,
        (own, low_x1, high_x1, low_y1, high_y1, low_c1, high_c1),
        [
            source.shape,
            (7, wide[0] - 4) + wide[1:],
            (mid_x, mid_y, mid_z),
            tiles(4 * plane + mid_x + 12),
            tiles(4 * plane + mid_x + 15),
            tiles(pairs * strip + mid_x),
            tiles(pairs * strip + mid_x),
        ],
        [(6,) + wide, (8,) + wide, wide, wide, (mid_x * size_y, mid_z)],
        far_out=(1,),
        sems=1,
    )
    low_x2, high_x2 = shifted(up_x, "gx", 1), shifted(down_x, "gx", -1)
    low_y2, high_y2 = shifted(up_y, "gy", 1), shifted(down_y, "gy", -1)
    up_c, down_c = call(
        functools.partial(corner_two_kernel, size_x, size_z),
        (low_y2, high_y2),
        [tiles(3 * strip + 2 * mid_x)] * 2,
    )
    low_c2, high_c2 = shifted(up_c, "gx", 1), shifted(down_c, "gx", -1)

    mid_wide = (mid_x + 2 * MID, 3 * mid_y, mid_z)
    window, mid_goal, slots = call(
        functools.partial(mid_kernel, count_x, count_y),
        (place, mid, low, low_x1, high_x1, low_y1, high_y1, low_c1, high_c1)
        + (mid_target, low_x2, high_x2, low_y2, high_y2, low_c2, high_c2),
        [(4,) + mid_wide, mid_wide, (devices, 4) + TILE],
        [(8,) + mid_wide] + [mid_wide] * 3 + [(low_x * mid_y, mid_z)],
        scalars=1,
    )
    own_half = lax.all_to_all(slots, ("gx", "gy"), 0, 0)
    other_half = lax.ppermute(own_half, "gx", [(i, i ^ 1) for i in range(count_x)])

    low_wide = (low_x * count_x, low_y * count_y, mid_z)
    low_planes = mid_wide[0] // 2
    (result,) = call(
        functools.partial(last_kernel, count_x, count_y),
        (place, own_half, other_half, window, mid_goal, coeffs, iterate)
        + (low_x2, high_x2, low_y2, high_y2, low_c2, high_c2),
        [source.shape],
        [(3,) + low_wide, (7,) + low_wide, low_wide, low_wide]
        + [(8,) + mid_wide, mid_wide, mid_wide, (low_planes * 32, mid_z)]
        + [(7,) + wide, wide, wide, (2, (mid_x + 4) * 2 * (mid_y + 8), mid_z)],
        scalars=1,
        far_in=(5,),
        sems=1,
    )
    return result


def solution(mesh):
    spec = P("gx", "gy", None)
    return jax.shard_map(
        local, mesh=mesh, in_specs=(spec,) * 6, out_specs=spec, check_vma=False
    )
```

```python
import functools
import math

import jax
import jax.numpy as jnp
from jax import lax
from jax.experimental import pallas as pl
from jax.experimental.pallas import tpu as pltpu
from jax.sharding import PartitionSpec as P

SWEEPS = 4
COARSE_SWEEPS = 8
F32 = jnp.float32
TILE = (8, 128)
PAD = 8
FINE = 5
MID = 6


def chebyshev_weights(sweeps):
    cheb_theta = 1.125
    cheb_delta = 0.875
    cheb_sigma = cheb_theta / cheb_delta
    rho_old = 1.0 / cheb_sigma
    weights = [(0.0, 1.0 / cheb_theta)]
    for sweep in range(1, sweeps):
        rho_new = 1.0 / (2.0 * cheb_sigma - rho_old)
        weights.append((rho_new * rho_old, 2.0 * rho_new / cheb_delta))
        rho_old = rho_new
    return weights


def iota(shape, axis):
    return lax.broadcasted_iota(jnp.int32, shape, axis)


def selector(rows, columns, hit):
    return jnp.where(hit(iota((rows, columns), 0), iota((rows, columns), 1)), 1.0, 0.0).astype(F32)


def pair_sum(size):
    return selector(size, size // 2, lambda k, m: k // 2 == m)


def pair_copy(size):
    return selector(size, 2 * size, lambda k, m: k == m // 2)


def dot(left, right):
    return lax.dot(left, right, precision=lax.Precision.HIGHEST, preferred_element_type=F32)


def roll(value, shift, axis):
    return pltpu.roll(value, shift % value.shape[axis], axis)


def each(start, stop, body, carry=0):
    if stop - start > 20:
        return lax.fori_loop(start, stop, body, carry, unroll=2)
    for i in range(start, stop):
        carry = body(i, carry)
    return carry


class Writer:
    def __init__(self, ref):
        self.ref, self.at = ref, 0

    def put(self, value):
        rows, columns = value.shape
        for r in range(0, rows, TILE[0]):
            for c in range(0, columns, TILE[1]):
                self.ref[self.at] = value[r : r + TILE[0], c : c + TILE[1]]
                self.at += 1


class Reader:
    def __init__(self, ref, at=0):
        self.ref, self.at = ref, at

    def get(self, rows, columns):
        lines = []
        for _ in range(rows // TILE[0]):
            parts = []
            for _ in range(columns // TILE[1]):
                parts.append(self.ref[self.at])
                self.at += 1
            lines.append(parts[0] if len(parts) == 1 else jnp.concatenate(parts, axis=1))
        return lines[0] if len(lines) == 1 else jnp.concatenate(lines, axis=0)


UP_PLANES = (5, 4, 4, 4, 4, 4)
DOWN_PLANES = (5, 4, 4, 5, 4, 4)
UP_CORNER = (4, 3, 3, 3, 4, 3)
DOWN_CORNER = (4, 3, 3, 4, 4, 3)


def tiles_of(rows, columns):
    return (rows // TILE[0]) * (columns // TILE[1])


def is_upper(width):
    return iota((TILE[0], width), 0) < TILE[0] // 2


def shifted(value, axis, step):
    count = lax.axis_size(axis)
    return lax.ppermute(value, axis, [(i, (i + step) % count) for i in range(count)])


def pack_kernel(
    ini_in, src_in, absorb_in, face_x_in, face_y_in, face_z_in,
    up_x, down_x, up_y, down_y, mid, low, own, rows_mid, sems,
):
    copies = []
    for field, ref in enumerate((ini_in, src_in, absorb_in, face_x_in, face_y_in, face_z_in)):
        copies.append(pltpu.make_async_copy(ref, own.at[field], sems.at[field]))
        copies[-1].start()
    for copy in copies:
        copy.wait()
    fields = tuple(own.at[field] for field in range(6))
    ini, src, absorb, face_x, face_y, face_z = fields
    size_x, size_y, size_z = ini.shape
    half = size_y // 2
    blocks = range(0, size_x, 2)

    def both_planes(ref):
        return [ref[plane] + ref[plane + 1] for plane in blocks]

    stacked = both_planes(absorb) + [face_x[plane] for plane in blocks] + both_planes(face_y)
    summed = dot(jnp.concatenate(stacked, axis=0), pair_sum(size_z))
    picked = dot(
        jnp.concatenate(both_planes(face_z), axis=0),
        selector(size_z, size_z // 2, lambda k, m: k == 2 * m),
    )
    count = summed.shape[0]
    rows_mid[:count] = summed
    rows_mid[count:] = picked
    out = Writer(mid)
    for array, (factor, sides) in enumerate(((0.125, 2), (0.25, 2), (0.25, 1), (0.25, 2))):
        lines = (size_x // 2) * half
        start = 2 * array * lines
        total = rows_mid[pl.ds(start, lines, 2), :]
        if sides == 2:
            total = total + rows_mid[pl.ds(start + 1, lines, 2), :]
        out.put(total * factor)

    mid_x, mid_z = size_x // 2, size_z // 2
    both = (0, 1)
    low_z = mid_z // 2

    def coarser(array, planes, sides):
        lines = []
        for block in range(mid_x // 2):
            total = None
            for plane in planes:
                for side in sides:
                    at = array * mid_x + 2 * block + plane
                    part = mid[at, pl.ds(side, half // 2, 2), :]
                    total = part if total is None else total + part
            lines.append(total)
        return jnp.concatenate(lines, axis=0)

    left = selector(mid_z, mid_z, lambda k, m: k // 2 == m)
    right = selector(mid_z, mid_z, lambda k, m: k // 2 == m - low_z)
    evens = selector(mid_z, mid_z, lambda k, m: k == 2 * m)
    low[0] = dot(coarser(0, both, both) * 0.125, right)
    low[1] = dot(coarser(1, (0,), both) * 0.25, left) + dot(coarser(2, both, (0,)) * 0.25, right)
    low[2] = dot(coarser(3, both, both) * 0.25, evens)

    tops, bottoms = Writer(up_x), Writer(down_x)
    for ref, count in zip(fields, UP_PLANES):
        for plane in range(size_x - count, size_x):
            tops.put(ref[plane])
    for ref, count in zip(fields, DOWN_PLANES):
        for plane in range(count):
            bottoms.put(ref[plane])

    upper = is_upper(size_z)
    tops_y, bottoms_y = Writer(up_y), Writer(down_y)
    for ref in fields:
        for pair in range(0, size_x, 2):
            one, two = ref[pair], ref[pair + 1]
            tops_y.put(jnp.where(upper, roll(one[size_y - 8 :], 4, 0), two[size_y - 8 :]))
            bottoms_y.put(jnp.where(upper, one[:8], roll(two[:8], 4, 0)))
    tops_y.put(ini[:, size_y - 5, :])
    bottoms_y.put(ini[:, 4, :])
    bottoms_y.put(face_y[:, 4, :])
    for writer in (tops, bottoms, tops_y, bottoms_y):
        for tile in range(mid.shape[0]):
            writer.put(mid[tile])


def corner_of(low_y, high_y, plane, upper, first_tile=0):
    width = upper.shape[1]
    at = first_tile + (plane // 2) * tiles_of(8, width)
    low = Reader(low_y, at).get(8, width)
    high = Reader(high_y, at).get(8, width)
    if plane % 2 == 0:
        return jnp.where(upper, low, roll(high, 4, 0))
    return jnp.where(upper, roll(low, 4, 0), high)


def corner_kernel(size_x, size_z, low_y, high_y, up, down):
    upper = is_upper(size_z)
    per_field = (size_x // 2) * tiles_of(8, size_z)
    tops, bottoms = Writer(up), Writer(down)
    for field in range(6):
        for plane in range(size_x - UP_CORNER[field], size_x):
            tops.put(corner_of(low_y, high_y, plane, upper, field * per_field))
        for plane in range(DOWN_CORNER[field]):
            bottoms.put(corner_of(low_y, high_y, plane, upper, field * per_field))
    mid_x = size_x // 2
    sides = [(ref, ref.shape[0] - 4 * mid_x) for ref in (low_y, high_y)]
    upper = is_upper(TILE[1])
    for writer, first, step in ((tops, mid_x - 1, -1), (bottoms, 0, 1)):
        for array in range(4):
            for q in range(2):
                for ref, start in sides:
                    writer.put(ref[start + array * mid_x + first + q * step])
        for array in range(4):
            for q in range(2, 4):
                one, two = (roll(ref[start + array * mid_x + first + q * step], 4, 0) for ref, start in sides)
                writer.put(jnp.where(upper, one, two))


MID_CORNER = 24


def whole_corner(ref, array, q, side):
    return ref[ref.shape[0] - MID_CORNER + (array * 2 + q) * 2 + side]


def part_corner(ref, array, q):
    return ref[ref.shape[0] - MID_CORNER + 16 + array * 2 + q - 2]


class Planes:
    def __init__(self, *parts):
        self.parts = parts
        self.shape = parts[0][2].shape

    def find(self, i):
        for start, stop, ref, offset, lead in self.parts:
            if start <= i < stop:
                return ref, lead + (i - start + offset,)
        raise IndexError(i)

    def __getitem__(self, i):
        ref, index = self.find(i)
        return ref[index]


class Stack:
    def __init__(self, *parts):
        self.parts = parts

    def of(self, kind):
        return Planes(*((a, b, ref, offset, (kind,)) for a, b, ref, offset in self.parts))

    def __getitem__(self, index):
        return self.of(index[0])[index[1]]

    def __setitem__(self, index, value):
        ref, place = self.of(index[0]).find(index[1])
        ref[place] = value


def scale_coeffs(scale, absorb, face_x, face_y, face_z, coeffs, planes, target=None, diagonal=None):
    rows, lanes = absorb.shape[-2:]
    lane = iota((rows, lanes), 1)

    def body(i, carry):
        xl, xh = face_x[i], face_x[i + 1]
        yl, zl = face_y[i], face_z[i]
        yh = roll(yl, -1, 0)
        zh = jnp.where(lane == lanes - 1, 0.0, roll(zl, -1, 1))
        diag = absorb[i] + scale * (xl + xh + yl + yh + zl + zh)
        inverse = 1.0 / diag
        scaled = scale * inverse
        coeffs[0, i] = scaled * xl
        coeffs[1, i] = scaled * xh
        coeffs[2, i] = scaled * yl
        coeffs[3, i] = scaled * yh
        coeffs[4, i] = jnp.where(lane == 0, 0.0, scaled * zl)
        coeffs[5, i] = scaled * zh
        if target is not None:
            coeffs[6, i] = target[i] * inverse
        else:
            coeffs[6, i] = inverse
        if diagonal is not None:
            coeffs[7, i] = diag
        return carry

    each(*planes, body)


def scaled_remain(coeffs, i, below, here, above, goal=None):
    total = (coeffs[6, i] if goal is None else goal[i]) - here
    total = total + coeffs[0, i] * below + coeffs[1, i] * above
    total = total + coeffs[2, i] * roll(here, 1, 0) + coeffs[3, i] * roll(here, -1, 0)
    return total + coeffs[4, i] * roll(here, 1, 1) + coeffs[5, i] * roll(here, -1, 1)


def sweep_window(iterate, update, coeffs, planes, pair, first, goal=None, source=None):
    start, stop = planes
    source = iterate if source is None else source

    def body(i, carry):
        below, here = carry
        above = source[i + 1]
        step = pair[1] * scaled_remain(coeffs, i, below, here, above, goal)
        if not first:
            step = step + pair[0] * update[i]
        update[i] = step
        iterate[i] = here + step
        return here, above

    each(start, stop, body, (source[start - 1], source[start]))


def assemble_own(window, own, low_y, high_y, low_start, high_start):
    size_x, size_y, size_z = own.shape
    high = PAD + size_y
    low_reader, high_reader = Reader(low_y, low_start), Reader(high_y, high_start)
    for pair in range(0, size_x, 2):
        window[pair, PAD:high] = own[pair]
        window[pair + 1, PAD:high] = own[pair + 1]
        tile = low_reader.get(8, size_z)
        window[pair, 0:8] = roll(tile, 4, 0)
        window[pair + 1, 0:8] = tile
        tile = high_reader.get(8, size_z)
        window[pair, high : high + 8] = tile
        window[pair + 1, high : high + 8] = roll(tile, 4, 0)


def assemble_side(window, first, count, rows, planes, plane_start, corners, corner_start, corner_count, from_end):
    size_y, size_z = rows
    high = PAD + size_y
    reader = Reader(planes, plane_start)
    for plane in range(count):
        window[first + plane, PAD:high] = reader.get(size_y, size_z)
    reader = Reader(corners, corner_start)
    first += count - corner_count if from_end else 0
    for plane in range(corner_count):
        tile = roll(reader.get(8, size_z), 4, 0)
        window[first + plane, 0:8] = tile
        window[first + plane, high : high + 8] = tile


def assemble_owns(windows, own, low_y, high_y):
    size_x, size_y, size_z = own.shape[1:]
    per_field = (size_x // 2) * tiles_of(8, size_z)
    for field in range(6):
        assemble_own(windows.at[field], own.at[field], low_y, high_y, field * per_field, field * per_field)
    low_line = Reader(low_y, 6 * per_field).get(8, size_z)
    high_reader = Reader(high_y, 6 * per_field)
    high_line = high_reader.get(8, size_z)
    face_line = high_reader.get(8, size_z)
    high = PAD + size_y
    for plane in range(size_x):
        windows[0, plane, 3:4] = low_line[plane : plane + 1]
        windows[0, plane, high + 4 : high + 5] = high_line[plane : plane + 1]
        windows[4, plane, high + 4 : high + 5] = face_line[plane : plane + 1]


def assemble_sides(side_windows, rows, low_x, high_x, low_c, high_c):
    plane_tiles, strip_tiles = tiles_of(*rows), tiles_of(8, rows[1])
    starts = [0] * 4
    for field in range(6):
        up, down, up_c, down_c = (
            kinds[field] for kinds in (UP_PLANES, DOWN_PLANES, UP_CORNER, DOWN_CORNER)
        )
        window = side_windows.at[field]
        assemble_side(
            window, FINE - up, up, rows, low_x, starts[0], low_c, starts[2], up_c, True
        )
        assemble_side(
            window, FINE, down, rows, high_x, starts[1], high_c, starts[3], down_c, False
        )
        starts[0] += up * plane_tiles
        starts[1] += down * plane_tiles
        starts[2] += up_c * strip_tiles
        starts[3] += down_c * strip_tiles


def own_kernel(own, low_y, high_y, windows, coeffs):
    assemble_owns(windows, own, low_y, high_y)
    fields = [windows.at[field] for field in range(6)]
    scale_coeffs(1.0, *fields[2:], coeffs, (0, own.shape[1] - 1), fields[1], True)


def fine_kernel(
    own_windows, own_coeffs, low_x, high_x, low_c, high_c,
    iterate_out, mid_target, up_x, down_x, up_y, down_y,
    side_windows, side_coeffs, iterate, update, rest,
):
    size_x, size_z = own_windows.shape[1], own_windows.shape[3]
    size_y = own_windows.shape[2] - 2 * PAD
    assemble_sides(side_windows, (size_y, size_z), low_x, high_x, low_c, high_c)
    end = FINE + size_x
    last = end + FINE - 1
    windows = Stack(
        (0, FINE, side_windows, 0), (FINE, end, own_windows, 0), (end, last + 1, side_windows, FINE)
    )
    coeffs = Stack(
        (0, FINE, side_coeffs, 0), (FINE, end - 1, own_coeffs, 0), (end - 1, last + 1, side_coeffs, FINE)
    )
    fields = [windows.of(field) for field in range(6)]
    scale_coeffs(1.0, *fields[2:], coeffs, (1, FINE), fields[1], True)
    scale_coeffs(1.0, *fields[2:], coeffs, (end - 1, last), fields[1], True)
    for sweep, pair in enumerate(chebyshev_weights(SWEEPS)):
        sweep_window(
            iterate, update, coeffs, (1 + sweep, last - sweep), pair, sweep == 0,
            source=fields[0] if sweep == 0 else None,
        )
    mid_x, mid_y = size_x // 2, size_y // 2
    lines = []
    for block in range(mid_x):
        total = None
        for plane in (FINE + 2 * block, FINE + 2 * block + 1):
            remain = scaled_remain(coeffs, plane, iterate[plane - 1], iterate[plane], iterate[plane + 1])
            remain = (remain * coeffs[7, plane])[PAD : PAD + size_y]
            total = remain if total is None else total + remain
        lines.append(total)
    rest[...] = dot(jnp.concatenate(lines, axis=0), pair_sum(size_z))
    count = mid_x * mid_y
    coarse = (rest[pl.ds(0, count, 2), :] + rest[pl.ds(1, count, 2), :]) * 0.125
    for block in range(mid_x):
        mid_target[block] = coarse[block * mid_y : (block + 1) * mid_y]
    for plane in range(size_x):
        iterate_out[plane] = iterate[FINE + plane, PAD : PAD + size_y]

    tops, bottoms = Writer(up_x), Writer(down_x)
    for plane in range(size_x - 4, size_x):
        tops.put(iterate_out[plane])
    for plane in range(4):
        bottoms.put(iterate_out[plane])
    upper = is_upper(size_z)
    tops_y, bottoms_y = Writer(up_y), Writer(down_y)
    for pair in range(0, size_x, 2):
        one, two = iterate_out[pair], iterate_out[pair + 1]
        tops_y.put(jnp.where(upper, roll(one[size_y - 8 :], 4, 0), two[size_y - 8 :]))
        bottoms_y.put(jnp.where(upper, one[:8], roll(two[:8], 4, 0)))
    for writer in (tops, bottoms, tops_y, bottoms_y):
        writer.put(coarse)
    low_start, high_start = (ref.shape[0] - 4 * mid_x for ref in (low_x, high_x))
    for array in range(4):
        tops.put(whole_corner(low_c, array, 0, 0))
        tops.put(low_x[low_start + array * mid_x + mid_x - 1])
        tops.put(whole_corner(low_c, array, 0, 1))
        bottoms.put(whole_corner(high_c, array, 0, 0))
        bottoms.put(high_x[high_start + array * mid_x])
        bottoms.put(whole_corner(high_c, array, 0, 1))
    bottoms.put(whole_corner(high_c, 1, 1, 0))
    bottoms.put(high_x[high_start + mid_x + 1])
    bottoms.put(whole_corner(high_c, 1, 1, 1))


def corner_two_kernel(size_x, size_z, low_y, high_y, up, down):
    upper = is_upper(size_z)
    tops, bottoms = Writer(up), Writer(down)
    for plane in range(size_x - 3, size_x):
        tops.put(corner_of(low_y, high_y, plane, upper))
    for plane in range(3):
        bottoms.put(corner_of(low_y, high_y, plane, upper))
    for writer in (tops, bottoms):
        for ref in (low_y, high_y):
            for tile in range(ref.shape[0] - size_x // 2, ref.shape[0]):
                writer.put(ref[tile])


def mid_coeffs_kernel(mid, low_x, high_x, low_y, high_y, low_c, high_c, low_x2, high_x2, coeffs, window):
    mid_y, mid_z = mid.shape[1:]
    mid_x = mid.shape[0] // 4
    mids = 4 * mid_x
    first = MID - mid_x
    blocks = {
        (0, 1): (low_x, low_x.shape[0] - mids), (1, 0): (low_y, low_y.shape[0] - mids),
        (1, 1): (mid, 0), (1, 2): (high_y, high_y.shape[0] - mids),
        (2, 1): (high_x, high_x.shape[0] - mids),
    }
    for (bx, by), (ref, start) in blocks.items():
        for array in range(4):
            for plane in range(mid_x):
                window[array, first + bx * mid_x + plane, by * mid_y : (by + 1) * mid_y] = ref[
                    start + array * mid_x + plane
                ]
    for ref, start, step in ((low_c, MID - 1, -1), (high_c, MID + mid_x, 1)):
        for array in range(4):
            for q in range(mid_x):
                if q < 2:
                    one, two = whole_corner(ref, array, q, 0), whole_corner(ref, array, q, 1)
                else:
                    one = two = roll(part_corner(ref, array, q), 4, 0)
                window[array, start + q * step, :mid_y] = one
                window[array, start + q * step, 2 * mid_y :] = two
    far = 3 * mid_x + first
    fine_tiles = 4 * tiles_of(2 * mid_y, 2 * mid_z)
    own_planes = fine_tiles + mid_x
    for array in range(4):
        for by in range(3):
            rows = slice(by * mid_y, (by + 1) * mid_y)
            window[array, first - 1, rows] = low_x2[own_planes + 3 * array + by]
            window[array, far, rows] = high_x2[own_planes + 3 * array + by]
    for by in range(3):
        window[1, far + 1, by * mid_y : (by + 1) * mid_y] = high_x2[own_planes + 12 + by]

    scale_coeffs(0.25, *(window.at[array] for array in range(4)), coeffs, (first - 1, far + 1), None, True)


def mid_kernel(
    count_x, count_y, place, low, mid_target, coeffs, low_x2, high_x2, low_y2, high_y2, low_c2, high_c2,
    goal, slots, target, iterate, update, rest,
):
    mid_x, mid_y, mid_z = mid_target.shape
    first = MID - mid_x
    far = 3 * mid_x + first
    fine_tiles = 4 * tiles_of(2 * mid_y, 2 * mid_z)
    blocks = {
        (0, 0): (low_c2, low_c2.shape[0] - 2 * mid_x), (0, 1): (low_x2, fine_tiles),
        (0, 2): (low_c2, low_c2.shape[0] - mid_x), (1, 0): (low_y2, low_y2.shape[0] - mid_x),
        (1, 2): (high_y2, high_y2.shape[0] - mid_x),
        (2, 0): (high_c2, high_c2.shape[0] - 2 * mid_x), (2, 1): (high_x2, fine_tiles),
        (2, 2): (high_c2, high_c2.shape[0] - mid_x),
    }
    for plane in range(mid_x):
        target[MID + plane, mid_y : 2 * mid_y] = mid_target[plane]
    for (bx, by), (ref, start) in blocks.items():
        for plane in range(mid_x):
            target[first + bx * mid_x + plane, by * mid_y : (by + 1) * mid_y] = ref[start + plane]

    weights = chebyshev_weights(SWEEPS)

    def start_sweep(i, carry):
        value = target[i] * coeffs[6, i]
        goal[i] = value
        update[i] = weights[0][1] * value
        iterate[i] = weights[0][1] * value
        return carry

    each(first, far, start_sweep)
    for sweep in range(1, SWEEPS):
        sweep_window(iterate, update, coeffs, (first + sweep, far - sweep), weights[sweep], False, goal)
    low_x_size = mid_x // 2
    for block in range(low_x_size):
        total = None
        for plane in (MID + 2 * block, MID + 2 * block + 1):
            remain = scaled_remain(coeffs, plane, iterate[plane - 1], iterate[plane], iterate[plane + 1], goal)
            remain = (remain * coeffs[7, plane])[mid_y : 2 * mid_y]
            total = remain if total is None else total + remain
        rest[block * mid_y : (block + 1) * mid_y] = total
    count = low_x_size * mid_y // 2
    summed = rest[pl.ds(0, count, 2), :] + rest[pl.ds(1, count, 2), :]
    coarse = dot(summed * 0.125, selector(mid_z, mid_z, lambda k, m: k // 2 == m))
    low_tiles = (coarse + low[0], low[1], low[2])
    iterates = [iterate[MID + plane, mid_y : 2 * mid_y] for plane in range(mid_x)]
    pairs = count_x // 2
    following = lax.rem(place[0] // 2 + 1, pairs)

    def fill(i, carry):
        edge = jnp.where(i == following, mid_target[mid_x - 1], mid_target[0])
        for j in range(count_y):
            for tile, value in enumerate(low_tiles + (edge,)):
                slots[2 * i * count_y + j, tile] = value
            for tile, value in enumerate(iterates):
                slots[(2 * i + 1) * count_y + j, tile] = value
        return carry

    each(0, pairs, fill)


def solve_low(count_x, count_y, half, fields, coeffs, iterate, update):
    size_x, size_y, lanes = iterate.shape
    low_x, low_y = size_x // count_x, size_y // count_y
    low_z = lanes // 2

    def place(i, carry):
        for j in range(count_y):
            for kind in range(3):
                tile = half(0, i * count_y + j, kind)
                for plane in range(low_x):
                    fields[kind, i * low_x + plane, j * low_y : (j + 1) * low_y] = tile[
                        plane * low_y : (plane + 1) * low_y
                    ]
        return carry

    each(0, count_x, place)
    lane = iota((size_y, lanes), 1)
    inside = lane < low_z
    scale = 0.0625
    weights = chebyshev_weights(COARSE_SWEEPS)

    def following(i):
        if isinstance(i, int):
            return (i + 1) % size_x
        return jnp.where(i == size_x - 1, 0, i + 1)

    def prepare(i, carry):
        first, second, third = fields[0, i], fields[1, i], fields[2, i]
        xl, xh = second, fields[1, following(i)]
        yl = roll(second, low_z, 1)
        yh = roll(yl, -1, 0)
        zl = third
        zh = jnp.where(lane == low_z - 1, 0.0, roll(third, -1, 1))
        diag = roll(first, low_z, 1) + scale * (xl + xh + yl + yh + zl + zh)
        inverse = jnp.where(inside, 1.0 / diag, 0.0)
        scaled = scale * inverse
        coeffs[0, i] = scaled * xl
        coeffs[1, i] = scaled * xh
        coeffs[2, i] = scaled * yl
        coeffs[3, i] = scaled * yh
        coeffs[4, i] = jnp.where(lane == 0, 0.0, scaled * zl)
        coeffs[5, i] = scaled * zh
        goal = first * inverse
        coeffs[6, i] = goal
        update[i] = weights[0][1] * goal
        iterate[i] = weights[0][1] * goal
        return carry

    each(0, size_x, prepare)
    for pair in weights[1:]:
        start = iterate[0]

        def body(i, carry, pair=pair, start=start):
            below, here = carry
            if isinstance(i, int):
                above = start if i == size_x - 1 else iterate[i + 1]
            else:
                above = jnp.where(i == size_x - 1, start, iterate[following(i)])
            step = pair[1] * scaled_remain(coeffs, i, below, here, above) + pair[0] * update[i]
            update[i] = step
            iterate[i] = here + step
            return here, above

        each(0, size_x, body, (iterate[size_x - 1], start))


def window_kernel(
    fields_own, low_x1, high_x1, low_y1, high_y1, low_c1, high_c1,
    own, low_x, high_x, low_y, high_y, low_c, high_c,
    window, coeffs, own_windows, side_windows,
):
    size_x, size_y, size_z = own.shape
    assemble_owns(own_windows, fields_own, low_y1, high_y1)
    assemble_sides(side_windows, (size_y, size_z), low_x1, high_x1, low_c1, high_c1)
    end = FINE + size_x
    windows = Stack(
        (0, FINE, side_windows, 0), (FINE, end, own_windows, 0), (end, end + FINE, side_windows, FINE)
    )
    fields = [windows.of(field) for field in range(6)]
    scale_coeffs(1.0, *fields[2:], Stack((2, end + 3, coeffs, 0)), (2, end + 3), fields[1])
    assemble_own(window.at[FINE : FINE + size_x], own, low_y, high_y, 0, 0)
    assemble_side(window, FINE - 4, 4, (size_y, size_z), low_x, 0, low_c, 0, 3, True)
    assemble_side(window, FINE + size_x, 4, (size_y, size_z), high_x, 0, high_c, 0, 3, False)


def last_kernel(
    count_x, count_y, place, own_half, other_half, mid_coeffs, goal_in, fine_coeffs, window,
    out,
    low_fields, low_coeffs, low_iterate, low_update,
    goal, mid_iterate, mid_update, spread_mid,
    iterate, update, spread,
):
    size_x, size_y, size_z = out.shape
    mid_x, mid_y, mid_z = size_x // 2, size_y // 2, size_z // 2
    last = size_x + 2 * FINE - 2
    coeffs = Stack((2, last, fine_coeffs, 0))
    me_x, me_y = place[0], place[1]
    even = me_x % 2 == 0

    def half(which, device, tile):
        one, two = own_half[device, tile], other_half[device, tile]
        return jnp.where(even, one, two) if which == 0 else jnp.where(even, two, one)

    solve_low(count_x, count_y, half, low_fields, low_coeffs, low_iterate, low_update)

    def device(dx, dy):
        return lax.rem(me_x + dx + count_x, count_x) * count_y + lax.rem(me_y + dy + count_y, count_y)

    first, far = MID - mid_x, MID + 2 * mid_x
    for dy in (-1, 0, 1):
        rows = slice((dy + 1) * mid_y, (dy + 2) * mid_y)
        for dx in (-1, 0, 1):
            for plane in range(mid_x):
                mid_iterate[MID + dx * mid_x + plane, rows] = half(1, device(dx, dy), plane)
        for plane in range(first):
            mid_iterate[plane, rows] = half(1, device(-2, dy), mid_x - first + plane)
            mid_iterate[far + plane, rows] = half(1, device(2, dy), plane)
    low_size_x, low_size_y = low_iterate.shape[:2]
    low_planes, low_rows = (mid_x + 2 * MID) // 2, 16
    low_y = mid_y // 2
    turn = lax.rem(low_size_y - me_y * low_y + low_y, low_size_y)
    picked = []
    for plane in range(low_planes):
        at = lax.rem(me_x * (mid_x // 2) - MID // 2 + plane + low_size_x, low_size_x)
        picked.append(pltpu.roll(low_iterate[at], turn, 0)[:low_rows])
    wide = dot(jnp.concatenate(picked, axis=0), selector(mid_z, mid_z, lambda k, m: k == m // 2))
    count = low_planes * low_rows
    spread_mid[pl.ds(0, count, 2), :] = wide
    spread_mid[pl.ds(1, count, 2), :] = wide
    for plane in range(low_planes):
        part = spread_mid[plane * 2 * low_rows : plane * 2 * low_rows + 3 * mid_y]
        mid_iterate[2 * plane] += part
        mid_iterate[2 * plane + 1] += part

    for plane in range(first, far):
        goal[plane] = goal_in[plane]
    for dy in (-1, 0, 1):
        rows = slice((dy + 1) * mid_y, (dy + 2) * mid_y)
        for plane, dx in ((first - 1, -2), (far, 2)):
            goal[plane, rows] = half(0, device(dx, dy), 3) * mid_coeffs[6, plane, rows]
    for sweep, pair in enumerate(chebyshev_weights(SWEEPS)):
        sweep_window(
            mid_iterate, mid_update, mid_coeffs, (first - 1 + sweep, far + 1 - sweep), pair, sweep == 0, goal
        )

    fine_low = FINE - 4
    planes = mid_x + 4
    rows = mid_y + 8
    picked = [roll(mid_iterate[MID - 2 + plane], -4, 0)[:rows] for plane in range(planes)]
    wide = dot(jnp.concatenate(picked, axis=0), pair_copy(mid_z))
    count = planes * rows
    for side in range(2):
        lanes = slice(side * mid_z, (side + 1) * mid_z)
        spread[side, pl.ds(0, count, 2), :] = wide[:, lanes]
        spread[side, pl.ds(1, count, 2), :] = wide[:, lanes]
    for plane in range(planes):
        lines = slice(plane * 2 * rows, (plane + 1) * 2 * rows)
        part = jnp.concatenate([spread[0, lines], spread[1, lines]], axis=1)
        for at in (fine_low + 2 * plane, fine_low + 2 * plane + 1):
            iterate[at] = window[at] + part
    for sweep, pair in enumerate(chebyshev_weights(SWEEPS)):
        sweep_window(
            iterate, update, coeffs, (2 + sweep, last - sweep), pair, sweep == 0
        )
    for plane in range(size_x):
        out[plane] = iterate[FINE + plane, PAD : PAD + size_y]


def call(kernel, inputs, outs, scratch=(), scalars=0, far_in=(), far_out=(), sems=0):
    def place(i):
        return pltpu.SMEM if i < scalars else pltpu.HBM if i in far_in else pltpu.VMEM

    near = [x.shape for i, x in enumerate(inputs) if i >= scalars and i not in far_in]
    near += [shape for i, shape in enumerate(outs) if i not in far_out] + list(scratch)
    used = 4 * sum(math.prod(shape) for shape in near)
    inputs = [pltpu.with_memory_space_constraint(x, pltpu.HBM) if i in far_in else x for i, x in enumerate(inputs)]
    return pl.pallas_call(
        kernel,
        out_shape=[
            pltpu.HBM(shape, F32) if i in far_out else jax.ShapeDtypeStruct(shape, F32)
            for i, shape in enumerate(outs)
        ],
        in_specs=[pl.BlockSpec(memory_space=place(i)) for i in range(len(inputs))],
        out_specs=[
            pl.BlockSpec(memory_space=pltpu.HBM if i in far_out else pltpu.VMEM) for i in range(len(outs))
        ],
        scratch_shapes=[pltpu.VMEM(shape, F32) for shape in scratch]
        + ([pltpu.SemaphoreType.DMA((sems,))] if sems > 1 else [pltpu.SemaphoreType.DMA] * sems),
        cost_estimate=pl.CostEstimate(flops=1000, bytes_accessed=1000, transcendentals=0),
        compiler_params=pltpu.CompilerParams(vmem_limit_bytes=used + used // 4 + 2 * 1024 * 1024),
    )(*inputs)


def local(source, initial, absorption, beta_x, beta_y, beta_z):
    size_x, size_y, size_z = source.shape
    mid_x, mid_y, mid_z = size_x // 2, size_y // 2, size_z // 2
    low_x, low_y = mid_x // 2, mid_y // 2
    count_x, count_y = lax.axis_size("gx"), lax.axis_size("gy")
    devices = count_x * count_y
    plane, strip = tiles_of(size_y, size_z), tiles_of(8, size_z)
    mids = 4 * mid_x

    def tiles(count):
        return (count,) + TILE

    place = jnp.stack([lax.axis_index("gx"), lax.axis_index("gy")]).astype(jnp.int32)
    pairs = size_x // 2
    up_x, down_x, up_y, down_y, mid, low, own = call(
        pack_kernel,
        (initial, source, absorption, beta_x, beta_y, beta_z),
        [
            tiles(sum(UP_PLANES) * plane + mids),
            tiles(sum(DOWN_PLANES) * plane + mids),
            tiles((6 * pairs + 1) * strip + mids),
            tiles((6 * pairs + 2) * strip + mids),
            tiles(mids),
            tiles(3),
            (6,) + source.shape,
        ],
        [(4 * mid_x * size_y, mid_z)],
        far_in=range(6),
        sems=6,
    )
    low_x1, high_x1 = shifted(up_x, "gx", 1), shifted(down_x, "gx", -1)
    low_y1, high_y1 = shifted(up_y, "gy", 1), shifted(down_y, "gy", -1)
    up_c, down_c = call(
        functools.partial(corner_kernel, size_x, size_z),
        (low_y1, high_y1),
        [tiles(sum(UP_CORNER) * strip + MID_CORNER), tiles(sum(DOWN_CORNER) * strip + MID_CORNER)],
    )
    low_c1, high_c1 = shifted(up_c, "gx", 1), shifted(down_c, "gx", -1)

    tall = (size_y + 2 * PAD, size_z)
    wide = (size_x + 2 * FINE,) + tall
    own_windows, own_coeffs = call(
        own_kernel, (own, low_y1, high_y1), [(6, size_x) + tall, (8, size_x - 1) + tall]
    )
    iterate, mid_target, up_x, down_x, up_y, down_y = call(
        fine_kernel,
        (own_windows, own_coeffs, low_x1, high_x1, low_c1, high_c1),
        [
            source.shape,
            (mid_x, mid_y, mid_z),
            tiles(4 * plane + mid_x + 12),
            tiles(4 * plane + mid_x + 15),
            tiles(pairs * strip + mid_x),
            tiles(pairs * strip + mid_x),
        ],
        [(6, 2 * FINE) + tall, (8, 2 * FINE + 1) + tall, wide, wide, (mid_x * size_y, mid_z)],
    )
    low_x2, high_x2 = shifted(up_x, "gx", 1), shifted(down_x, "gx", -1)
    low_y2, high_y2 = shifted(up_y, "gy", 1), shifted(down_y, "gy", -1)
    up_c, down_c = call(
        functools.partial(corner_two_kernel, size_x, size_z),
        (low_y2, high_y2),
        [tiles(3 * strip + 2 * mid_x)] * 2,
    )
    low_c2, high_c2 = shifted(up_c, "gx", 1), shifted(down_c, "gx", -1)

    mid_wide = (mid_x + 2 * MID, 3 * mid_y, mid_z)
    (mid_coeffs,) = call(
        mid_coeffs_kernel,
        (mid, low_x1, high_x1, low_y1, high_y1, low_c1, high_c1, low_x2, high_x2),
        [(8,) + mid_wide],
        [(4,) + mid_wide],
    )
    goal, slots = call(
        functools.partial(mid_kernel, count_x, count_y),
        (place, low, mid_target, mid_coeffs, low_x2, high_x2, low_y2, high_y2, low_c2, high_c2),
        [mid_wide, (devices, 4) + TILE],
        [mid_wide] * 3 + [(low_x * mid_y, mid_z)],
        scalars=1,
    )
    own_half = lax.all_to_all(slots, ("gx", "gy"), 0, 0)
    other_half = lax.ppermute(own_half, "gx", [(i, i ^ 1) for i in range(count_x)])

    window, coeffs = call(
        window_kernel,
        (own, low_x1, high_x1, low_y1, high_y1, low_c1, high_c1)
        + (iterate, low_x2, high_x2, low_y2, high_y2, low_c2, high_c2),
        [wide, (7, wide[0] - 4) + tall],
        [(6, size_x) + tall, (6, 2 * FINE) + tall],
    )
    low_wide = (low_x * count_x, low_y * count_y, mid_z)
    low_planes = mid_wide[0] // 2
    (result,) = call(
        functools.partial(last_kernel, count_x, count_y),
        (place, own_half, other_half, mid_coeffs, goal, coeffs, window),
        [source.shape],
        [(3,) + low_wide, (7,) + low_wide, low_wide, low_wide]
        + [mid_wide, mid_wide, mid_wide, (low_planes * 32, mid_z)]
        + [wide, wide, (2, (mid_x + 4) * 2 * (mid_y + 8), mid_z)],
        scalars=1,
    )
    return result


def solution(mesh):
    spec = P("gx", "gy", None)
    return jax.shard_map(
        local, mesh=mesh, in_specs=(spec,) * 6, out_specs=spec, check_vma=False
    )
```

```python
import functools
import math

import jax
import jax.numpy as jnp
from jax import lax
from jax.experimental import pallas as pl
from jax.experimental.pallas import tpu as pltpu
from jax.sharding import PartitionSpec as P

SWEEPS = 4
COARSE_SWEEPS = 8
F32 = jnp.float32
TILE = (8, 128)
PAD = 8
FINE = 5
MID = 6


def chebyshev_weights(sweeps):
    cheb_theta = 1.125
    cheb_delta = 0.875
    cheb_sigma = cheb_theta / cheb_delta
    rho_old = 1.0 / cheb_sigma
    weights = [(0.0, 1.0 / cheb_theta)]
    for sweep in range(1, sweeps):
        rho_new = 1.0 / (2.0 * cheb_sigma - rho_old)
        weights.append((rho_new * rho_old, 2.0 * rho_new / cheb_delta))
        rho_old = rho_new
    return weights


def iota(shape, axis):
    return lax.broadcasted_iota(jnp.int32, shape, axis)


def selector(rows, columns, hit):
    return jnp.where(hit(iota((rows, columns), 0), iota((rows, columns), 1)), 1.0, 0.0).astype(F32)


def pair_sum(size):
    return selector(size, size // 2, lambda k, m: k // 2 == m)


def pair_copy(size):
    return selector(size, 2 * size, lambda k, m: k == m // 2)


def dot(left, right):
    return lax.dot(left, right, precision=lax.Precision.HIGHEST, preferred_element_type=F32)


def roll(value, shift, axis):
    return pltpu.roll(value, shift % value.shape[axis], axis)


def each(start, stop, body, carry=0):
    if stop - start > 20:
        return lax.fori_loop(start, stop, body, carry, unroll=2)
    for i in range(start, stop):
        carry = body(i, carry)
    return carry


class Writer:
    def __init__(self, ref):
        self.ref, self.at = ref, 0

    def put(self, value):
        rows, columns = value.shape
        for r in range(0, rows, TILE[0]):
            for c in range(0, columns, TILE[1]):
                self.ref[self.at] = value[r : r + TILE[0], c : c + TILE[1]]
                self.at += 1


class Reader:
    def __init__(self, ref, at=0):
        self.ref, self.at = ref, at

    def get(self, rows, columns):
        lines = []
        for _ in range(rows // TILE[0]):
            parts = []
            for _ in range(columns // TILE[1]):
                parts.append(self.ref[self.at])
                self.at += 1
            lines.append(parts[0] if len(parts) == 1 else jnp.concatenate(parts, axis=1))
        return lines[0] if len(lines) == 1 else jnp.concatenate(lines, axis=0)


UP_PLANES = (5, 4, 4, 4, 4, 4)
DOWN_PLANES = (5, 4, 4, 5, 4, 4)
UP_CORNER = (4, 3, 3, 3, 4, 3)
DOWN_CORNER = (4, 3, 3, 4, 4, 3)
STRIP = 3


def corner_tiles(counts):
    return sum(count - 1 for count in counts)


def tiles_of(rows, columns):
    return (rows // TILE[0]) * (columns // TILE[1])


def is_upper(width):
    return iota((TILE[0], width), 0) < TILE[0] // 2


def shifted(value, axis, step):
    count = lax.axis_size(axis)
    return lax.ppermute(value, axis, [(i, (i + step) % count) for i in range(count)])


def pack_kernel(
    ini_in, src_in, absorb_in, face_x_in, face_y_in, face_z_in,
    up_x, down_x, up_y, down_y, mid, low, own, rows_mid, sems,
):
    copies = []
    for field, ref in enumerate((ini_in, src_in, absorb_in, face_x_in, face_y_in, face_z_in)):
        copies.append(pltpu.make_async_copy(ref, own.at[field], sems.at[field]))
        copies[-1].start()
    for copy in copies:
        copy.wait()
    fields = tuple(own.at[field] for field in range(6))
    ini, src, absorb, face_x, face_y, face_z = fields
    size_x, size_y, size_z = ini.shape
    half = size_y // 2
    blocks = range(0, size_x, 2)

    def both_planes(ref):
        return [ref[plane] + ref[plane + 1] for plane in blocks]

    stacked = both_planes(absorb) + [face_x[plane] for plane in blocks] + both_planes(face_y)
    summed = dot(jnp.concatenate(stacked, axis=0), pair_sum(size_z))
    picked = dot(
        jnp.concatenate(both_planes(face_z), axis=0),
        selector(size_z, size_z // 2, lambda k, m: k == 2 * m),
    )
    count = summed.shape[0]
    rows_mid[:count] = summed
    rows_mid[count:] = picked
    out = Writer(mid)
    for array, (factor, sides) in enumerate(((0.125, 2), (0.25, 2), (0.25, 1), (0.25, 2))):
        lines = (size_x // 2) * half
        start = 2 * array * lines
        total = rows_mid[pl.ds(start, lines, 2), :]
        if sides == 2:
            total = total + rows_mid[pl.ds(start + 1, lines, 2), :]
        out.put(total * factor)

    mid_x, mid_z = size_x // 2, size_z // 2
    both = (0, 1)
    low_z = mid_z // 2

    def coarser(array, planes, sides):
        lines = []
        for block in range(mid_x // 2):
            total = None
            for plane in planes:
                for side in sides:
                    at = array * mid_x + 2 * block + plane
                    part = mid[at, pl.ds(side, half // 2, 2), :]
                    total = part if total is None else total + part
            lines.append(total)
        return jnp.concatenate(lines, axis=0)

    left = selector(mid_z, mid_z, lambda k, m: k // 2 == m)
    right = selector(mid_z, mid_z, lambda k, m: k // 2 == m - low_z)
    evens = selector(mid_z, mid_z, lambda k, m: k == 2 * m)
    low[0] = dot(coarser(0, both, both) * 0.125, right)
    low[1] = dot(coarser(1, (0,), both) * 0.25, left) + dot(coarser(2, both, (0,)) * 0.25, right)
    low[2] = dot(coarser(3, both, both) * 0.25, evens)

    tops, bottoms = Writer(up_x), Writer(down_x)
    for ref, count in zip(fields, UP_PLANES):
        for plane in range(size_x - count, size_x):
            tops.put(ref[plane])
    for ref, count in zip(fields, DOWN_PLANES):
        for plane in range(count):
            bottoms.put(ref[plane])

    upper = is_upper(size_z)
    tops_y, bottoms_y = Writer(up_y), Writer(down_y)
    for ref in fields:
        for pair in range(0, size_x, 2):
            one, two = ref[pair], ref[pair + 1]
            tops_y.put(jnp.where(upper, roll(one[size_y - 8 :], 4, 0), two[size_y - 8 :]))
            bottoms_y.put(jnp.where(upper, one[:8], roll(two[:8], 4, 0)))
    tops_y.put(ini[:, size_y - 5, :])
    bottoms_y.put(ini[:, 4, :])
    bottoms_y.put(face_y[:, 4, :])
    for writer in (tops_y, bottoms_y):
        for tile in (1, 2):
            writer.put(low[tile])
    row, upper = iota(TILE, 0), is_upper(TILE[1])
    for array in range(4):
        parts = [mid[array * mid_x + plane] for plane in range(mid_x)]
        for pair in range(0, mid_x, 2):
            one, two = parts[pair], parts[pair + 1]
            tops_y.put(jnp.where(upper, roll(one, 4, 0), two))
            bottoms_y.put(jnp.where(upper, one, roll(two, 4, 0)))
        far_low, far_high = roll(parts[0], -2, 0), roll(parts[0], -4, 0)
        for plane in range(1, mid_x):
            far_low = jnp.where(row < 2 * plane, far_low, roll(parts[plane], 2 * plane - 2, 0))
            far_high = jnp.where(row < 2 * plane, far_high, roll(parts[plane], 2 * plane - 4, 0))
        tops_y.put(far_low)
        bottoms_y.put(far_high)


def corner_of(low_y, high_y, plane, upper, first_tile=0):
    width = upper.shape[1]
    at = first_tile + (plane // 2) * tiles_of(8, width)
    low = Reader(low_y, at).get(8, width)
    high = Reader(high_y, at).get(8, width)
    if plane % 2 == 0:
        return jnp.where(upper, low, roll(high, 4, 0))
    return jnp.where(upper, roll(low, 4, 0), high)


def mix(near, far):
    row = iota(near.shape, 0)
    return jnp.where((row >= 2) & (row < 6), near, roll(far, 3, 0))


def put_corners(writer, low_y, high_y, planes, upper, first_tile):
    parts = [corner_of(low_y, high_y, plane, upper, first_tile) for plane in planes]
    for part in parts[:-2]:
        writer.put(part)
    writer.put(mix(*parts[-2:]))


def mid_strip(ref, array, plane, low):
    start = ref.shape[0] - 4 * STRIP + array * STRIP
    near, far, row = ref[start + plane // 2], ref[start + 2], iota(TILE, 0)
    if (plane % 2 == 0) == low:
        near = roll(near, 4, 0)
    far = roll(far, (2 if low else 4) - 2 * plane, 0)
    return jnp.where(row >= 4, near, far) if low else jnp.where(row < 4, near, far)


def corner_kernel(size_x, size_z, low_y, high_y, mid, low_faces, up, down):
    upper = is_upper(size_z)
    per_field = (size_x // 2) * tiles_of(8, size_z)
    tops, bottoms = Writer(up), Writer(down)
    for field in range(6):
        start = field * per_field
        planes = [size_x - 1 - plane for plane in range(UP_CORNER[field])]
        put_corners(tops, low_y, high_y, planes, upper, start)
        put_corners(bottoms, low_y, high_y, range(DOWN_CORNER[field]), upper, start)
    mid_x = size_x // 2
    upper = is_upper(TILE[1])
    for writer, wanted in (
        (tops, [(array, mid_x - 1) for array in range(4)]),
        (bottoms, [(array, 0) for array in range(4)] + [(1, 1)]),
    ):
        for array, plane in wanted:
            writer.put(
                jnp.where(upper, mid_strip(high_y, array, plane, False), mid_strip(low_y, array, plane, True))
            )
        for array, plane in wanted:
            writer.put(mid[array * mid_x + plane])
        for tiles in ((low_faces[1], low_faces[2]), low_tiles_of(low_y), low_tiles_of(high_y)):
            for tile in tiles:
                writer.put(tile)


def low_tiles_of(ref):
    end = ref.shape[0] - 4 * STRIP
    return ref[end - 2], ref[end - 1]


class Planes:
    def __init__(self, *parts):
        self.parts = parts
        self.shape = parts[0][2].shape

    def find(self, i):
        for start, stop, ref, offset, lead in self.parts:
            if start <= i < stop:
                return ref, lead + (i - start + offset,)
        raise IndexError(i)

    def __getitem__(self, i):
        ref, index = self.find(i)
        return ref[index]


class Stack:
    def __init__(self, *parts):
        self.parts = parts

    def of(self, kind):
        return Planes(*((a, b, ref, offset, (kind,)) for a, b, ref, offset in self.parts))

    def __getitem__(self, index):
        return self.of(index[0])[index[1]]

    def __setitem__(self, index, value):
        ref, place = self.of(index[0]).find(index[1])
        ref[place] = value


def scale_coeffs(scale, absorb, face_x, face_y, face_z, coeffs, planes, target=None, diagonal=None):
    rows, lanes = absorb.shape[-2:]
    lane = iota((rows, lanes), 1)

    def body(i, carry):
        xl, xh = face_x[i], face_x[i + 1]
        yl, zl = face_y[i], face_z[i]
        yh = roll(yl, -1, 0)
        zh = jnp.where(lane == lanes - 1, 0.0, roll(zl, -1, 1))
        diag = absorb[i] + scale * (xl + xh + yl + yh + zl + zh)
        inverse = 1.0 / diag
        scaled = scale * inverse
        coeffs[0, i] = scaled * xl
        coeffs[1, i] = scaled * xh
        coeffs[2, i] = scaled * yl
        coeffs[3, i] = scaled * yh
        coeffs[4, i] = jnp.where(lane == 0, 0.0, scaled * zl)
        coeffs[5, i] = scaled * zh
        if target is not None:
            coeffs[6, i] = target[i] * inverse
        else:
            coeffs[6, i] = inverse
        if diagonal is not None:
            coeffs[7, i] = diag
        return carry

    each(*planes, body)


def scaled_remain(coeffs, i, below, here, above, goal=None):
    total = (coeffs[6, i] if goal is None else goal[i]) - here
    total = total + coeffs[0, i] * below + coeffs[1, i] * above
    total = total + coeffs[2, i] * roll(here, 1, 0) + coeffs[3, i] * roll(here, -1, 0)
    return total + coeffs[4, i] * roll(here, 1, 1) + coeffs[5, i] * roll(here, -1, 1)


def sweep_window(iterate, update, coeffs, planes, pair, first, goal=None, source=None):
    start, stop = planes
    source = iterate if source is None else source

    def body(i, carry):
        below, here = carry
        above = source[i + 1]
        step = pair[1] * scaled_remain(coeffs, i, below, here, above, goal)
        if not first:
            step = step + pair[0] * update[i]
        update[i] = step
        iterate[i] = here + step
        return here, above

    each(start, stop, body, (source[start - 1], source[start]))


def assemble_own(window, own, low_y, high_y, low_start, high_start):
    size_x, size_y, size_z = own.shape
    high = PAD + size_y
    low_reader, high_reader = Reader(low_y, low_start), Reader(high_y, high_start)
    for pair in range(0, size_x, 2):
        window[pair, PAD:high] = own[pair]
        window[pair + 1, PAD:high] = own[pair + 1]
        tile = low_reader.get(8, size_z)
        window[pair, 0:8] = roll(tile, 4, 0)
        window[pair + 1, 0:8] = tile
        tile = high_reader.get(8, size_z)
        window[pair, high : high + 8] = tile
        window[pair + 1, high : high + 8] = roll(tile, 4, 0)


def assemble_side(window, first, count, rows, planes, plane_start, corners, corner_start, corner_count, from_end):
    size_y, size_z = rows
    high = PAD + size_y
    reader = Reader(planes, plane_start)
    for plane in range(count):
        window[first + plane, PAD:high] = reader.get(size_y, size_z)
    reader = Reader(corners, corner_start)
    tiles = [roll(reader.get(8, size_z), 4, 0) for _ in range(corner_count - 1)]
    tiles.append(roll(tiles[-1], -3, 0))
    for plane, tile in enumerate(tiles):
        at = first + count - 1 - plane if from_end else first + plane
        window[at, 0:8] = tile
        window[at, high : high + 8] = tile


def assemble_owns(windows, own, low_y, high_y):
    size_x, size_y, size_z = own.shape[1:]
    per_field = (size_x // 2) * tiles_of(8, size_z)
    for field in range(6):
        assemble_own(windows.at[field], own.at[field], low_y, high_y, field * per_field, field * per_field)
    low_line = Reader(low_y, 6 * per_field).get(8, size_z)
    high_reader = Reader(high_y, 6 * per_field)
    high_line = high_reader.get(8, size_z)
    face_line = high_reader.get(8, size_z)
    high = PAD + size_y
    for plane in range(size_x):
        windows[0, plane, 3:4] = low_line[plane : plane + 1]
        windows[0, plane, high + 4 : high + 5] = high_line[plane : plane + 1]
        windows[4, plane, high + 4 : high + 5] = face_line[plane : plane + 1]


def assemble_sides(side_windows, rows, low_x, high_x, low_c, high_c):
    plane_tiles, strip_tiles = tiles_of(*rows), tiles_of(8, rows[1])
    starts = [0] * 4
    for field in range(6):
        up, down, up_c, down_c = (
            kinds[field] for kinds in (UP_PLANES, DOWN_PLANES, UP_CORNER, DOWN_CORNER)
        )
        window = side_windows.at[field]
        assemble_side(
            window, FINE - up, up, rows, low_x, starts[0], low_c, starts[2], up_c, True
        )
        assemble_side(
            window, FINE, down, rows, high_x, starts[1], high_c, starts[3], down_c, False
        )
        starts[0] += up * plane_tiles
        starts[1] += down * plane_tiles
        starts[2] += (up_c - 1) * strip_tiles
        starts[3] += (down_c - 1) * strip_tiles


def own_kernel(own, low_y, high_y, windows, coeffs, up_corner, down_corner):
    assemble_owns(windows, own, low_y, high_y)
    fields = [windows.at[field] for field in range(6)]
    scale_coeffs(1.0, *fields[2:], coeffs, (0, own.shape[1] - 1), fields[1], True)
    mid_x = own.shape[1] // 2
    tops, bottoms = Writer(up_corner), Writer(down_corner)
    upper = is_upper(TILE[1])
    sides = ((low_y, True), (high_y, False))
    for writer, first, step in ((tops, mid_x - 1, -1), (bottoms, 0, 1)):
        for array in range(4):
            for q in range(2):
                for ref, low in sides:
                    writer.put(mid_strip(ref, array, first + q * step, low))
        for array in range(4):
            for q in range(2, 4):
                one, two = (roll(mid_strip(ref, array, first + q * step, low), 4, 0) for ref, low in sides)
                writer.put(jnp.where(upper, one, two))


def fine_kernel(
    own_windows, own_coeffs, up_corner, down_corner, mid, low_x, high_x, low_c, high_c,
    iterate_out, mid_target, up_x, down_x, up_y, down_y,
    side_windows, side_coeffs, iterate, update, rest,
):
    size_x, size_z = own_windows.shape[1], own_windows.shape[3]
    size_y = own_windows.shape[2] - 2 * PAD
    assemble_sides(side_windows, (size_y, size_z), low_x, high_x, low_c, high_c)
    end = FINE + size_x
    last = end + FINE - 1
    windows = Stack(
        (0, FINE, side_windows, 0), (FINE, end, own_windows, 0), (end, last + 1, side_windows, FINE)
    )
    coeffs = Stack(
        (0, FINE, side_coeffs, 0), (FINE, end - 1, own_coeffs, 0), (end - 1, last + 1, side_coeffs, FINE)
    )
    fields = [windows.of(field) for field in range(6)]
    scale_coeffs(1.0, *fields[2:], coeffs, (1, FINE), fields[1], True)
    scale_coeffs(1.0, *fields[2:], coeffs, (end - 1, last), fields[1], True)
    for sweep, pair in enumerate(chebyshev_weights(SWEEPS)):
        sweep_window(
            iterate, update, coeffs, (1 + sweep, last - sweep), pair, sweep == 0,
            source=fields[0] if sweep == 0 else None,
        )
    mid_x, mid_y = size_x // 2, size_y // 2
    lines = []
    for block in range(mid_x):
        total = None
        for plane in (FINE + 2 * block, FINE + 2 * block + 1):
            remain = scaled_remain(coeffs, plane, iterate[plane - 1], iterate[plane], iterate[plane + 1])
            remain = (remain * coeffs[7, plane])[PAD : PAD + size_y]
            total = remain if total is None else total + remain
        lines.append(total)
    rest[...] = dot(jnp.concatenate(lines, axis=0), pair_sum(size_z))
    count = mid_x * mid_y
    coarse = (rest[pl.ds(0, count, 2), :] + rest[pl.ds(1, count, 2), :]) * 0.125
    for block in range(mid_x):
        mid_target[block] = coarse[block * mid_y : (block + 1) * mid_y]
    for plane in range(size_x):
        iterate_out[plane] = iterate[FINE + plane, PAD : PAD + size_y]

    tops, bottoms = Writer(up_x), Writer(down_x)
    for plane in range(size_x - 4, size_x):
        tops.put(iterate_out[plane])
    for plane in range(4):
        bottoms.put(iterate_out[plane])
    upper = is_upper(size_z)
    tops_y, bottoms_y = Writer(up_y), Writer(down_y)
    for pair in range(0, size_x, 2):
        one, two = iterate_out[pair], iterate_out[pair + 1]
        tops_y.put(jnp.where(upper, roll(one[size_y - 8 :], 4, 0), two[size_y - 8 :]))
        bottoms_y.put(jnp.where(upper, one[:8], roll(two[:8], 4, 0)))
    for writer in (tops, bottoms, tops_y, bottoms_y):
        writer.put(coarse)
    for writer, ref in ((tops, up_corner), (bottoms, down_corner)):
        for tile in range(MID_CORNER):
            writer.put(ref[tile])
    for writer in (tops, bottoms):
        for tile in range(mid.shape[0]):
            writer.put(mid[tile])
    for writer, corners, extra in ((tops, low_c, 4), (bottoms, high_c, 5)):
        start = corners.shape[0] - PASSED - 2 * extra
        for tile in range(start, corners.shape[0]):
            writer.put(corners[tile])


MID_CORNER = 24
PASSED = 6


def whole_corner(ref, start, array, q, side):
    return ref[start + (array * 2 + q) * 2 + side]


def part_corner(ref, start, array, q):
    return ref[start + 16 + array * 2 + q - 2]


def corner_two_kernel(size_x, size_z, low_y, high_y, up, down):
    upper = is_upper(size_z)
    tops, bottoms = Writer(up), Writer(down)
    put_corners(tops, low_y, high_y, [size_x - 1, size_x - 2, size_x - 3], upper, 0)
    put_corners(bottoms, low_y, high_y, range(3), upper, 0)
    for writer in (tops, bottoms):
        for ref in (low_y, high_y):
            for tile in range(ref.shape[0] - size_x // 2, ref.shape[0]):
                writer.put(ref[tile])


def mid_coeffs_kernel(mid, low_y, high_y, low_x2, high_x2, coeffs, window):
    mid_y, mid_z = mid.shape[1:]
    mid_x = mid.shape[0] // 4
    mids = 4 * mid_x
    first = MID - mid_x
    corner = 4 * tiles_of(2 * mid_y, 2 * mid_z) + mid_x
    passed = corner + MID_CORNER
    for ref, start, block in ((low_x2, passed, 0), (mid, 0, 1), (high_x2, passed, 2)):
        for array in range(4):
            for plane in range(mid_x):
                window[array, first + block * mid_x + plane, mid_y : 2 * mid_y] = ref[start + array * mid_x + plane]
    for array in range(4):
        for plane in range(mid_x):
            window[array, MID + plane, :mid_y] = mid_strip(low_y, array, plane, True)
            window[array, MID + plane, 2 * mid_y :] = mid_strip(high_y, array, plane, False)
    passed += mids
    far = 3 * mid_x + first
    for ref, start, step, end, extra in (
        (low_x2, MID - 1, -1, first - 1, 4), (high_x2, MID + mid_x, 1, far, 5)
    ):
        for array in range(4):
            for q in range(mid_x):
                if q < 2:
                    one, two = (whole_corner(ref, corner, array, q, side) for side in range(2))
                else:
                    one = two = roll(part_corner(ref, corner, array, q), 4, 0)
                window[array, start + q * step, :mid_y] = one
                window[array, start + q * step, 2 * mid_y :] = two
        for place in range(extra):
            array, plane = (place, end) if place < 4 else (1, end + 1)
            window[array, plane, :mid_y] = ref[passed + place]
            window[array, plane, 2 * mid_y :] = ref[passed + place]
            window[array, plane, mid_y : 2 * mid_y] = ref[passed + extra + place]
    scale_coeffs(0.25, *(window.at[array] for array in range(4)), coeffs, (first - 1, far + 1), None, True)


def mid_kernel(
    count_x, count_y, place, low, mid_target, coeffs, low_x2, high_x2, low_y2, high_y2, low_c2, high_c2,
    goal, slots, target, iterate, update, rest,
):
    mid_x, mid_y, mid_z = mid_target.shape
    first = MID - mid_x
    far = 3 * mid_x + first
    fine_tiles = 4 * tiles_of(2 * mid_y, 2 * mid_z)
    blocks = {
        (0, 0): (low_c2, low_c2.shape[0] - 2 * mid_x), (0, 1): (low_x2, fine_tiles),
        (0, 2): (low_c2, low_c2.shape[0] - mid_x), (1, 0): (low_y2, low_y2.shape[0] - mid_x),
        (1, 2): (high_y2, high_y2.shape[0] - mid_x),
        (2, 0): (high_c2, high_c2.shape[0] - 2 * mid_x), (2, 1): (high_x2, fine_tiles),
        (2, 2): (high_c2, high_c2.shape[0] - mid_x),
    }
    for plane in range(mid_x):
        target[MID + plane, mid_y : 2 * mid_y] = mid_target[plane]
    for (bx, by), (ref, start) in blocks.items():
        for plane in range(mid_x):
            target[first + bx * mid_x + plane, by * mid_y : (by + 1) * mid_y] = ref[start + plane]

    weights = chebyshev_weights(SWEEPS)

    def start_sweep(i, carry):
        value = target[i] * coeffs[6, i]
        goal[i] = value
        update[i] = weights[0][1] * value
        iterate[i] = weights[0][1] * value
        return carry

    each(first, far, start_sweep)
    for sweep in range(1, SWEEPS):
        sweep_window(iterate, update, coeffs, (first + sweep, far - sweep), weights[sweep], False, goal)
    low_x_size = mid_x // 2
    for block in range(low_x_size):
        total = None
        for plane in (MID + 2 * block, MID + 2 * block + 1):
            remain = scaled_remain(coeffs, plane, iterate[plane - 1], iterate[plane], iterate[plane + 1], goal)
            remain = (remain * coeffs[7, plane])[mid_y : 2 * mid_y]
            total = remain if total is None else total + remain
        rest[block * mid_y : (block + 1) * mid_y] = total
    count = low_x_size * mid_y // 2
    summed = rest[pl.ds(0, count, 2), :] + rest[pl.ds(1, count, 2), :]
    coarse = dot(summed * 0.125, selector(mid_z, mid_z, lambda k, m: k // 2 == m))
    tiles = (coarse + low[0], low[1], low[2])
    x1 = [iterate[MID + plane, mid_y : 2 * mid_y] for plane in range(mid_x)]
    pairs = count_x // 2
    own, even = place[0] // 2, place[0] % 2 == 0
    above, below = lax.rem(own + 1, pairs), lax.rem(own + pairs - 1, pairs)

    def fill(i, carry):
        up, down = i == above, i == below
        edge = jnp.where(up, mid_target[mid_x - 1], mid_target[0])
        near_pair = up | down | (i == own)
        far_side = (up & even) | (down & jnp.logical_not(even))
        for j in range(count_y):
            me = place[1]
            beside = (j == me) | (j == lax.rem(me + 1, count_y)) | (j == lax.rem(me + count_y - 1, count_y))
            near, side = near_pair & beside, far_side & beside
            one, two = 2 * i * count_y + j, (2 * i + 1) * count_y + j
            slots[one, 0] = tiles[0]
            slots[one, 1] = jnp.where(near, edge, tiles[1])
            slots[one, 2] = jnp.where(near, jnp.where(side & even, x1[2], x1[0]), tiles[2])
            slots[two, 0] = jnp.where(near, jnp.where(side, tiles[1], x1[1]), tiles[0])
            slots[two, 1] = jnp.where(near, jnp.where(side, tiles[2], x1[2]), tiles[1])
            slots[two, 2] = jnp.where(
                near, jnp.where(side & jnp.logical_not(even), x1[1], x1[3]), tiles[2]
            )
        return carry

    each(0, pairs, fill)


def solve_low(count_x, count_y, gathered, fields, coeffs, iterate, update):
    size_x, size_y, lanes = iterate.shape
    low_x, low_y = size_x // count_x, size_y // count_y
    low_z = lanes // 2

    def place(i, carry):
        for j in range(count_y):
            for kind in range(3):
                tile = gathered[i * count_y + j, kind]
                for plane in range(low_x):
                    fields[kind, i * low_x + plane, j * low_y : (j + 1) * low_y] = tile[
                        plane * low_y : (plane + 1) * low_y
                    ]
        return carry

    each(0, count_x, place)
    lane = iota((size_y, lanes), 1)
    inside = lane < low_z
    scale = 0.0625
    weights = chebyshev_weights(COARSE_SWEEPS)

    def following(i):
        if isinstance(i, int):
            return (i + 1) % size_x
        return jnp.where(i == size_x - 1, 0, i + 1)

    def prepare(i, carry):
        first, second, third = fields[0, i], fields[1, i], fields[2, i]
        xl, xh = second, fields[1, following(i)]
        yl = roll(second, low_z, 1)
        yh = roll(yl, -1, 0)
        zl = third
        zh = jnp.where(lane == low_z - 1, 0.0, roll(third, -1, 1))
        diag = roll(first, low_z, 1) + scale * (xl + xh + yl + yh + zl + zh)
        inverse = jnp.where(inside, 1.0 / diag, 0.0)
        scaled = scale * inverse
        coeffs[0, i] = scaled * xl
        coeffs[1, i] = scaled * xh
        coeffs[2, i] = scaled * yl
        coeffs[3, i] = scaled * yh
        coeffs[4, i] = jnp.where(lane == 0, 0.0, scaled * zl)
        coeffs[5, i] = scaled * zh
        goal = first * inverse
        coeffs[6, i] = goal
        update[i] = weights[0][1] * goal
        iterate[i] = weights[0][1] * goal
        return carry

    each(0, size_x, prepare)
    for pair in weights[1:]:
        start = iterate[0]

        def body(i, carry, pair=pair, start=start):
            below, here = carry
            if isinstance(i, int):
                above = start if i == size_x - 1 else iterate[i + 1]
            else:
                above = jnp.where(i == size_x - 1, start, iterate[following(i)])
            step = pair[1] * scaled_remain(coeffs, i, below, here, above) + pair[0] * update[i]
            update[i] = step
            iterate[i] = here + step
            return here, above

        each(0, size_x, body, (iterate[size_x - 1], start))


def window_kernel(
    fields_own, low_x1, high_x1, low_y1, high_y1, low_c1, high_c1,
    own, low_x, high_x, low_y, high_y, low_c, high_c,
    low, window, coeffs, near, own_windows, side_windows,
):
    known = {(0, 0): (low[1], low[2]), (0, -1): low_tiles_of(low_y1), (0, 1): low_tiles_of(high_y1)}
    for step, ref, distance in ((-1, low_c1, 1), (1, high_c1, 1), (-1, low_x, 2), (1, high_x, 2)):
        start = ref.shape[0] - PASSED
        for place, dy in enumerate((0, -1, 1)):
            known[step * distance, dy] = (ref[start + 2 * place], ref[start + 2 * place + 1])
    for (dx, dy), tiles in known.items():
        for kind in range(2):
            near[((dx + 2) * 3 + dy + 1) * 2 + kind] = tiles[kind]
    size_x, size_y, size_z = own.shape
    assemble_owns(own_windows, fields_own, low_y1, high_y1)
    assemble_sides(side_windows, (size_y, size_z), low_x1, high_x1, low_c1, high_c1)
    end = FINE + size_x
    windows = Stack(
        (0, FINE, side_windows, 0), (FINE, end, own_windows, 0), (end, end + FINE, side_windows, FINE)
    )
    fields = [windows.of(field) for field in range(6)]
    scale_coeffs(1.0, *fields[2:], Stack((2, end + 3, coeffs, 0)), (2, end + 3), fields[1])
    assemble_own(window.at[FINE : FINE + size_x], own, low_y, high_y, 0, 0)
    assemble_side(window, FINE - 4, 4, (size_y, size_z), low_x, 0, low_c, 0, 3, True)
    assemble_side(window, FINE + size_x, 4, (size_y, size_z), high_x, 0, high_c, 0, 3, False)


def last_kernel(
    count_x, count_y, place, own_half, other_half, mid_coeffs, goal_in, fine_coeffs, window, near,
    out,
    gathered, low_fields, low_coeffs, low_iterate, low_update,
    goal, mid_iterate, mid_update, spread_mid,
    iterate, update, spread,
):
    size_x, size_y, size_z = out.shape
    mid_x, mid_y, mid_z = size_x // 2, size_y // 2, size_z // 2
    last = size_x + 2 * FINE - 2
    coeffs = Stack((2, last, fine_coeffs, 0))
    me_x, me_y = place[0], place[1]
    even = me_x % 2 == 0

    def half(which, device, tile):
        one, two = own_half[device, tile], other_half[device, tile]
        return jnp.where(even, one, two) if which == 0 else jnp.where(even, two, one)

    def device(dx, dy):
        return lax.rem(me_x + dx + count_x, count_x) * count_y + lax.rem(me_y + dy + count_y, count_y)

    def take(i, carry):
        for kind in range(3):
            gathered[i, kind] = half(0, i, kind)
        return carry

    each(0, count_x * count_y, take)
    side = me_x % 2
    for dy in (-1, 0, 1):
        for source in (device(-2 - side, dy), device(3 - side, dy)):
            for kind in range(2):
                gathered[source, 1 + kind] = half(1, source, kind)
    for dy in (-1, 0, 1):
        for dx in range(-2, 3):
            for kind in range(2):
                gathered[device(dx, dy), 1 + kind] = near[((dx + 2) * 3 + dy + 1) * 2 + kind]
    solve_low(count_x, count_y, gathered, low_fields, low_coeffs, low_iterate, low_update)

    first, far = MID - mid_x, MID + 2 * mid_x
    for dy in (-1, 0, 1):
        rows = slice((dy + 1) * mid_y, (dy + 2) * mid_y)
        for dx in (-1, 0, 1):
            source = device(dx, dy)
            start = MID + dx * mid_x
            mid_iterate[start, rows] = half(0, source, 2)
            for plane in range(1, mid_x):
                mid_iterate[start + plane, rows] = half(1, source, plane - 1)
        source = device(-2, dy)
        mid_iterate[0, rows] = jnp.where(even, half(0, source, 2), half(1, source, 1))
        mid_iterate[1, rows] = half(1, source, 2)
        source = device(2, dy)
        mid_iterate[far, rows] = half(0, source, 2)
        mid_iterate[far + 1, rows] = jnp.where(even, half(1, source, 0), half(1, source, 2))
    low_size_x, low_size_y = low_iterate.shape[:2]
    low_planes, low_rows = (mid_x + 2 * MID) // 2, 16
    low_y = mid_y // 2
    turn = lax.rem(low_size_y - me_y * low_y + low_y, low_size_y)
    picked = []
    for plane in range(low_planes):
        at = lax.rem(me_x * (mid_x // 2) - MID // 2 + plane + low_size_x, low_size_x)
        picked.append(pltpu.roll(low_iterate[at], turn, 0)[:low_rows])
    wide = dot(jnp.concatenate(picked, axis=0), selector(mid_z, mid_z, lambda k, m: k == m // 2))
    count = low_planes * low_rows
    spread_mid[pl.ds(0, count, 2), :] = wide
    spread_mid[pl.ds(1, count, 2), :] = wide
    for plane in range(low_planes):
        part = spread_mid[plane * 2 * low_rows : plane * 2 * low_rows + 3 * mid_y]
        mid_iterate[2 * plane] += part
        mid_iterate[2 * plane + 1] += part

    for plane in range(first, far):
        goal[plane] = goal_in[plane]
    for dy in (-1, 0, 1):
        rows = slice((dy + 1) * mid_y, (dy + 2) * mid_y)
        for plane, dx in ((first - 1, -2), (far, 2)):
            goal[plane, rows] = half(0, device(dx, dy), 1) * mid_coeffs[6, plane, rows]
    for sweep, pair in enumerate(chebyshev_weights(SWEEPS)):
        sweep_window(
            mid_iterate, mid_update, mid_coeffs, (first - 1 + sweep, far + 1 - sweep), pair, sweep == 0, goal
        )

    fine_low = FINE - 4
    planes = mid_x + 4
    rows = mid_y + 8
    picked = [roll(mid_iterate[MID - 2 + plane], -4, 0)[:rows] for plane in range(planes)]
    wide = dot(jnp.concatenate(picked, axis=0), pair_copy(mid_z))
    count = planes * rows
    for side in range(2):
        lanes = slice(side * mid_z, (side + 1) * mid_z)
        spread[side, pl.ds(0, count, 2), :] = wide[:, lanes]
        spread[side, pl.ds(1, count, 2), :] = wide[:, lanes]
    for plane in range(planes):
        lines = slice(plane * 2 * rows, (plane + 1) * 2 * rows)
        part = jnp.concatenate([spread[0, lines], spread[1, lines]], axis=1)
        for at in (fine_low + 2 * plane, fine_low + 2 * plane + 1):
            iterate[at] = window[at] + part
    for sweep, pair in enumerate(chebyshev_weights(SWEEPS)):
        sweep_window(
            iterate, update, coeffs, (2 + sweep, last - sweep), pair, sweep == 0
        )
    for plane in range(size_x):
        out[plane] = iterate[FINE + plane, PAD : PAD + size_y]


def call(kernel, inputs, outs, scratch=(), scalars=0, far_in=(), far_out=(), sems=0):
    def place(i):
        return pltpu.SMEM if i < scalars else pltpu.HBM if i in far_in else pltpu.VMEM

    near = [x.shape for i, x in enumerate(inputs) if i >= scalars and i not in far_in]
    near += [shape for i, shape in enumerate(outs) if i not in far_out] + list(scratch)
    used = 4 * sum(math.prod(shape) for shape in near)
    inputs = [pltpu.with_memory_space_constraint(x, pltpu.HBM) if i in far_in else x for i, x in enumerate(inputs)]
    return pl.pallas_call(
        kernel,
        out_shape=[
            pltpu.HBM(shape, F32) if i in far_out else jax.ShapeDtypeStruct(shape, F32)
            for i, shape in enumerate(outs)
        ],
        in_specs=[pl.BlockSpec(memory_space=place(i)) for i in range(len(inputs))],
        out_specs=[
            pl.BlockSpec(memory_space=pltpu.HBM if i in far_out else pltpu.VMEM) for i in range(len(outs))
        ],
        scratch_shapes=[pltpu.VMEM(shape, F32) for shape in scratch]
        + ([pltpu.SemaphoreType.DMA((sems,))] if sems > 1 else [pltpu.SemaphoreType.DMA] * sems),
        cost_estimate=pl.CostEstimate(flops=1000, bytes_accessed=1000, transcendentals=0),
        compiler_params=pltpu.CompilerParams(vmem_limit_bytes=used + used // 4 + 2 * 1024 * 1024),
    )(*inputs)


def local(source, initial, absorption, beta_x, beta_y, beta_z):
    size_x, size_y, size_z = source.shape
    mid_x, mid_y, mid_z = size_x // 2, size_y // 2, size_z // 2
    low_x, low_y = mid_x // 2, mid_y // 2
    count_x, count_y = lax.axis_size("gx"), lax.axis_size("gy")
    devices = count_x * count_y
    plane, strip = tiles_of(size_y, size_z), tiles_of(8, size_z)
    mids = 4 * mid_x

    def tiles(count):
        return (count,) + TILE

    place = jnp.stack([lax.axis_index("gx"), lax.axis_index("gy")]).astype(jnp.int32)
    pairs = size_x // 2
    up_x, down_x, up_y, down_y, mid, low, own = call(
        pack_kernel,
        (initial, source, absorption, beta_x, beta_y, beta_z),
        [
            tiles(sum(UP_PLANES) * plane),
            tiles(sum(DOWN_PLANES) * plane),
            tiles((6 * pairs + 1) * strip + 2 + 4 * STRIP),
            tiles((6 * pairs + 2) * strip + 2 + 4 * STRIP),
            tiles(mids),
            tiles(3),
            (6,) + source.shape,
        ],
        [(4 * mid_x * size_y, mid_z)],
        far_in=range(6),
        sems=6,
    )
    low_x1, high_x1 = shifted(up_x, "gx", 1), shifted(down_x, "gx", -1)
    low_y1, high_y1 = shifted(up_y, "gy", 1), shifted(down_y, "gy", -1)
    up_c, down_c = call(
        functools.partial(corner_kernel, size_x, size_z),
        (low_y1, high_y1, mid, low),
        [tiles(corner_tiles(UP_CORNER) * strip + 14), tiles(corner_tiles(DOWN_CORNER) * strip + 16)],
    )
    low_c1, high_c1 = shifted(up_c, "gx", 1), shifted(down_c, "gx", -1)

    tall = (size_y + 2 * PAD, size_z)
    wide = (size_x + 2 * FINE,) + tall
    own_windows, own_coeffs, up_corner, down_corner = call(
        own_kernel,
        (own, low_y1, high_y1),
        [(6, size_x) + tall, (8, size_x - 1) + tall, tiles(MID_CORNER), tiles(MID_CORNER)],
    )
    iterate, mid_target, up_x, down_x, up_y, down_y = call(
        fine_kernel,
        (own_windows, own_coeffs, up_corner, down_corner, mid, low_x1, high_x1, low_c1, high_c1),
        [
            source.shape,
            (mid_x, mid_y, mid_z),
            tiles(4 * plane + mid_x + MID_CORNER + mids + 8 + PASSED),
            tiles(4 * plane + mid_x + MID_CORNER + mids + 10 + PASSED),
            tiles(pairs * strip + mid_x),
            tiles(pairs * strip + mid_x),
        ],
        [(6, 2 * FINE) + tall, (8, 2 * FINE + 1) + tall, wide, wide, (mid_x * size_y, mid_z)],
    )
    low_x2, high_x2 = shifted(up_x, "gx", 1), shifted(down_x, "gx", -1)
    low_y2, high_y2 = shifted(up_y, "gy", 1), shifted(down_y, "gy", -1)
    up_c, down_c = call(
        functools.partial(corner_two_kernel, size_x, size_z),
        (low_y2, high_y2),
        [tiles(2 * strip + 2 * mid_x)] * 2,
    )
    low_c2, high_c2 = shifted(up_c, "gx", 1), shifted(down_c, "gx", -1)

    mid_wide = (mid_x + 2 * MID, 3 * mid_y, mid_z)
    (mid_coeffs,) = call(
        mid_coeffs_kernel,
        (mid, low_y1, high_y1, low_x2, high_x2),
        [(8,) + mid_wide],
        [(4,) + mid_wide],
    )
    goal, slots = call(
        functools.partial(mid_kernel, count_x, count_y),
        (place, low, mid_target, mid_coeffs, low_x2, high_x2, low_y2, high_y2, low_c2, high_c2),
        [mid_wide, (devices, 3) + TILE],
        [mid_wide] * 3 + [(low_x * mid_y, mid_z)],
        scalars=1,
    )
    own_half = lax.all_to_all(slots, ("gx", "gy"), 0, 0)
    other_half = lax.ppermute(own_half, "gx", [(i, i ^ 1) for i in range(count_x)])

    window, coeffs, near = call(
        window_kernel,
        (own, low_x1, high_x1, low_y1, high_y1, low_c1, high_c1)
        + (iterate, low_x2, high_x2, low_y2, high_y2, low_c2, high_c2, low),
        [wide, (7, wide[0] - 4) + tall, tiles(30)],
        [(6, size_x) + tall, (6, 2 * FINE) + tall],
    )
    low_wide = (low_x * count_x, low_y * count_y, mid_z)
    low_planes = mid_wide[0] // 2
    (result,) = call(
        functools.partial(last_kernel, count_x, count_y),
        (place, own_half, other_half, mid_coeffs, goal, coeffs, window, near),
        [source.shape],
        [(devices, 3) + TILE, (3,) + low_wide, (7,) + low_wide, low_wide, low_wide]
        + [mid_wide, mid_wide, mid_wide, (low_planes * 32, mid_z)]
        + [wide, wide, (2, (mid_x + 4) * 2 * (mid_y + 8), mid_z)],
        scalars=1,
    )
    return result


def solution(mesh):
    spec = P("gx", "gy", None)
    return jax.shard_map(
        local, mesh=mesh, in_specs=(spec,) * 6, out_specs=spec, check_vma=False
    )
```

```python
import functools
import math

import jax
import jax.numpy as jnp
from jax import lax
from jax.experimental import pallas as pl
from jax.experimental.pallas import tpu as pltpu
from jax.sharding import PartitionSpec as P

SWEEPS = 4
COARSE_SWEEPS = 8
F32 = jnp.float32
TILE = (8, 128)
PAD = 8
FINE = 5
MID = 6


def chebyshev_weights(sweeps):
    cheb_theta = 1.125
    cheb_delta = 0.875
    cheb_sigma = cheb_theta / cheb_delta
    rho_old = 1.0 / cheb_sigma
    weights = [(0.0, 1.0 / cheb_theta)]
    for sweep in range(1, sweeps):
        rho_new = 1.0 / (2.0 * cheb_sigma - rho_old)
        weights.append((rho_new * rho_old, 2.0 * rho_new / cheb_delta))
        rho_old = rho_new
    return weights


def iota(shape, axis):
    return lax.broadcasted_iota(jnp.int32, shape, axis)


def roll(value, shift, axis):
    return pltpu.roll(value, shift % value.shape[axis], axis)


def take(tile, index, axis):
    return jnp.take_along_axis(tile, index, axis=axis, mode="promise_in_bounds")


def rows_spread(tile, half):
    return take(tile, iota(TILE, 0) // 2 + 4 * half, 0)


def lanes_spread(tile, half):
    return take(tile, iota(TILE, 1) // 2 + 64 * half, 1)


def rows_merge(one, two, pairs=True):
    row = iota(TILE, 0)
    if pairs:
        one, two = one + roll(one, -1, 0), two + roll(two, -1, 0)
    index = (2 * row) % TILE[0]
    return jnp.where(row < TILE[0] // 2, take(one, index, 0), take(two, index, 0))


def lanes_merge(one, two, pairs=True):
    lane = iota(TILE, 1)
    if pairs:
        one, two = one + roll(one, -1, 1), two + roll(two, -1, 1)
    index = (2 * lane) % TILE[1]
    return jnp.where(lane < TILE[1] // 2, take(one, index, 1), take(two, index, 1))


def merge(plane, row_pairs=True, lane_pairs=True):
    halves = []
    for side in range(2):
        lanes = slice(side * TILE[1], (side + 1) * TILE[1])
        halves.append(rows_merge(plane[: TILE[0], lanes], plane[TILE[0] :, lanes], row_pairs))
    return lanes_merge(*halves, lane_pairs)


def each(start, stop, body, carry=0):
    if stop - start > 20:
        return lax.fori_loop(start, stop, body, carry, unroll=2)
    for i in range(start, stop):
        carry = body(i, carry)
    return carry


def here():
    return lax.axis_index("gx"), lax.axis_index("gy")


class Writer:
    def __init__(self, ref):
        self.ref, self.at = ref, 0

    def put(self, value):
        rows, columns = value.shape
        for r in range(0, rows, TILE[0]):
            for c in range(0, columns, TILE[1]):
                self.ref[self.at] = value[r : r + TILE[0], c : c + TILE[1]]
                self.at += 1


class Tiles:
    def __init__(self):
        self.tiles = []

    def put(self, value):
        rows, columns = value.shape
        for r in range(0, rows, TILE[0]):
            for c in range(0, columns, TILE[1]):
                self.tiles.append(value[r : r + TILE[0], c : c + TILE[1]])


def send(first, second, even, up, down):
    for at, (one, two) in enumerate(zip(up.tiles, down.tiles, strict=True)):
        first[at] = jnp.where(even, one, two)
        second[at] = jnp.where(even, two, one)


class Got:
    def __init__(self, first, second, even, low):
        self.refs = (second, first) if low else (first, second)
        self.even, self.shape = even, first.shape

    def __getitem__(self, at):
        return jnp.where(self.even, self.refs[0][at], self.refs[1][at])


def got(first, second, even):
    return Got(first, second, even, True), Got(first, second, even, False)


class Reader:
    def __init__(self, ref, at=0):
        self.ref, self.at = ref, at

    def get(self, rows, columns):
        lines = []
        for _ in range(rows // TILE[0]):
            parts = []
            for _ in range(columns // TILE[1]):
                parts.append(self.ref[self.at])
                self.at += 1
            lines.append(parts[0] if len(parts) == 1 else jnp.concatenate(parts, axis=1))
        return lines[0] if len(lines) == 1 else jnp.concatenate(lines, axis=0)


UP_PLANES = (5, 4, 4, 4, 4, 4)
DOWN_PLANES = (5, 4, 4, 5, 4, 4)
UP_CORNER = (4, 3, 3, 3, 4, 3)
DOWN_CORNER = (4, 3, 3, 4, 4, 3)
STRIP = 3


def corner_tiles(counts):
    return sum(count - 1 for count in counts)


def tiles_of(rows, columns):
    return (rows // TILE[0]) * (columns // TILE[1])


def is_upper(width):
    return iota((TILE[0], width), 0) < TILE[0] // 2


def swapped(first, second, axis):
    count = lax.axis_size(axis)
    outer = [(i, (i + 1 if i % 2 else i - 1) % count) for i in range(count)]
    return lax.ppermute(first, axis, [(i, i ^ 1) for i in range(count)]), lax.ppermute(second, axis, outer)


def shifted(value, axis, step):
    count = lax.axis_size(axis)
    return lax.ppermute(value, axis, [(i, (i + step) % count) for i in range(count)])


def pack_kernel(
    ini_in, src_in, absorb_in, face_x_in, face_y_in, face_z_in,
    up_x, down_x, up_y, down_y, mid, low, own, sems,
):
    copies = []
    for field, ref in enumerate((ini_in, src_in, absorb_in, face_x_in, face_y_in, face_z_in)):
        copies.append(pltpu.make_async_copy(ref, own.at[field], sems.at[field]))
        copies[-1].start()
    for copy in copies:
        copy.wait()
    fields = tuple(own.at[field] for field in range(6))
    ini, src, absorb, face_x, face_y, face_z = fields
    size_x, size_y, size_z = ini.shape
    mid_x = size_x // 2
    for block in range(mid_x):
        one, two = 2 * block, 2 * block + 1
        mid[block] = merge(absorb[one] + absorb[two]) * 0.125
        mid[mid_x + block] = merge(face_x[one]) * 0.25
        mid[2 * mid_x + block] = merge(face_y[one] + face_y[two], row_pairs=False) * 0.25
        mid[3 * mid_x + block] = merge(face_z[one] + face_z[two], lane_pairs=False) * 0.25

    def coarser(array, planes, row_pairs=True, lane_pairs=True):
        parts = []
        for block in range(0, mid_x, 2):
            total = None
            for plane in range(planes):
                part = mid[array * mid_x + block + plane]
                total = part if total is None else total + part
            parts.append(total)
        tile = rows_merge(*parts, row_pairs)
        return lanes_merge(tile, tile, lane_pairs)

    left = iota(TILE, 1) < TILE[1] // 2
    low[0] = jnp.where(left, 0.0, coarser(0, 2) * 0.125)
    low[1] = jnp.where(left, coarser(1, 1), coarser(2, 2, row_pairs=False)) * 0.25
    low[2] = jnp.where(left, coarser(3, 2, lane_pairs=False) * 0.25, 0.0)

    tops, bottoms = Writer(up_x), Writer(down_x)
    for ref, count in zip(fields, UP_PLANES):
        for plane in range(size_x - count, size_x):
            tops.put(ref[plane])
    for ref, count in zip(fields, DOWN_PLANES):
        for plane in range(count):
            bottoms.put(ref[plane])

    upper = is_upper(size_z)
    tops_y, bottoms_y = Writer(up_y), Writer(down_y)
    for ref in fields:
        for pair in range(0, size_x, 2):
            one, two = ref[pair], ref[pair + 1]
            tops_y.put(jnp.where(upper, roll(one[size_y - 8 :], 4, 0), two[size_y - 8 :]))
            bottoms_y.put(jnp.where(upper, one[:8], roll(two[:8], 4, 0)))
    tops_y.put(ini[:, size_y - 5, :])
    bottoms_y.put(ini[:, 4, :])
    bottoms_y.put(face_y[:, 4, :])
    for writer in (tops_y, bottoms_y):
        for tile in (1, 2):
            writer.put(low[tile])
    row, upper = iota(TILE, 0), is_upper(TILE[1])
    for array in range(4):
        parts = [mid[array * mid_x + plane] for plane in range(mid_x)]
        for pair in range(0, mid_x, 2):
            one, two = parts[pair], parts[pair + 1]
            tops_y.put(jnp.where(upper, roll(one, 4, 0), two))
            bottoms_y.put(jnp.where(upper, one, roll(two, 4, 0)))
        far_low, far_high = roll(parts[0], -2, 0), roll(parts[0], -4, 0)
        for plane in range(1, mid_x):
            far_low = jnp.where(row < 2 * plane, far_low, roll(parts[plane], 2 * plane - 2, 0))
            far_high = jnp.where(row < 2 * plane, far_high, roll(parts[plane], 2 * plane - 4, 0))
        tops_y.put(far_low)
        bottoms_y.put(far_high)


def corner_of(low_y, high_y, plane, upper, first_tile=0):
    width = upper.shape[1]
    at = first_tile + (plane // 2) * tiles_of(8, width)
    low = Reader(low_y, at).get(8, width)
    high = Reader(high_y, at).get(8, width)
    if plane % 2 == 0:
        return jnp.where(upper, low, roll(high, 4, 0))
    return jnp.where(upper, roll(low, 4, 0), high)


def mix(near, far):
    row = iota(near.shape, 0)
    return jnp.where((row >= 2) & (row < 6), near, roll(far, 3, 0))


def put_corners(writer, low_y, high_y, planes, upper, first_tile):
    parts = [corner_of(low_y, high_y, plane, upper, first_tile) for plane in planes]
    for part in parts[:-2]:
        writer.put(part)
    writer.put(mix(*parts[-2:]))


def mid_strip(ref, array, plane, low):
    start = ref.shape[0] - 4 * STRIP + array * STRIP
    near, far, row = ref[start + plane // 2], ref[start + 2], iota(TILE, 0)
    if (plane % 2 == 0) == low:
        near = roll(near, 4, 0)
    far = roll(far, (2 if low else 4) - 2 * plane, 0)
    return jnp.where(row >= 4, near, far) if low else jnp.where(row < 4, near, far)


def corner_kernel(size_x, size_z, low_y, high_y, mid, low_faces, first, second):
    place = here()
    upper = is_upper(size_z)
    per_field = (size_x // 2) * tiles_of(8, size_z)
    tops, bottoms = Tiles(), Tiles()
    for field in range(6):
        start = field * per_field
        planes = [size_x - 1 - plane for plane in range(UP_CORNER[field])]
        put_corners(tops, low_y, high_y, planes, upper, start)
        put_corners(bottoms, low_y, high_y, range(DOWN_CORNER[field]), upper, start)
    mid_x = size_x // 2
    upper = is_upper(TILE[1])
    for _ in range(len(bottoms.tiles) - len(tops.tiles)):
        tops.put(low_faces[0])
    for writer, near, next_plane in ((tops, mid_x - 1, mid_x - 2), (bottoms, 0, 1)):
        wanted = [(array, near) for array in range(4)] + [(1, next_plane)]
        for array, plane in wanted:
            writer.put(
                jnp.where(upper, mid_strip(high_y, array, plane, False), mid_strip(low_y, array, plane, True))
            )
        for array, plane in wanted:
            writer.put(mid[array * mid_x + plane])
        for tiles in ((low_faces[1], low_faces[2]), low_tiles_of(low_y), low_tiles_of(high_y)):
            for tile in tiles:
                writer.put(tile)
    send(first, second, place[0] % 2 == 0, tops, bottoms)


def low_tiles_of(ref):
    end = ref.shape[0] - 4 * STRIP
    return ref[end - 2], ref[end - 1]


class Planes:
    def __init__(self, *parts):
        self.parts = parts
        self.shape = parts[0][2].shape

    def find(self, i):
        for start, stop, ref, offset, lead in self.parts:
            if start <= i < stop:
                return ref, lead + (i - start + offset,)
        raise IndexError(i)

    def __getitem__(self, i):
        ref, index = self.find(i)
        return ref[index]


class Stack:
    def __init__(self, *parts):
        self.parts = parts

    def of(self, kind):
        return Planes(*((a, b, ref, offset, (kind,)) for a, b, ref, offset in self.parts))

    def __getitem__(self, index):
        return self.of(index[0])[index[1]]

    def __setitem__(self, index, value):
        ref, place = self.of(index[0]).find(index[1])
        ref[place] = value


def scale_coeffs(scale, absorb, face_x, face_y, face_z, coeffs, planes, target=None, diagonal=None):
    rows, lanes = absorb.shape[-2:]
    lane = iota((rows, lanes), 1)

    def body(i, carry):
        xl, xh = face_x[i], face_x[i + 1]
        yl, zl = face_y[i], face_z[i]
        yh = roll(yl, -1, 0)
        zh = jnp.where(lane == lanes - 1, 0.0, roll(zl, -1, 1))
        diag = absorb[i] + scale * (xl + xh + yl + yh + zl + zh)
        inverse = 1.0 / diag
        scaled = scale * inverse
        coeffs[0, i] = scaled * xl
        coeffs[1, i] = scaled * xh
        coeffs[2, i] = scaled * yl
        coeffs[3, i] = scaled * yh
        coeffs[4, i] = jnp.where(lane == 0, 0.0, scaled * zl)
        coeffs[5, i] = scaled * zh
        if target is not None:
            coeffs[6, i] = target[i] * inverse
        else:
            coeffs[6, i] = inverse
        if diagonal is not None:
            coeffs[7, i] = diag
        return carry

    each(*planes, body)


def scaled_remain(coeffs, i, below, here, above, goal=None):
    along_z = coeffs[4, i] * roll(here, 1, 1) + coeffs[5, i] * roll(here, -1, 1)
    along_y = coeffs[2, i] * roll(here, 1, 0) + coeffs[3, i] * roll(here, -1, 0)
    along_x = coeffs[0, i] * below + coeffs[1, i] * above
    return ((coeffs[6, i] if goal is None else goal[i]) - here + along_x) + (along_y + along_z)


def sweep_window(iterate, update, coeffs, planes, pair, first, goal=None, source=None):
    start, stop = planes
    source = iterate if source is None else source

    def body(i, carry):
        below, here = carry
        above = source[i + 1]
        step = pair[1] * scaled_remain(coeffs, i, below, here, above, goal)
        if not first:
            step = step + pair[0] * update[i]
        update[i] = step
        iterate[i] = here + step
        return here, above

    each(start, stop, body, (source[start - 1], source[start]))


def assemble_own(window, own, low_y, high_y, low_start, high_start):
    size_x, size_y, size_z = own.shape
    high = PAD + size_y
    low_reader, high_reader = Reader(low_y, low_start), Reader(high_y, high_start)
    for pair in range(0, size_x, 2):
        window[pair, PAD:high] = own[pair]
        window[pair + 1, PAD:high] = own[pair + 1]
        tile = low_reader.get(8, size_z)
        window[pair, 0:8] = roll(tile, 4, 0)
        window[pair + 1, 0:8] = tile
        tile = high_reader.get(8, size_z)
        window[pair, high : high + 8] = tile
        window[pair + 1, high : high + 8] = roll(tile, 4, 0)


def assemble_side(window, first, count, rows, planes, plane_start, corners, corner_start, corner_count, from_end):
    size_y, size_z = rows
    high = PAD + size_y
    reader = Reader(planes, plane_start)
    for plane in range(count):
        window[first + plane, PAD:high] = reader.get(size_y, size_z)
    reader = Reader(corners, corner_start)
    tiles = [roll(reader.get(8, size_z), 4, 0) for _ in range(corner_count - 1)]
    tiles.append(roll(tiles[-1], -3, 0))
    for plane, tile in enumerate(tiles):
        at = first + count - 1 - plane if from_end else first + plane
        window[at, 0:8] = tile
        window[at, high : high + 8] = tile


def assemble_owns(windows, own, low_y, high_y):
    size_x, size_y, size_z = own.shape[1:]
    per_field = (size_x // 2) * tiles_of(8, size_z)
    for field in range(6):
        assemble_own(windows.at[field], own.at[field], low_y, high_y, field * per_field, field * per_field)
    low_line = Reader(low_y, 6 * per_field).get(8, size_z)
    high_reader = Reader(high_y, 6 * per_field)
    high_line = high_reader.get(8, size_z)
    face_line = high_reader.get(8, size_z)
    high = PAD + size_y
    for plane in range(size_x):
        windows[0, plane, 3:4] = low_line[plane : plane + 1]
        windows[0, plane, high + 4 : high + 5] = high_line[plane : plane + 1]
        windows[4, plane, high + 4 : high + 5] = face_line[plane : plane + 1]


def assemble_sides(side_windows, rows, low_x, high_x, low_c, high_c):
    plane_tiles, strip_tiles = tiles_of(*rows), tiles_of(8, rows[1])
    starts = [0] * 4
    for field in range(6):
        up, down, up_c, down_c = (
            kinds[field] for kinds in (UP_PLANES, DOWN_PLANES, UP_CORNER, DOWN_CORNER)
        )
        window = side_windows.at[field]
        assemble_side(
            window, FINE - up, up, rows, low_x, starts[0], low_c, starts[2], up_c, True
        )
        assemble_side(
            window, FINE, down, rows, high_x, starts[1], high_c, starts[3], down_c, False
        )
        starts[0] += up * plane_tiles
        starts[1] += down * plane_tiles
        starts[2] += (up_c - 1) * strip_tiles
        starts[3] += (down_c - 1) * strip_tiles


def own_kernel(own, low_y, high_y, windows, coeffs, up_corner, down_corner):
    assemble_owns(windows, own, low_y, high_y)
    fields = [windows.at[field] for field in range(6)]
    scale_coeffs(1.0, *fields[2:], coeffs, (0, own.shape[1] - 1), fields[1], True)
    mid_x = own.shape[1] // 2
    tops, bottoms = Writer(up_corner), Writer(down_corner)
    upper = is_upper(TILE[1])
    sides = ((low_y, True), (high_y, False))
    for writer, first, step in ((tops, mid_x - 1, -1), (bottoms, 0, 1)):
        for array in range(4):
            for q in range(2):
                for ref, low in sides:
                    writer.put(mid_strip(ref, array, first + q * step, low))
        for array in range(4):
            for q in range(2, 4):
                one, two = (roll(mid_strip(ref, array, first + q * step, low), 4, 0) for ref, low in sides)
                writer.put(jnp.where(upper, one, two))


def fine_kernel(
    own_windows, own_coeffs, up_corner, down_corner, mid, low_x, high_x, first_c, second_c,
    iterate_out, mid_target, first_x, second_x, first_y, second_y,
    side_windows, side_coeffs, iterate, update,
):
    size_x, size_z = own_windows.shape[1], own_windows.shape[3]
    size_y = own_windows.shape[2] - 2 * PAD
    place = here()
    even = place[0] % 2 == 0
    low_c, high_c = got(first_c, second_c, even)
    assemble_sides(side_windows, (size_y, size_z), low_x, high_x, low_c, high_c)
    end = FINE + size_x
    last = end + FINE - 1
    windows = Stack(
        (0, FINE, side_windows, 0), (FINE, end, own_windows, 0), (end, last + 1, side_windows, FINE)
    )
    coeffs = Stack(
        (0, FINE, side_coeffs, 0), (FINE, end - 1, own_coeffs, 0), (end - 1, last + 1, side_coeffs, FINE)
    )
    fields = [windows.of(field) for field in range(6)]
    scale_coeffs(1.0, *fields[2:], coeffs, (1, FINE), fields[1], True)
    scale_coeffs(1.0, *fields[2:], coeffs, (end - 1, last), fields[1], True)
    for sweep, pair in enumerate(chebyshev_weights(SWEEPS)):
        sweep_window(
            iterate, update, coeffs, (1 + sweep, last - sweep), pair, sweep == 0,
            source=fields[0] if sweep == 0 else None,
        )
    mid_x, mid_y = size_x // 2, size_y // 2
    coarse = []
    for block in range(mid_x):
        total = None
        for plane in (FINE + 2 * block, FINE + 2 * block + 1):
            remain = scaled_remain(coeffs, plane, iterate[plane - 1], iterate[plane], iterate[plane + 1])
            remain = (remain * coeffs[7, plane])[PAD : PAD + size_y]
            total = remain if total is None else total + remain
        coarse.append(merge(total) * 0.125)
        mid_target[block] = coarse[block]
    for plane in range(size_x):
        iterate_out[plane] = iterate[FINE + plane, PAD : PAD + size_y]

    tops, bottoms = Tiles(), Tiles()
    for plane in range(size_x - 4, size_x):
        tops.put(iterate_out[plane])
    for plane in range(4):
        bottoms.put(iterate_out[plane])
    upper = is_upper(size_z)
    tops_y, bottoms_y = Tiles(), Tiles()
    for pair in range(0, size_x, 2):
        one, two = iterate_out[pair], iterate_out[pair + 1]
        tops_y.put(jnp.where(upper, roll(one[size_y - 8 :], 4, 0), two[size_y - 8 :]))
        bottoms_y.put(jnp.where(upper, one[:8], roll(two[:8], 4, 0)))
    for writer in (tops, bottoms, tops_y, bottoms_y):
        for tile in coarse:
            writer.put(tile)
    for writer, ref in ((tops, up_corner), (bottoms, down_corner)):
        for tile in range(MID_CORNER):
            writer.put(ref[tile])
    for writer in (tops, bottoms):
        for tile in range(mid.shape[0]):
            writer.put(mid[tile])
    for writer, corners in ((tops, low_c), (bottoms, high_c)):
        for tile in range(corners.shape[0] - PASSED - 10, corners.shape[0]):
            writer.put(corners[tile])
    send(first_x, second_x, even, tops, bottoms)
    send(first_y, second_y, place[1] % 2 == 0, tops_y, bottoms_y)


MID_CORNER = 24
PASSED = 6


def whole_corner(ref, start, array, q, side):
    return ref[start + (array * 2 + q) * 2 + side]


def part_corner(ref, start, array, q):
    return ref[start + 16 + array * 2 + q - 2]


def corner_two_kernel(size_x, size_z, first_y, second_y, first, second):
    place = here()
    upper = is_upper(size_z)
    low_y, high_y = got(first_y, second_y, place[1] % 2 == 0)
    tops, bottoms = Tiles(), Tiles()
    put_corners(tops, low_y, high_y, [size_x - 1, size_x - 2, size_x - 3], upper, 0)
    put_corners(bottoms, low_y, high_y, range(3), upper, 0)
    for writer in (tops, bottoms):
        for ref in (low_y, high_y):
            for tile in range(ref.shape[0] - size_x // 2, ref.shape[0]):
                writer.put(ref[tile])
    send(first, second, place[0] % 2 == 0, tops, bottoms)


def mid_coeffs_kernel(mid, low_y, high_y, first_x2, second_x2, coeffs, window):
    place = here()
    low_x2, high_x2 = got(first_x2, second_x2, place[0] % 2 == 0)
    mid_y, mid_z = mid.shape[1:]
    mid_x = mid.shape[0] // 4
    mids = 4 * mid_x
    first = MID - mid_x
    corner = 4 * tiles_of(2 * mid_y, 2 * mid_z) + mid_x
    passed = corner + MID_CORNER
    for ref, start, block in ((low_x2, passed, 0), (mid, 0, 1), (high_x2, passed, 2)):
        for array in range(4):
            for plane in range(mid_x):
                window[array, first + block * mid_x + plane, mid_y : 2 * mid_y] = ref[start + array * mid_x + plane]
    for array in range(4):
        for plane in range(mid_x):
            window[array, MID + plane, :mid_y] = mid_strip(low_y, array, plane, True)
            window[array, MID + plane, 2 * mid_y :] = mid_strip(high_y, array, plane, False)
    passed += mids
    far = 3 * mid_x + first
    for ref, start, step, end in ((low_x2, MID - 1, -1, first - 1), (high_x2, MID + mid_x, 1, far)):
        for array in range(4):
            for q in range(mid_x):
                if q < 2:
                    one, two = (whole_corner(ref, corner, array, q, side) for side in range(2))
                else:
                    one = two = roll(part_corner(ref, corner, array, q), 4, 0)
                window[array, start + q * step, :mid_y] = one
                window[array, start + q * step, 2 * mid_y :] = two
        for at in range(5):
            array, plane = (at, end) if at < 4 else (1, end + step)
            window[array, plane, :mid_y] = ref[passed + at]
            window[array, plane, 2 * mid_y :] = ref[passed + at]
            window[array, plane, mid_y : 2 * mid_y] = ref[passed + 5 + at]
    scale_coeffs(0.25, *(window.at[array] for array in range(4)), coeffs, (first - 1, far + 1), None, True)


def mid_kernel(
    count_x, count_y, low, mid_target, coeffs, first_x2, second_x2, first_y2, second_y2, first_c2, second_c2,
    goal, slots, target, iterate, update,
):
    mid_x, mid_y, mid_z = mid_target.shape
    first = MID - mid_x
    far = 3 * mid_x + first
    fine_tiles = 4 * tiles_of(2 * mid_y, 2 * mid_z)
    place = here()
    even = place[0] % 2 == 0
    low_x2, high_x2 = got(first_x2, second_x2, even)
    low_y2, high_y2 = got(first_y2, second_y2, place[1] % 2 == 0)
    low_c2, high_c2 = got(first_c2, second_c2, even)
    blocks = {
        (0, 0): (low_c2, low_c2.shape[0] - 2 * mid_x), (0, 1): (low_x2, fine_tiles),
        (0, 2): (low_c2, low_c2.shape[0] - mid_x), (1, 0): (low_y2, low_y2.shape[0] - mid_x),
        (1, 2): (high_y2, high_y2.shape[0] - mid_x),
        (2, 0): (high_c2, high_c2.shape[0] - 2 * mid_x), (2, 1): (high_x2, fine_tiles),
        (2, 2): (high_c2, high_c2.shape[0] - mid_x),
    }
    for plane in range(mid_x):
        target[MID + plane, mid_y : 2 * mid_y] = mid_target[plane]
    for (bx, by), (ref, start) in blocks.items():
        for plane in range(mid_x):
            target[first + bx * mid_x + plane, by * mid_y : (by + 1) * mid_y] = ref[start + plane]

    weights = chebyshev_weights(SWEEPS)

    def start_sweep(i, carry):
        value = target[i] * coeffs[6, i]
        goal[i] = value
        update[i] = weights[0][1] * value
        iterate[i] = weights[0][1] * value
        return carry

    each(first, far, start_sweep)
    for sweep in range(1, SWEEPS):
        sweep_window(iterate, update, coeffs, (first + sweep, far - sweep), weights[sweep], False, goal)
    parts = []
    for block in range(0, mid_x, 2):
        total = None
        for plane in (MID + block, MID + block + 1):
            remain = scaled_remain(coeffs, plane, iterate[plane - 1], iterate[plane], iterate[plane + 1], goal)
            remain = (remain * coeffs[7, plane])[mid_y : 2 * mid_y]
            total = remain if total is None else total + remain
        parts.append(total)
    coarse = rows_merge(*parts)
    coarse = lanes_merge(coarse, coarse) * 0.125
    tiles = (jnp.where(iota(TILE, 1) < TILE[1] // 2, coarse, low[0]), low[1], low[2])
    x1 = [iterate[MID + plane, mid_y : 2 * mid_y] for plane in range(mid_x)]
    pairs = count_x // 2
    own = place[0] // 2
    above, below = lax.rem(own + 1, pairs), lax.rem(own + pairs - 1, pairs)

    def fill(i, carry):
        up, down = i == above, i == below
        edge = jnp.where(up, mid_target[mid_x - 1], mid_target[0])
        near_pair = up | down | (i == own)
        far_side = (up & even) | (down & jnp.logical_not(even))
        for j in range(count_y):
            me = place[1]
            beside = (j == me) | (j == lax.rem(me + 1, count_y)) | (j == lax.rem(me + count_y - 1, count_y))
            near, side = near_pair & beside, far_side & beside
            one, two = 2 * i * count_y + j, (2 * i + 1) * count_y + j
            slots[one, 0] = tiles[0]
            slots[one, 1] = jnp.where(near, edge, tiles[1])
            slots[one, 2] = jnp.where(near, jnp.where(side & even, x1[2], x1[0]), tiles[2])
            slots[two, 0] = jnp.where(near, jnp.where(side, tiles[1], x1[1]), tiles[0])
            slots[two, 1] = jnp.where(near, jnp.where(side, tiles[2], x1[2]), tiles[1])
            slots[two, 2] = jnp.where(
                near, jnp.where(side & jnp.logical_not(even), x1[1], x1[3]), tiles[2]
            )
        return carry

    each(0, pairs, fill)


def solve_low(count_x, count_y, gathered, fields, coeffs, iterate, update):
    size_x, size_y, lanes = iterate.shape
    low_x, low_y = size_x // count_x, size_y // count_y
    low_z = lanes // 2

    def place(i, carry):
        for j in range(count_y):
            for kind in range(3):
                tile = gathered[i * count_y + j, kind]
                for plane in range(low_x):
                    fields[kind, i * low_x + plane, j * low_y : (j + 1) * low_y] = tile[
                        plane * low_y : (plane + 1) * low_y
                    ]
        return carry

    each(0, count_x, place)
    lane = iota((size_y, lanes), 1)
    inside = lane < low_z
    scale = 0.0625
    weights = chebyshev_weights(COARSE_SWEEPS)

    def following(i):
        if isinstance(i, int):
            return (i + 1) % size_x
        return jnp.where(i == size_x - 1, 0, i + 1)

    def prepare(i, carry):
        first, second, third = fields[0, i], fields[1, i], fields[2, i]
        xl, xh = second, fields[1, following(i)]
        yl = roll(second, low_z, 1)
        yh = roll(yl, -1, 0)
        zl = third
        zh = jnp.where(lane == low_z - 1, 0.0, roll(third, -1, 1))
        diag = roll(first, low_z, 1) + scale * (xl + xh + yl + yh + zl + zh)
        inverse = jnp.where(inside, 1.0 / diag, 0.0)
        scaled = scale * inverse
        coeffs[0, i] = scaled * xl
        coeffs[1, i] = scaled * xh
        coeffs[2, i] = scaled * yl
        coeffs[3, i] = scaled * yh
        coeffs[4, i] = jnp.where(lane == 0, 0.0, scaled * zl)
        coeffs[5, i] = scaled * zh
        goal = first * inverse
        coeffs[6, i] = goal
        update[i] = weights[0][1] * goal
        iterate[i] = weights[0][1] * goal
        return carry

    each(0, size_x, prepare)
    for pair in weights[1:]:
        start = iterate[0]

        def body(i, carry, pair=pair, start=start):
            below, here = carry
            if isinstance(i, int):
                above = start if i == size_x - 1 else iterate[i + 1]
            else:
                above = jnp.where(i == size_x - 1, start, iterate[following(i)])
            step = pair[1] * scaled_remain(coeffs, i, below, here, above) + pair[0] * update[i]
            update[i] = step
            iterate[i] = here + step
            return here, above

        each(0, size_x, body, (iterate[size_x - 1], start))


def window_kernel(
    fields_own, low_x1, high_x1, low_y1, high_y1, first_c1, second_c1,
    own, first_x, second_x, first_y, second_y, first_c, second_c,
    low, window, coeffs, near, own_windows, side_windows,
):
    place = here()
    even = place[0] % 2 == 0
    low_c1, high_c1 = got(first_c1, second_c1, even)
    low_x, high_x = got(first_x, second_x, even)
    low_y, high_y = got(first_y, second_y, place[1] % 2 == 0)
    low_c, high_c = got(first_c, second_c, even)
    known = {(0, 0): (low[1], low[2]), (0, -1): low_tiles_of(low_y1), (0, 1): low_tiles_of(high_y1)}
    for step, ref, distance in ((-1, low_c1, 1), (1, high_c1, 1), (-1, low_x, 2), (1, high_x, 2)):
        start = ref.shape[0] - PASSED
        for at, dy in enumerate((0, -1, 1)):
            known[step * distance, dy] = (ref[start + 2 * at], ref[start + 2 * at + 1])
    for (dx, dy), tiles in known.items():
        for kind in range(2):
            near[((dx + 2) * 3 + dy + 1) * 2 + kind] = tiles[kind]
    size_x, size_y, size_z = own.shape
    assemble_owns(own_windows, fields_own, low_y1, high_y1)
    assemble_sides(side_windows, (size_y, size_z), low_x1, high_x1, low_c1, high_c1)
    end = FINE + size_x
    windows = Stack(
        (0, FINE, side_windows, 0), (FINE, end, own_windows, 0), (end, end + FINE, side_windows, FINE)
    )
    fields = [windows.of(field) for field in range(6)]
    scale_coeffs(1.0, *fields[2:], Stack((2, end + 3, coeffs, 0)), (2, end + 3), fields[1])
    assemble_own(window.at[FINE : FINE + size_x], own, low_y, high_y, 0, 0)
    assemble_side(window, FINE - 4, 4, (size_y, size_z), low_x, 0, low_c, 0, 3, True)
    assemble_side(window, FINE + size_x, 4, (size_y, size_z), high_x, 0, high_c, 0, 3, False)


def last_kernel(
    count_x, count_y, own_half, other_half, mid_coeffs, goal_in, fine_coeffs, window, near,
    out,
    gathered, low_fields, low_coeffs, low_iterate, low_update,
    goal, mid_iterate, mid_update,
    iterate, update,
):
    size_x, size_y, size_z = out.shape
    mid_x, mid_y, mid_z = size_x // 2, size_y // 2, size_z // 2
    last = size_x + 2 * FINE - 2
    coeffs = Stack((2, last, fine_coeffs, 0))
    me_x, me_y = here()
    even = me_x % 2 == 0

    def half(which, device, tile):
        one, two = own_half[device, tile], other_half[device, tile]
        return jnp.where(even, one, two) if which == 0 else jnp.where(even, two, one)

    def device(dx, dy):
        return lax.rem(me_x + dx + count_x, count_x) * count_y + lax.rem(me_y + dy + count_y, count_y)

    def take(i, carry):
        for kind in range(3):
            gathered[i, kind] = half(0, i, kind)
        return carry

    each(0, count_x * count_y, take)
    side = me_x % 2
    for dy in (-1, 0, 1):
        for source in (device(-2 - side, dy), device(3 - side, dy)):
            for kind in range(2):
                gathered[source, 1 + kind] = half(1, source, kind)
    for dy in (-1, 0, 1):
        for dx in range(-2, 3):
            for kind in range(2):
                gathered[device(dx, dy), 1 + kind] = near[((dx + 2) * 3 + dy + 1) * 2 + kind]
    solve_low(count_x, count_y, gathered, low_fields, low_coeffs, low_iterate, low_update)

    first, far = MID - mid_x, MID + 2 * mid_x
    for dy in (-1, 0, 1):
        rows = slice((dy + 1) * mid_y, (dy + 2) * mid_y)
        for dx in (-1, 0, 1):
            source = device(dx, dy)
            start = MID + dx * mid_x
            mid_iterate[start, rows] = half(0, source, 2)
            for plane in range(1, mid_x):
                mid_iterate[start + plane, rows] = half(1, source, plane - 1)
        source = device(-2, dy)
        mid_iterate[0, rows] = jnp.where(even, half(0, source, 2), half(1, source, 1))
        mid_iterate[1, rows] = half(1, source, 2)
        source = device(2, dy)
        mid_iterate[far, rows] = half(0, source, 2)
        mid_iterate[far + 1, rows] = jnp.where(even, half(1, source, 0), half(1, source, 2))
    low_size_x, low_size_y = low_iterate.shape[:2]
    low_y = mid_y // 2
    turn = lax.rem(low_size_y - me_y * low_y + low_y, low_size_y)
    for plane in range((mid_x + 2 * MID) // 2):
        at = lax.rem(me_x * (mid_x // 2) - MID // 2 + plane + low_size_x, low_size_x)
        turned = pltpu.roll(low_iterate[at], turn, 0)
        one, two = lanes_spread(turned[: TILE[0]], 0), lanes_spread(turned[TILE[0] : 2 * TILE[0]], 0)
        part = jnp.concatenate([rows_spread(one, 0), rows_spread(one, 1), rows_spread(two, 0)], axis=0)
        mid_iterate[2 * plane] += part
        mid_iterate[2 * plane + 1] += part

    for plane in range(first, far):
        goal[plane] = goal_in[plane]
    for dy in (-1, 0, 1):
        rows = slice((dy + 1) * mid_y, (dy + 2) * mid_y)
        for plane, dx in ((first - 1, -2), (far, 2)):
            goal[plane, rows] = half(0, device(dx, dy), 1) * mid_coeffs[6, plane, rows]
    for sweep, pair in enumerate(chebyshev_weights(SWEEPS)):
        sweep_window(
            mid_iterate, mid_update, mid_coeffs, (first - 1 + sweep, far + 1 - sweep), pair, sweep == 0, goal
        )

    fine_low = FINE - 4
    for plane in range(mid_x + 4):
        turned = roll(mid_iterate[MID - 2 + plane], -4, 0)
        lines = []
        for r in range(2):
            tile = turned[r * TILE[0] : (r + 1) * TILE[0]]
            for side in range(2):
                line = rows_spread(tile, side)
                lines.append(jnp.concatenate([lanes_spread(line, 0), lanes_spread(line, 1)], axis=1))
        part = jnp.concatenate(lines, axis=0)
        for at in (fine_low + 2 * plane, fine_low + 2 * plane + 1):
            iterate[at] = window[at] + part
    for sweep, pair in enumerate(chebyshev_weights(SWEEPS)):
        sweep_window(
            iterate, update, coeffs, (2 + sweep, last - sweep), pair, sweep == 0
        )
    for plane in range(size_x):
        out[plane] = iterate[FINE + plane, PAD : PAD + size_y]


def call(kernel, inputs, outs, scratch=(), scalars=0, far_in=(), far_out=(), sems=0):
    def place(i):
        return pltpu.SMEM if i < scalars else pltpu.HBM if i in far_in else pltpu.VMEM

    near = [x.shape for i, x in enumerate(inputs) if i >= scalars and i not in far_in]
    near += [shape for i, shape in enumerate(outs) if i not in far_out] + list(scratch)
    used = 4 * sum(math.prod(shape) for shape in near)
    inputs = [pltpu.with_memory_space_constraint(x, pltpu.HBM) if i in far_in else x for i, x in enumerate(inputs)]
    return pl.pallas_call(
        kernel,
        out_shape=[
            pltpu.HBM(shape, F32) if i in far_out else jax.ShapeDtypeStruct(shape, F32)
            for i, shape in enumerate(outs)
        ],
        in_specs=[pl.BlockSpec(memory_space=place(i)) for i in range(len(inputs))],
        out_specs=[
            pl.BlockSpec(memory_space=pltpu.HBM if i in far_out else pltpu.VMEM) for i in range(len(outs))
        ],
        scratch_shapes=[pltpu.VMEM(shape, F32) for shape in scratch]
        + ([pltpu.SemaphoreType.DMA((sems,))] if sems > 1 else [pltpu.SemaphoreType.DMA] * sems),
        cost_estimate=pl.CostEstimate(flops=1000, bytes_accessed=1000, transcendentals=0),
        compiler_params=pltpu.CompilerParams(vmem_limit_bytes=used + used // 4 + 2 * 1024 * 1024),
    )(*inputs)


def local(source, initial, absorption, beta_x, beta_y, beta_z):
    size_x, size_y, size_z = source.shape
    mid_x, mid_y, mid_z = size_x // 2, size_y // 2, size_z // 2
    low_x, low_y = mid_x // 2, mid_y // 2
    count_x, count_y = lax.axis_size("gx"), lax.axis_size("gy")
    devices = count_x * count_y
    plane, strip = tiles_of(size_y, size_z), tiles_of(8, size_z)
    mids = 4 * mid_x

    def tiles(count):
        return (count,) + TILE

    pairs = size_x // 2
    up_x, down_x, up_y, down_y, mid, low, own = call(
        pack_kernel,
        (initial, source, absorption, beta_x, beta_y, beta_z),
        [
            tiles(sum(UP_PLANES) * plane),
            tiles(sum(DOWN_PLANES) * plane),
            tiles((6 * pairs + 1) * strip + 2 + 4 * STRIP),
            tiles((6 * pairs + 2) * strip + 2 + 4 * STRIP),
            tiles(mids),
            tiles(3),
            (6,) + source.shape,
        ],
        far_in=range(6),
        sems=6,
    )
    low_x1, high_x1 = shifted(up_x, "gx", 1), shifted(down_x, "gx", -1)
    low_y1, high_y1 = shifted(up_y, "gy", 1), shifted(down_y, "gy", -1)
    first_c1, second_c1 = call(
        functools.partial(corner_kernel, size_x, size_z),
        (low_y1, high_y1, mid, low),
        [tiles(corner_tiles(DOWN_CORNER) * strip + 16)] * 2,
    )
    first_c1, second_c1 = swapped(first_c1, second_c1, "gx")

    tall = (size_y + 2 * PAD, size_z)
    wide = (size_x + 2 * FINE,) + tall
    own_windows, own_coeffs, up_corner, down_corner = call(
        own_kernel,
        (own, low_y1, high_y1),
        [(6, size_x) + tall, (8, size_x - 1) + tall, tiles(MID_CORNER), tiles(MID_CORNER)],
    )
    iterate, mid_target, first_x2, second_x2, first_y2, second_y2 = call(
        fine_kernel,
        (own_windows, own_coeffs, up_corner, down_corner, mid, low_x1, high_x1, first_c1, second_c1),
        [
            source.shape,
            (mid_x, mid_y, mid_z),
            tiles(4 * plane + mid_x + MID_CORNER + mids + 10 + PASSED),
            tiles(4 * plane + mid_x + MID_CORNER + mids + 10 + PASSED),
            tiles(pairs * strip + mid_x),
            tiles(pairs * strip + mid_x),
        ],
        scratch=[(6, 2 * FINE) + tall, (8, 2 * FINE + 1) + tall, wide, wide],
    )
    first_x2, second_x2 = swapped(first_x2, second_x2, "gx")
    first_y2, second_y2 = swapped(first_y2, second_y2, "gy")
    first_c2, second_c2 = call(
        functools.partial(corner_two_kernel, size_x, size_z),
        (first_y2, second_y2),
        [tiles(2 * strip + 2 * mid_x)] * 2,
    )
    first_c2, second_c2 = swapped(first_c2, second_c2, "gx")

    mid_wide = (mid_x + 2 * MID, 3 * mid_y, mid_z)
    (mid_coeffs,) = call(
        mid_coeffs_kernel,
        (mid, low_y1, high_y1, first_x2, second_x2),
        [(8,) + mid_wide],
        [(4,) + mid_wide],
    )
    goal, slots = call(
        functools.partial(mid_kernel, count_x, count_y),
        (low, mid_target, mid_coeffs, first_x2, second_x2, first_y2, second_y2, first_c2, second_c2),
        [mid_wide, (devices, 3) + TILE],
        [mid_wide] * 3,
    )
    own_half = lax.all_to_all(slots, ("gx", "gy"), 0, 0)
    other_half = lax.ppermute(own_half, "gx", [(i, i ^ 1) for i in range(count_x)])

    window, coeffs, near = call(
        window_kernel,
        (own, low_x1, high_x1, low_y1, high_y1, first_c1, second_c1)
        + (iterate, first_x2, second_x2, first_y2, second_y2, first_c2, second_c2, low),
        [wide, (7, wide[0] - 4) + tall, tiles(30)],
        [(6, size_x) + tall, (6, 2 * FINE) + tall],
    )
    low_wide = (low_x * count_x, low_y * count_y, mid_z)
    (result,) = call(
        functools.partial(last_kernel, count_x, count_y),
        (own_half, other_half, mid_coeffs, goal, coeffs, window, near),
        [source.shape],
        [(devices, 3) + TILE, (3,) + low_wide, (7,) + low_wide, low_wide, low_wide]
        + [mid_wide, mid_wide, mid_wide]
        + [wide, wide],
    )
    return result


def solution(mesh):
    spec = P("gx", "gy", None)
    return jax.shard_map(
        local, mesh=mesh, in_specs=(spec,) * 6, out_specs=spec, check_vma=False
    )
```

```python
import functools
import math

import jax
import jax.numpy as jnp
from jax import lax
from jax.experimental import pallas as pl
from jax.experimental.pallas import tpu as pltpu
from jax.sharding import PartitionSpec as P

SWEEPS = 4
COARSE_SWEEPS = 8
F32 = jnp.float32
TILE = (8, 128)
PAD = 8
FINE = 5
MID = 6


def chebyshev_weights(sweeps):
    cheb_theta = 1.125
    cheb_delta = 0.875
    cheb_sigma = cheb_theta / cheb_delta
    rho_old = 1.0 / cheb_sigma
    weights = [(0.0, 1.0 / cheb_theta)]
    for sweep in range(1, sweeps):
        rho_new = 1.0 / (2.0 * cheb_sigma - rho_old)
        weights.append((rho_new * rho_old, 2.0 * rho_new / cheb_delta))
        rho_old = rho_new
    return weights


def iota(shape, axis):
    return lax.broadcasted_iota(jnp.int32, shape, axis)


def roll(value, shift, axis):
    return pltpu.roll(value, shift % value.shape[axis], axis)


def take(tile, index, axis):
    return jnp.take_along_axis(tile, index, axis=axis, mode="promise_in_bounds")


def rows_spread(tile, half):
    return take(tile, iota(TILE, 0) // 2 + 4 * half, 0)


def lanes_spread(tile, half):
    return take(tile, iota(TILE, 1) // 2 + 64 * half, 1)


def rows_merge(one, two, pairs=True):
    row = iota(TILE, 0)
    if pairs:
        one, two = one + roll(one, -1, 0), two + roll(two, -1, 0)
    index = (2 * row) % TILE[0]
    return jnp.where(row < TILE[0] // 2, take(one, index, 0), take(two, index, 0))


def lanes_merge(one, two, pairs=True):
    lane = iota(TILE, 1)
    if pairs:
        one, two = one + roll(one, -1, 1), two + roll(two, -1, 1)
    index = (2 * lane) % TILE[1]
    return jnp.where(lane < TILE[1] // 2, take(one, index, 1), take(two, index, 1))


def merge(plane, row_pairs=True, lane_pairs=True):
    halves = []
    for side in range(2):
        lanes = slice(side * TILE[1], (side + 1) * TILE[1])
        halves.append(rows_merge(plane[: TILE[0], lanes], plane[TILE[0] :, lanes], row_pairs))
    return lanes_merge(*halves, lane_pairs)


def each(start, stop, body, carry=0):
    if stop - start > 20:
        return lax.fori_loop(start, stop, body, carry, unroll=2)
    for i in range(start, stop):
        carry = body(i, carry)
    return carry


def here():
    return lax.axis_index("gx"), lax.axis_index("gy")


class Writer:
    def __init__(self, ref):
        self.ref, self.at = ref, 0

    def put(self, value):
        rows, columns = value.shape
        for r in range(0, rows, TILE[0]):
            for c in range(0, columns, TILE[1]):
                self.ref[self.at] = value[r : r + TILE[0], c : c + TILE[1]]
                self.at += 1


class Tiles:
    def __init__(self):
        self.tiles = []

    def put(self, value):
        rows, columns = value.shape
        for r in range(0, rows, TILE[0]):
            for c in range(0, columns, TILE[1]):
                self.tiles.append(value[r : r + TILE[0], c : c + TILE[1]])


def send(first, second, even, up, down):
    for at, (one, two) in enumerate(zip(up.tiles, down.tiles, strict=True)):
        first[at] = jnp.where(even, one, two)
        second[at] = jnp.where(even, two, one)


class Got:
    def __init__(self, first, second, even, low):
        self.refs = (second, first) if low else (first, second)
        self.even, self.shape = even, first.shape

    def __getitem__(self, at):
        return jnp.where(self.even, self.refs[0][at], self.refs[1][at])


def got(first, second, even):
    return Got(first, second, even, True), Got(first, second, even, False)


class Reader:
    def __init__(self, ref, at=0):
        self.ref, self.at = ref, at

    def get(self, rows, columns):
        lines = []
        for _ in range(rows // TILE[0]):
            parts = []
            for _ in range(columns // TILE[1]):
                parts.append(self.ref[self.at])
                self.at += 1
            lines.append(parts[0] if len(parts) == 1 else jnp.concatenate(parts, axis=1))
        return lines[0] if len(lines) == 1 else jnp.concatenate(lines, axis=0)


UP_PLANES = (5, 4, 4, 4, 4, 4)
DOWN_PLANES = (5, 4, 4, 5, 4, 4)
UP_CORNER = (4, 3, 3, 3, 4, 3)
DOWN_CORNER = (4, 3, 3, 4, 4, 3)
STRIP = 3


def corner_tiles(counts):
    return sum(count - 1 for count in counts)


def tiles_of(rows, columns):
    return (rows // TILE[0]) * (columns // TILE[1])


def is_upper(width):
    return iota((TILE[0], width), 0) < TILE[0] // 2


def swapped(first, second, axis):
    count = lax.axis_size(axis)
    outer = [(i, (i + 1 if i % 2 else i - 1) % count) for i in range(count)]
    inner = [(i, i ^ 1) for i in range(count)]
    if axis == "gy":
        inner, outer = outer, inner
    return lax.ppermute(first, axis, inner), lax.ppermute(second, axis, outer)


def shifted(value, axis, step):
    count = lax.axis_size(axis)
    return lax.ppermute(value, axis, [(i, (i + step) % count) for i in range(count)])


def pack_kernel(
    ini_in, src_in, absorb_in, face_x_in, face_y_in, face_z_in,
    up_x, down_x, up_y, down_y, mid, low, own, sems,
):
    copies = []
    for field, ref in enumerate((ini_in, src_in, absorb_in, face_x_in, face_y_in, face_z_in)):
        copies.append(pltpu.make_async_copy(ref, own.at[field], sems.at[field]))
        copies[-1].start()
    for copy in copies:
        copy.wait()
    fields = tuple(own.at[field] for field in range(6))
    ini, src, absorb, face_x, face_y, face_z = fields
    size_x, size_y, size_z = ini.shape
    mid_x = size_x // 2
    for block in range(mid_x):
        one, two = 2 * block, 2 * block + 1
        mid[block] = merge(absorb[one] + absorb[two]) * 0.125
        mid[mid_x + block] = merge(face_x[one]) * 0.25
        mid[2 * mid_x + block] = merge(face_y[one] + face_y[two], row_pairs=False) * 0.25
        mid[3 * mid_x + block] = merge(face_z[one] + face_z[two], lane_pairs=False) * 0.25

    def coarser(array, planes, row_pairs=True, lane_pairs=True):
        parts = []
        for block in range(0, mid_x, 2):
            total = None
            for plane in range(planes):
                part = mid[array * mid_x + block + plane]
                total = part if total is None else total + part
            parts.append(total)
        tile = rows_merge(*parts, row_pairs)
        return lanes_merge(tile, tile, lane_pairs)

    left = iota(TILE, 1) < TILE[1] // 2
    low[0] = jnp.where(left, coarser(2, 2, row_pairs=False), coarser(3, 2, lane_pairs=False)) * 0.25
    low[1] = jnp.where(left, coarser(0, 2) * 0.125, coarser(1, 1) * 0.25)

    tops, bottoms = Writer(up_x), Writer(down_x)
    for ref, count in zip(fields, UP_PLANES):
        for plane in range(size_x - count, size_x):
            tops.put(ref[plane])
    for ref, count in zip(fields, DOWN_PLANES):
        for plane in range(count):
            bottoms.put(ref[plane])

    upper = is_upper(size_z)
    tops_y, bottoms_y = Writer(up_y), Writer(down_y)
    for ref in fields:
        for pair in range(0, size_x, 2):
            one, two = ref[pair], ref[pair + 1]
            tops_y.put(jnp.where(upper, roll(one[size_y - 8 :], 4, 0), two[size_y - 8 :]))
            bottoms_y.put(jnp.where(upper, one[:8], roll(two[:8], 4, 0)))
    tops_y.put(ini[:, size_y - 5, :])
    bottoms_y.put(ini[:, 4, :])
    bottoms_y.put(face_y[:, 4, :])
    for writer in (tops_y, bottoms_y):
        for tile in range(2):
            writer.put(low[tile])
    row, upper = iota(TILE, 0), is_upper(TILE[1])
    for array in range(4):
        parts = [mid[array * mid_x + plane] for plane in range(mid_x)]
        for pair in range(0, mid_x, 2):
            one, two = parts[pair], parts[pair + 1]
            tops_y.put(jnp.where(upper, roll(one, 4, 0), two))
            bottoms_y.put(jnp.where(upper, one, roll(two, 4, 0)))
        far_low, far_high = roll(parts[0], -2, 0), roll(parts[0], -4, 0)
        for plane in range(1, mid_x):
            far_low = jnp.where(row < 2 * plane, far_low, roll(parts[plane], 2 * plane - 2, 0))
            far_high = jnp.where(row < 2 * plane, far_high, roll(parts[plane], 2 * plane - 4, 0))
        tops_y.put(far_low)
        bottoms_y.put(far_high)


def corner_of(low_y, high_y, plane, upper, first_tile=0):
    width = upper.shape[1]
    at = first_tile + (plane // 2) * tiles_of(8, width)
    low = Reader(low_y, at).get(8, width)
    high = Reader(high_y, at).get(8, width)
    if plane % 2 == 0:
        return jnp.where(upper, low, roll(high, 4, 0))
    return jnp.where(upper, roll(low, 4, 0), high)


def mix(near, far):
    row = iota(near.shape, 0)
    return jnp.where((row >= 2) & (row < 6), near, roll(far, 3, 0))


def put_corners(writer, low_y, high_y, planes, upper, first_tile):
    parts = [corner_of(low_y, high_y, plane, upper, first_tile) for plane in planes]
    for part in parts[:-2]:
        writer.put(part)
    writer.put(mix(*parts[-2:]))


def mid_strip(ref, array, plane, low):
    start = ref.shape[0] - 4 * STRIP + array * STRIP
    near, far, row = ref[start + plane // 2], ref[start + 2], iota(TILE, 0)
    if (plane % 2 == 0) == low:
        near = roll(near, 4, 0)
    far = roll(far, (2 if low else 4) - 2 * plane, 0)
    return jnp.where(row >= 4, near, far) if low else jnp.where(row < 4, near, far)


def corner_kernel(size_x, size_z, low_y, high_y, mid, low_faces, first, second):
    place = here()
    upper = is_upper(size_z)
    per_field = (size_x // 2) * tiles_of(8, size_z)
    tops, bottoms = Tiles(), Tiles()
    for field in range(6):
        start = field * per_field
        planes = [size_x - 1 - plane for plane in range(UP_CORNER[field])]
        put_corners(tops, low_y, high_y, planes, upper, start)
        put_corners(bottoms, low_y, high_y, range(DOWN_CORNER[field]), upper, start)
    mid_x = size_x // 2
    upper = is_upper(TILE[1])
    for _ in range(len(bottoms.tiles) - len(tops.tiles)):
        tops.put(low_faces[0])
    for writer, near, next_plane in ((tops, mid_x - 1, mid_x - 2), (bottoms, 0, 1)):
        wanted = [(array, near) for array in range(4)] + [(1, next_plane)]
        for array, plane in wanted:
            writer.put(
                jnp.where(upper, mid_strip(high_y, array, plane, False), mid_strip(low_y, array, plane, True))
            )
        for array, plane in wanted:
            writer.put(mid[array * mid_x + plane])
        for tiles in ((low_faces[0], low_faces[1]), low_tiles_of(low_y), low_tiles_of(high_y)):
            for tile in tiles:
                writer.put(tile)
    send(first, second, place[0] % 2 == 0, tops, bottoms)


def low_tiles_of(ref):
    end = ref.shape[0] - 4 * STRIP
    return ref[end - 2], ref[end - 1]


class Planes:
    def __init__(self, *parts):
        self.parts = parts
        self.shape = parts[0][2].shape

    def find(self, i):
        for start, stop, ref, offset, lead in self.parts:
            if start <= i < stop:
                return ref, lead + (i - start + offset,)
        raise IndexError(i)

    def __getitem__(self, i):
        ref, index = self.find(i)
        return ref[index]


class Stack:
    def __init__(self, *parts):
        self.parts = parts

    def of(self, kind):
        return Planes(*((a, b, ref, offset, (kind,)) for a, b, ref, offset in self.parts))

    def __getitem__(self, index):
        return self.of(index[0])[index[1]]

    def __setitem__(self, index, value):
        ref, place = self.of(index[0]).find(index[1])
        ref[place] = value


def scale_coeffs(scale, absorb, face_x, face_y, face_z, coeffs, planes, target=None, diagonal=None):
    rows, lanes = absorb.shape[-2:]
    lane = iota((rows, lanes), 1)

    def body(i, carry):
        xl, xh = face_x[i], face_x[i + 1]
        yl, zl = face_y[i], face_z[i]
        yh = roll(yl, -1, 0)
        zh = jnp.where(lane == lanes - 1, 0.0, roll(zl, -1, 1))
        diag = absorb[i] + scale * (xl + xh + yl + yh + zl + zh)
        inverse = 1.0 / diag
        scaled = scale * inverse
        coeffs[0, i] = scaled * xl
        coeffs[1, i] = scaled * xh
        coeffs[2, i] = scaled * yl
        coeffs[3, i] = scaled * yh
        coeffs[4, i] = jnp.where(lane == 0, 0.0, scaled * zl)
        coeffs[5, i] = scaled * zh
        if target is not None:
            coeffs[6, i] = target[i] * inverse
        else:
            coeffs[6, i] = inverse
        if diagonal is not None:
            coeffs[7, i] = diag
        return carry

    each(*planes, body)


def scaled_remain(coeffs, i, below, here, above, goal=None):
    along_z = coeffs[4, i] * roll(here, 1, 1) + coeffs[5, i] * roll(here, -1, 1)
    along_y = coeffs[2, i] * roll(here, 1, 0) + coeffs[3, i] * roll(here, -1, 0)
    along_x = coeffs[0, i] * below + coeffs[1, i] * above
    return ((coeffs[6, i] if goal is None else goal[i]) - here + along_x) + (along_y + along_z)


def sweep_window(iterate, update, coeffs, planes, pair, first, goal=None, source=None):
    start, stop = planes
    source = iterate if source is None else source

    def body(i, carry):
        below, here = carry
        above = source[i + 1]
        step = pair[1] * scaled_remain(coeffs, i, below, here, above, goal)
        if not first:
            step = step + pair[0] * update[i]
        update[i] = step
        iterate[i] = here + step
        return here, above

    each(start, stop, body, (source[start - 1], source[start]))


def assemble_own(window, own, low_y, high_y, low_start, high_start):
    size_x, size_y, size_z = own.shape
    high = PAD + size_y
    low_reader, high_reader = Reader(low_y, low_start), Reader(high_y, high_start)
    for pair in range(0, size_x, 2):
        window[pair, PAD:high] = own[pair]
        window[pair + 1, PAD:high] = own[pair + 1]
        tile = low_reader.get(8, size_z)
        window[pair, 0:8] = roll(tile, 4, 0)
        window[pair + 1, 0:8] = tile
        tile = high_reader.get(8, size_z)
        window[pair, high : high + 8] = tile
        window[pair + 1, high : high + 8] = roll(tile, 4, 0)


def assemble_side(window, first, count, rows, planes, plane_start, corners, corner_start, corner_count, from_end):
    size_y, size_z = rows
    high = PAD + size_y
    reader = Reader(planes, plane_start)
    for plane in range(count):
        window[first + plane, PAD:high] = reader.get(size_y, size_z)
    reader = Reader(corners, corner_start)
    tiles = [roll(reader.get(8, size_z), 4, 0) for _ in range(corner_count - 1)]
    tiles.append(roll(tiles[-1], -3, 0))
    for plane, tile in enumerate(tiles):
        at = first + count - 1 - plane if from_end else first + plane
        window[at, 0:8] = tile
        window[at, high : high + 8] = tile


def assemble_owns(windows, own, low_y, high_y):
    size_x, size_y, size_z = own.shape[1:]
    per_field = (size_x // 2) * tiles_of(8, size_z)
    for field in range(6):
        assemble_own(windows.at[field], own.at[field], low_y, high_y, field * per_field, field * per_field)
    low_line = Reader(low_y, 6 * per_field).get(8, size_z)
    high_reader = Reader(high_y, 6 * per_field)
    high_line = high_reader.get(8, size_z)
    face_line = high_reader.get(8, size_z)
    high = PAD + size_y
    for plane in range(size_x):
        windows[0, plane, 3:4] = low_line[plane : plane + 1]
        windows[0, plane, high + 4 : high + 5] = high_line[plane : plane + 1]
        windows[4, plane, high + 4 : high + 5] = face_line[plane : plane + 1]


def assemble_sides(side_windows, rows, low_x, high_x, low_c, high_c):
    plane_tiles, strip_tiles = tiles_of(*rows), tiles_of(8, rows[1])
    starts = [0] * 4
    for field in range(6):
        up, down, up_c, down_c = (
            kinds[field] for kinds in (UP_PLANES, DOWN_PLANES, UP_CORNER, DOWN_CORNER)
        )
        window = side_windows.at[field]
        assemble_side(
            window, FINE - up, up, rows, low_x, starts[0], low_c, starts[2], up_c, True
        )
        assemble_side(
            window, FINE, down, rows, high_x, starts[1], high_c, starts[3], down_c, False
        )
        starts[0] += up * plane_tiles
        starts[1] += down * plane_tiles
        starts[2] += (up_c - 1) * strip_tiles
        starts[3] += (down_c - 1) * strip_tiles


def own_kernel(own, low_y, high_y, windows, coeffs, up_corner, down_corner):
    assemble_owns(windows, own, low_y, high_y)
    fields = [windows.at[field] for field in range(6)]
    scale_coeffs(1.0, *fields[2:], coeffs, (0, own.shape[1] - 1), fields[1], True)
    mid_x = own.shape[1] // 2
    tops, bottoms = Writer(up_corner), Writer(down_corner)
    upper = is_upper(TILE[1])
    sides = ((low_y, True), (high_y, False))
    for writer, first, step in ((tops, mid_x - 1, -1), (bottoms, 0, 1)):
        for array in range(4):
            for q in range(2):
                for ref, low in sides:
                    writer.put(mid_strip(ref, array, first + q * step, low))
        for array in range(4):
            for q in range(2, 4):
                one, two = (roll(mid_strip(ref, array, first + q * step, low), 4, 0) for ref, low in sides)
                writer.put(jnp.where(upper, one, two))


def fine_kernel(
    own_windows, own_coeffs, up_corner, down_corner, mid, low_x, high_x, first_c, second_c,
    iterate_out, mid_target, first_x, second_x, first_y, second_y,
    side_windows, side_coeffs, iterate, update,
):
    size_x, size_z = own_windows.shape[1], own_windows.shape[3]
    size_y = own_windows.shape[2] - 2 * PAD
    place = here()
    even = place[0] % 2 == 0
    low_c, high_c = got(first_c, second_c, even)
    assemble_sides(side_windows, (size_y, size_z), low_x, high_x, low_c, high_c)
    end = FINE + size_x
    last = end + FINE - 1
    windows = Stack(
        (0, FINE, side_windows, 0), (FINE, end, own_windows, 0), (end, last + 1, side_windows, FINE)
    )
    coeffs = Stack(
        (0, FINE, side_coeffs, 0), (FINE, end - 1, own_coeffs, 0), (end - 1, last + 1, side_coeffs, FINE)
    )
    fields = [windows.of(field) for field in range(6)]
    scale_coeffs(1.0, *fields[2:], coeffs, (1, FINE), fields[1], True)
    scale_coeffs(1.0, *fields[2:], coeffs, (end - 1, last), fields[1], True)
    for sweep, pair in enumerate(chebyshev_weights(SWEEPS)):
        sweep_window(
            iterate, update, coeffs, (1 + sweep, last - sweep), pair, sweep == 0,
            source=fields[0] if sweep == 0 else None,
        )
    mid_x, mid_y = size_x // 2, size_y // 2
    coarse = []
    for block in range(mid_x):
        total = None
        for plane in (FINE + 2 * block, FINE + 2 * block + 1):
            remain = scaled_remain(coeffs, plane, iterate[plane - 1], iterate[plane], iterate[plane + 1])
            remain = (remain * coeffs[7, plane])[PAD : PAD + size_y]
            total = remain if total is None else total + remain
        coarse.append(merge(total) * 0.125)
        mid_target[block] = coarse[block]
    for plane in range(size_x):
        iterate_out[plane] = iterate[FINE + plane, PAD : PAD + size_y]

    tops, bottoms = Tiles(), Tiles()
    for plane in range(size_x - 4, size_x):
        tops.put(iterate_out[plane])
    for plane in range(4):
        bottoms.put(iterate_out[plane])
    upper = is_upper(size_z)
    tops_y, bottoms_y = Tiles(), Tiles()
    for pair in range(0, size_x, 2):
        one, two = iterate_out[pair], iterate_out[pair + 1]
        tops_y.put(jnp.where(upper, roll(one[size_y - 8 :], 4, 0), two[size_y - 8 :]))
        bottoms_y.put(jnp.where(upper, one[:8], roll(two[:8], 4, 0)))
    for writer in (tops, bottoms, tops_y, bottoms_y):
        for tile in coarse:
            writer.put(tile)
    for writer, ref in ((tops, up_corner), (bottoms, down_corner)):
        for tile in range(MID_CORNER):
            writer.put(ref[tile])
    for writer in (tops, bottoms):
        for tile in range(mid.shape[0]):
            writer.put(mid[tile])
    for writer, corners in ((tops, low_c), (bottoms, high_c)):
        for tile in range(corners.shape[0] - PASSED - 10, corners.shape[0]):
            writer.put(corners[tile])
    send(first_x, second_x, even, tops, bottoms)
    send(first_y, second_y, place[1] % 2 == 1, tops_y, bottoms_y)


MID_CORNER = 24
PASSED = 6


def whole_corner(ref, start, array, q, side):
    return ref[start + (array * 2 + q) * 2 + side]


def part_corner(ref, start, array, q):
    return ref[start + 16 + array * 2 + q - 2]


def corner_two_kernel(size_x, size_z, first_y, second_y, first, second):
    place = here()
    upper = is_upper(size_z)
    low_y, high_y = got(first_y, second_y, place[1] % 2 == 1)
    tops, bottoms = Tiles(), Tiles()
    put_corners(tops, low_y, high_y, [size_x - 1, size_x - 2, size_x - 3], upper, 0)
    put_corners(bottoms, low_y, high_y, range(3), upper, 0)
    for writer in (tops, bottoms):
        for ref in (low_y, high_y):
            for tile in range(ref.shape[0] - size_x // 2, ref.shape[0]):
                writer.put(ref[tile])
    send(first, second, place[0] % 2 == 0, tops, bottoms)


def level_two_near(near, low, low_y, high_y, low_c, high_c, low_x2, high_x2):
    known = {(0, 0): (low[0], low[1]), (0, -1): low_tiles_of(low_y), (0, 1): low_tiles_of(high_y)}
    for step, ref, distance in ((-1, low_c, 1), (1, high_c, 1), (-1, low_x2, 2), (1, high_x2, 2)):
        start = ref.shape[0] - PASSED
        for at, dy in enumerate((0, -1, 1)):
            known[step * distance, dy] = (ref[start + 2 * at], ref[start + 2 * at + 1])
    for (dx, dy), tiles in known.items():
        for kind in range(2):
            near[((dx + 2) * 3 + dy + 1) * 2 + kind] = tiles[kind]


def mid_coeffs_kernel(
    mid, low, low_y, high_y, first_c, second_c, first_x2, second_x2, coeffs, near, window
):
    place = here()
    low_x2, high_x2 = got(first_x2, second_x2, place[0] % 2 == 0)
    low_c, high_c = got(first_c, second_c, place[0] % 2 == 0)
    level_two_near(near, low, low_y, high_y, low_c, high_c, low_x2, high_x2)
    mid_y, mid_z = mid.shape[1:]
    mid_x = mid.shape[0] // 4
    mids = 4 * mid_x
    first = MID - mid_x
    corner = 4 * tiles_of(2 * mid_y, 2 * mid_z) + mid_x
    passed = corner + MID_CORNER
    for ref, start, block in ((low_x2, passed, 0), (mid, 0, 1), (high_x2, passed, 2)):
        for array in range(4):
            for plane in range(mid_x):
                window[array, first + block * mid_x + plane, mid_y : 2 * mid_y] = ref[start + array * mid_x + plane]
    for array in range(4):
        for plane in range(mid_x):
            window[array, MID + plane, :mid_y] = mid_strip(low_y, array, plane, True)
            window[array, MID + plane, 2 * mid_y :] = mid_strip(high_y, array, plane, False)
    passed += mids
    far = 3 * mid_x + first
    for ref, start, step, end in ((low_x2, MID - 1, -1, first - 1), (high_x2, MID + mid_x, 1, far)):
        for array in range(4):
            for q in range(mid_x):
                if q < 2:
                    one, two = (whole_corner(ref, corner, array, q, side) for side in range(2))
                else:
                    one = two = roll(part_corner(ref, corner, array, q), 4, 0)
                window[array, start + q * step, :mid_y] = one
                window[array, start + q * step, 2 * mid_y :] = two
        for at in range(5):
            array, plane = (at, end) if at < 4 else (1, end + step)
            window[array, plane, :mid_y] = ref[passed + at]
            window[array, plane, 2 * mid_y :] = ref[passed + at]
            window[array, plane, mid_y : 2 * mid_y] = ref[passed + 5 + at]
    scale_coeffs(0.25, *(window.at[array] for array in range(4)), coeffs, (first - 1, far + 1), None, True)


def mid_kernel(
    count_x, count_y, low, mid_target, coeffs, first_x2, second_x2, first_y2, second_y2, first_c2, second_c2,
    goal, slots, target, iterate, update,
):
    mid_x, mid_y, mid_z = mid_target.shape
    first = MID - mid_x
    far = 3 * mid_x + first
    fine_tiles = 4 * tiles_of(2 * mid_y, 2 * mid_z)
    place = here()
    even = place[0] % 2 == 0
    low_x2, high_x2 = got(first_x2, second_x2, even)
    low_y2, high_y2 = got(first_y2, second_y2, place[1] % 2 == 1)
    low_c2, high_c2 = got(first_c2, second_c2, even)
    blocks = {
        (0, 0): (low_c2, low_c2.shape[0] - 2 * mid_x), (0, 1): (low_x2, fine_tiles),
        (0, 2): (low_c2, low_c2.shape[0] - mid_x), (1, 0): (low_y2, low_y2.shape[0] - mid_x),
        (1, 2): (high_y2, high_y2.shape[0] - mid_x),
        (2, 0): (high_c2, high_c2.shape[0] - 2 * mid_x), (2, 1): (high_x2, fine_tiles),
        (2, 2): (high_c2, high_c2.shape[0] - mid_x),
    }
    for plane in range(mid_x):
        target[MID + plane, mid_y : 2 * mid_y] = mid_target[plane]
    for (bx, by), (ref, start) in blocks.items():
        for plane in range(mid_x):
            target[first + bx * mid_x + plane, by * mid_y : (by + 1) * mid_y] = ref[start + plane]

    weights = chebyshev_weights(SWEEPS)

    def start_sweep(i, carry):
        value = target[i] * coeffs[6, i]
        goal[i] = value
        update[i] = weights[0][1] * value
        iterate[i] = weights[0][1] * value
        return carry

    each(first, far, start_sweep)
    for sweep in range(1, SWEEPS):
        sweep_window(iterate, update, coeffs, (first + sweep, far - sweep), weights[sweep], False, goal)
    parts = []
    for block in range(0, mid_x, 2):
        total = None
        for plane in (MID + block, MID + block + 1):
            remain = scaled_remain(coeffs, plane, iterate[plane - 1], iterate[plane], iterate[plane + 1], goal)
            remain = (remain * coeffs[7, plane])[mid_y : 2 * mid_y]
            total = remain if total is None else total + remain
        parts.append(total)
    coarse = rows_merge(*parts)
    coarse = lanes_merge(coarse, coarse) * 0.125
    left = iota(TILE, 1) < TILE[1] // 2
    x1 = [iterate[MID + plane, mid_y : 2 * mid_y] for plane in range(mid_x)]
    low_one, low_two = low[0], low[1]
    pairs = count_x // 2
    own = place[0] // 2
    above, below = lax.rem(own + 1, pairs), lax.rem(own + pairs - 1, pairs)
    odd = jnp.logical_not(even)

    def fill(i, carry):
        up, down = i == above, i == below
        edge = jnp.where(up, mid_target[mid_x - 1], mid_target[0])
        edge_left, edge_right = jnp.where(left, coarse, roll(edge, TILE[1] // 2, 1)), jnp.where(left, coarse, edge)
        near_pair = up | down | (i == own)
        for j in range(count_y):
            me = place[1]
            beside = (j == me) | (j == lax.rem(me + 1, count_y)) | (j == lax.rem(me + count_y - 1, count_y))
            far = jnp.logical_not(near_pair & beside)
            one, two = 2 * i * count_y + j, (2 * i + 1) * count_y + j
            slots[one, 0] = edge_left
            slots[two, 0] = edge_right
            for at, tile in ((1, low_one), (2, low_two)):
                slots[one, at] = jnp.where(far | (down & odd), tile, jnp.where(up & even, x1[at + 1], x1[at - 1]))
                slots[two, at] = jnp.where(far | (up & even), tile, jnp.where(down & odd, x1[at - 1], x1[at + 1]))
        return carry

    each(0, pairs, fill)


def low_kernel(count_x, count_y, own_half, near, iterate, gathered, fields, coeffs, update):
    size_x, size_y, lanes = iterate.shape
    low_x, low_y = size_x // count_x, size_y // count_y
    low_z = lanes // 2
    me_x, me_y = here()

    def take_all(i, carry):
        for kind in range(3):
            gathered[i, kind] = own_half[i, kind]
        return carry

    each(0, count_x * count_y, take_all)
    for dy in (-1, 0, 1):
        for dx in range(-2, 3):
            source = lax.rem(me_x + dx + count_x, count_x) * count_y + lax.rem(me_y + dy + count_y, count_y)
            for kind in range(2):
                gathered[source, 1 + kind] = near[((dx + 2) * 3 + dy + 1) * 2 + kind]

    def place(i, carry):
        for j in range(count_y):
            for kind in range(3):
                tile = gathered[i * count_y + j, kind]
                for plane in range(low_x):
                    fields[kind, i * low_x + plane, j * low_y : (j + 1) * low_y] = tile[
                        plane * low_y : (plane + 1) * low_y
                    ]
        return carry

    each(0, count_x, place)
    lane = iota((size_y, lanes), 1)
    inside = lane < low_z
    scale = 0.0625
    weights = chebyshev_weights(COARSE_SWEEPS)

    def following(i):
        if isinstance(i, int):
            return (i + 1) % size_x
        return jnp.where(i == size_x - 1, 0, i + 1)

    def prepare(i, carry):
        yl, xl = fields[1, i], roll(fields[2, i], low_z, 1)
        zl, xh = roll(fields[1, i], low_z, 1), roll(fields[2, following(i)], low_z, 1)
        yh = roll(yl, -1, 0)
        zh = jnp.where(lane == low_z - 1, 0.0, roll(zl, -1, 1))
        diag = fields[2, i] + scale * (xl + xh + yl + yh + zl + zh)
        inverse = jnp.where(inside, 1.0 / diag, 0.0)
        scaled = scale * inverse
        coeffs[0, i] = scaled * xl
        coeffs[1, i] = scaled * xh
        coeffs[2, i] = scaled * yl
        coeffs[3, i] = scaled * yh
        coeffs[4, i] = jnp.where(lane == 0, 0.0, scaled * zl)
        coeffs[5, i] = scaled * zh
        goal = jnp.where(inside, fields[0, i], 0.0) * inverse
        coeffs[6, i] = goal
        update[i] = weights[0][1] * goal
        iterate[i] = weights[0][1] * goal
        return carry

    each(0, size_x, prepare)
    for pair in weights[1:]:
        start = iterate[0]

        def body(i, carry, pair=pair, start=start):
            below, here = carry
            if isinstance(i, int):
                above = start if i == size_x - 1 else iterate[i + 1]
            else:
                above = jnp.where(i == size_x - 1, start, iterate[following(i)])
            step = pair[1] * scaled_remain(coeffs, i, below, here, above) + pair[0] * update[i]
            update[i] = step
            iterate[i] = here + step
            return here, above

        each(0, size_x, body, (iterate[size_x - 1], start))


def window_kernel(
    fields_own, low_x1, high_x1, low_y1, high_y1, first_c1, second_c1,
    own, first_x, second_x, first_y, second_y, first_c, second_c,
    window, coeffs, own_windows, side_windows,
):
    place = here()
    even = place[0] % 2 == 0
    low_c1, high_c1 = got(first_c1, second_c1, even)
    low_x, high_x = got(first_x, second_x, even)
    low_y, high_y = got(first_y, second_y, place[1] % 2 == 1)
    low_c, high_c = got(first_c, second_c, even)
    size_x, size_y, size_z = own.shape
    assemble_owns(own_windows, fields_own, low_y1, high_y1)
    assemble_sides(side_windows, (size_y, size_z), low_x1, high_x1, low_c1, high_c1)
    end = FINE + size_x
    windows = Stack(
        (0, FINE, side_windows, 0), (FINE, end, own_windows, 0), (end, end + FINE, side_windows, FINE)
    )
    fields = [windows.of(field) for field in range(6)]
    scale_coeffs(1.0, *fields[2:], Stack((2, end + 3, coeffs, 0)), (2, end + 3), fields[1])
    assemble_own(window.at[FINE : FINE + size_x], own, low_y, high_y, 0, 0)
    assemble_side(window, FINE - 4, 4, (size_y, size_z), low_x, 0, low_c, 0, 3, True)
    assemble_side(window, FINE + size_x, 4, (size_y, size_z), high_x, 0, high_c, 0, 3, False)


def last_kernel(
    count_x, count_y, own_half, other_half, low_iterate, mid_coeffs, goal_in, fine_coeffs, window,
    out,
    goal, mid_iterate, mid_update,
    iterate, update,
):
    size_x, size_y, size_z = out.shape
    mid_x, mid_y, mid_z = size_x // 2, size_y // 2, size_z // 2
    last = size_x + 2 * FINE - 2
    coeffs = Stack((2, last, fine_coeffs, 0))
    me_x, me_y = here()
    even = me_x % 2 == 0

    def half(which, device, tile):
        one, two = own_half[device, tile], other_half[device, tile]
        return jnp.where(even, one, two) if which == 0 else jnp.where(even, two, one)

    def device(dx, dy):
        return lax.rem(me_x + dx + count_x, count_x) * count_y + lax.rem(me_y + dy + count_y, count_y)

    first, far = MID - mid_x, MID + 2 * mid_x
    for dy in (-1, 0, 1):
        rows = slice((dy + 1) * mid_y, (dy + 2) * mid_y)
        for dx in (-1, 0, 1):
            source = device(dx, dy)
            start = MID + dx * mid_x
            for plane in range(mid_x):
                mid_iterate[start + plane, rows] = half(plane // 2, source, 1 + plane % 2)
        for plane in range(2):
            mid_iterate[plane, rows] = own_half[device(-2, dy), 1 + plane]
            mid_iterate[far + plane, rows] = own_half[device(2, dy), 1 + plane]
    low_size_x, low_size_y = low_iterate.shape[:2]
    low_y = mid_y // 2
    turn = lax.rem(low_size_y - me_y * low_y + low_y, low_size_y)
    for plane in range((mid_x + 2 * MID) // 2):
        at = lax.rem(me_x * (mid_x // 2) - MID // 2 + plane + low_size_x, low_size_x)
        turned = pltpu.roll(low_iterate[at], turn, 0)
        one, two = lanes_spread(turned[: TILE[0]], 0), lanes_spread(turned[TILE[0] : 2 * TILE[0]], 0)
        part = jnp.concatenate([rows_spread(one, 0), rows_spread(one, 1), rows_spread(two, 0)], axis=0)
        mid_iterate[2 * plane] += part
        mid_iterate[2 * plane + 1] += part

    left = iota(TILE, 1) < TILE[1] // 2
    for plane in range(first, far):
        goal[plane] = goal_in[plane]
    for dy in (-1, 0, 1):
        rows = slice((dy + 1) * mid_y, (dy + 2) * mid_y)
        for plane, dx in ((first - 1, -2), (far, 2)):
            source = device(dx, dy)
            edge = jnp.where(left, roll(half(0, source, 0), TILE[1] // 2, 1), half(1, source, 0))
            goal[plane, rows] = edge * mid_coeffs[6, plane, rows]
    for sweep, pair in enumerate(chebyshev_weights(SWEEPS)):
        sweep_window(
            mid_iterate, mid_update, mid_coeffs, (first - 1 + sweep, far + 1 - sweep), pair, sweep == 0, goal
        )

    fine_low = FINE - 4
    for plane in range(mid_x + 4):
        turned = roll(mid_iterate[MID - 2 + plane], -4, 0)
        lines = []
        for r in range(2):
            tile = turned[r * TILE[0] : (r + 1) * TILE[0]]
            for side in range(2):
                line = rows_spread(tile, side)
                lines.append(jnp.concatenate([lanes_spread(line, 0), lanes_spread(line, 1)], axis=1))
        part = jnp.concatenate(lines, axis=0)
        for at in (fine_low + 2 * plane, fine_low + 2 * plane + 1):
            iterate[at] = window[at] + part
    for sweep, pair in enumerate(chebyshev_weights(SWEEPS)):
        sweep_window(
            iterate, update, coeffs, (2 + sweep, last - sweep), pair, sweep == 0
        )
    for plane in range(size_x):
        out[plane] = iterate[FINE + plane, PAD : PAD + size_y]


def call(kernel, inputs, outs, scratch=(), scalars=0, far_in=(), far_out=(), sems=0):
    def place(i):
        return pltpu.SMEM if i < scalars else pltpu.HBM if i in far_in else pltpu.VMEM

    near = [x.shape for i, x in enumerate(inputs) if i >= scalars and i not in far_in]
    near += [shape for i, shape in enumerate(outs) if i not in far_out] + list(scratch)
    used = 4 * sum(math.prod(shape) for shape in near)
    inputs = [pltpu.with_memory_space_constraint(x, pltpu.HBM) if i in far_in else x for i, x in enumerate(inputs)]
    return pl.pallas_call(
        kernel,
        out_shape=[
            pltpu.HBM(shape, F32) if i in far_out else jax.ShapeDtypeStruct(shape, F32)
            for i, shape in enumerate(outs)
        ],
        in_specs=[pl.BlockSpec(memory_space=place(i)) for i in range(len(inputs))],
        out_specs=[
            pl.BlockSpec(memory_space=pltpu.HBM if i in far_out else pltpu.VMEM) for i in range(len(outs))
        ],
        scratch_shapes=[pltpu.VMEM(shape, F32) for shape in scratch]
        + ([pltpu.SemaphoreType.DMA((sems,))] if sems > 1 else [pltpu.SemaphoreType.DMA] * sems),
        cost_estimate=pl.CostEstimate(flops=1000, bytes_accessed=1000, transcendentals=0),
        compiler_params=pltpu.CompilerParams(vmem_limit_bytes=used + used // 4 + 2 * 1024 * 1024),
    )(*inputs)


def local(source, initial, absorption, beta_x, beta_y, beta_z):
    size_x, size_y, size_z = source.shape
    mid_x, mid_y, mid_z = size_x // 2, size_y // 2, size_z // 2
    low_x, low_y = mid_x // 2, mid_y // 2
    count_x, count_y = lax.axis_size("gx"), lax.axis_size("gy")
    devices = count_x * count_y
    plane, strip = tiles_of(size_y, size_z), tiles_of(8, size_z)
    mids = 4 * mid_x

    def tiles(count):
        return (count,) + TILE

    pairs = size_x // 2
    up_x, down_x, up_y, down_y, mid, low, own = call(
        pack_kernel,
        (initial, source, absorption, beta_x, beta_y, beta_z),
        [
            tiles(sum(UP_PLANES) * plane),
            tiles(sum(DOWN_PLANES) * plane),
            tiles((6 * pairs + 1) * strip + 2 + 4 * STRIP),
            tiles((6 * pairs + 2) * strip + 2 + 4 * STRIP),
            tiles(mids),
            tiles(2),
            (6,) + source.shape,
        ],
        far_in=range(6),
        sems=6,
    )
    low_x1, high_x1 = shifted(up_x, "gx", 1), shifted(down_x, "gx", -1)
    low_y1, high_y1 = shifted(up_y, "gy", 1), shifted(down_y, "gy", -1)
    first_c1, second_c1 = call(
        functools.partial(corner_kernel, size_x, size_z),
        (low_y1, high_y1, mid, low),
        [tiles(corner_tiles(DOWN_CORNER) * strip + 16)] * 2,
    )
    first_c1, second_c1 = swapped(first_c1, second_c1, "gx")

    tall = (size_y + 2 * PAD, size_z)
    wide = (size_x + 2 * FINE,) + tall
    own_windows, own_coeffs, up_corner, down_corner = call(
        own_kernel,
        (own, low_y1, high_y1),
        [(6, size_x) + tall, (8, size_x - 1) + tall, tiles(MID_CORNER), tiles(MID_CORNER)],
    )
    iterate, mid_target, first_x2, second_x2, first_y2, second_y2 = call(
        fine_kernel,
        (own_windows, own_coeffs, up_corner, down_corner, mid, low_x1, high_x1, first_c1, second_c1),
        [
            source.shape,
            (mid_x, mid_y, mid_z),
            tiles(4 * plane + mid_x + MID_CORNER + mids + 10 + PASSED),
            tiles(4 * plane + mid_x + MID_CORNER + mids + 10 + PASSED),
            tiles(pairs * strip + mid_x),
            tiles(pairs * strip + mid_x),
        ],
        scratch=[(6, 2 * FINE) + tall, (8, 2 * FINE + 1) + tall, wide, wide],
    )
    first_x2, second_x2 = swapped(first_x2, second_x2, "gx")
    first_y2, second_y2 = swapped(first_y2, second_y2, "gy")
    first_c2, second_c2 = call(
        functools.partial(corner_two_kernel, size_x, size_z),
        (first_y2, second_y2),
        [tiles(2 * strip + 2 * mid_x)] * 2,
    )
    first_c2, second_c2 = swapped(first_c2, second_c2, "gx")

    mid_wide = (mid_x + 2 * MID, 3 * mid_y, mid_z)
    mid_coeffs, near = call(
        mid_coeffs_kernel,
        (mid, low, low_y1, high_y1, first_c1, second_c1, first_x2, second_x2),
        [(8,) + mid_wide, tiles(30)],
        [(4,) + mid_wide],
    )
    goal, slots = call(
        functools.partial(mid_kernel, count_x, count_y),
        (low, mid_target, mid_coeffs, first_x2, second_x2, first_y2, second_y2, first_c2, second_c2),
        [mid_wide, (devices, 3) + TILE],
        [mid_wide] * 3,
    )
    own_half = lax.all_to_all(slots, ("gx", "gy"), 0, 0)
    other_half = lax.ppermute(own_half, "gx", [(i, i ^ 1) for i in range(count_x)])

    window, coeffs = call(
        window_kernel,
        (own, low_x1, high_x1, low_y1, high_y1, first_c1, second_c1)
        + (iterate, first_x2, second_x2, first_y2, second_y2, first_c2, second_c2),
        [wide, (7, wide[0] - 4) + tall],
        [(6, size_x) + tall, (6, 2 * FINE) + tall],
    )
    low_wide = (low_x * count_x, low_y * count_y, mid_z)
    (low_iterate,) = call(
        functools.partial(low_kernel, count_x, count_y),
        (own_half, near),
        [low_wide],
        [(devices, 3) + TILE, (3,) + low_wide, (7,) + low_wide, low_wide],
    )
    (result,) = call(
        functools.partial(last_kernel, count_x, count_y),
        (own_half, other_half, low_iterate, mid_coeffs, goal, coeffs, window),
        [source.shape],
        [mid_wide, mid_wide, mid_wide]
        + [wide, wide],
    )
    return result


def solution(mesh):
    spec = P("gx", "gy", None)
    return jax.shard_map(
        local, mesh=mesh, in_specs=(spec,) * 6, out_specs=spec, check_vma=False
    )
```

```python
import functools
import math

import jax
import jax.numpy as jnp
from jax import lax
from jax.experimental import pallas as pl
from jax.experimental.pallas import tpu as pltpu
from jax.sharding import PartitionSpec as P

SWEEPS = 4
COARSE_SWEEPS = 8
F32 = jnp.float32
TILE = (8, 128)
PAD = 8
FINE = 5
MID = 6


def chebyshev_weights(sweeps):
    cheb_theta = 1.125
    cheb_delta = 0.875
    cheb_sigma = cheb_theta / cheb_delta
    rho_old = 1.0 / cheb_sigma
    weights = [(0.0, 1.0 / cheb_theta)]
    for sweep in range(1, sweeps):
        rho_new = 1.0 / (2.0 * cheb_sigma - rho_old)
        weights.append((rho_new * rho_old, 2.0 * rho_new / cheb_delta))
        rho_old = rho_new
    return weights


def iota(shape, axis):
    return lax.broadcasted_iota(jnp.int32, shape, axis)


def roll(value, shift, axis):
    return pltpu.roll(value, shift % value.shape[axis], axis)


def take(tile, index, axis):
    return jnp.take_along_axis(tile, index, axis=axis, mode="promise_in_bounds")


def rows_spread(tile, half):
    return take(tile, iota(TILE, 0) // 2 + 4 * half, 0)


def lanes_spread(tile, half):
    return take(tile, iota(TILE, 1) // 2 + 64 * half, 1)


def rows_merge(one, two, pairs=True):
    row = iota(TILE, 0)
    if pairs:
        one, two = one + roll(one, -1, 0), two + roll(two, -1, 0)
    index = (2 * row) % TILE[0]
    return jnp.where(row < TILE[0] // 2, take(one, index, 0), take(two, index, 0))


def lanes_merge(one, two, pairs=True):
    lane = iota(TILE, 1)
    if pairs:
        one, two = one + roll(one, -1, 1), two + roll(two, -1, 1)
    index = (2 * lane) % TILE[1]
    return jnp.where(lane < TILE[1] // 2, take(one, index, 1), take(two, index, 1))


def merge(plane, row_pairs=True, lane_pairs=True):
    halves = []
    for side in range(2):
        lanes = slice(side * TILE[1], (side + 1) * TILE[1])
        halves.append(rows_merge(plane[: TILE[0], lanes], plane[TILE[0] :, lanes], row_pairs))
    return lanes_merge(*halves, lane_pairs)


def each(start, stop, body, carry=0):
    if stop - start > 20:
        return lax.fori_loop(start, stop, body, carry, unroll=2)
    for i in range(start, stop):
        carry = body(i, carry)
    return carry


def here():
    return lax.axis_index("gx"), lax.axis_index("gy")


class Writer:
    def __init__(self, ref):
        self.ref, self.at = ref, 0

    def put(self, value):
        rows, columns = value.shape
        for r in range(0, rows, TILE[0]):
            for c in range(0, columns, TILE[1]):
                self.ref[self.at] = value[r : r + TILE[0], c : c + TILE[1]]
                self.at += 1


class Tiles:
    def __init__(self):
        self.tiles = []

    def put(self, value):
        rows, columns = value.shape
        for r in range(0, rows, TILE[0]):
            for c in range(0, columns, TILE[1]):
                self.tiles.append(value[r : r + TILE[0], c : c + TILE[1]])


def send(first, second, even, up, down):
    for at, (one, two) in enumerate(zip(up.tiles, down.tiles, strict=True)):
        first[at] = jnp.where(even, one, two)
        second[at] = jnp.where(even, two, one)


class Got:
    def __init__(self, first, second, even, low):
        self.refs = (second, first) if low else (first, second)
        self.even, self.shape = even, first.shape

    def __getitem__(self, at):
        return jnp.where(self.even, self.refs[0][at], self.refs[1][at])


def got(first, second, even):
    return Got(first, second, even, True), Got(first, second, even, False)


class Reader:
    def __init__(self, ref, at=0):
        self.ref, self.at = ref, at

    def get(self, rows, columns):
        lines = []
        for _ in range(rows // TILE[0]):
            parts = []
            for _ in range(columns // TILE[1]):
                parts.append(self.ref[self.at])
                self.at += 1
            lines.append(parts[0] if len(parts) == 1 else jnp.concatenate(parts, axis=1))
        return lines[0] if len(lines) == 1 else jnp.concatenate(lines, axis=0)


UP_PLANES = (5, 4, 4, 4, 4, 4)
DOWN_PLANES = (5, 4, 4, 5, 4, 4)
UP_CORNER = (4, 3, 3, 3, 4, 3)
DOWN_CORNER = (4, 3, 3, 4, 4, 3)
STRIP = 2


def corner_tiles(counts):
    return sum(count - 1 for count in counts)


def tiles_of(rows, columns):
    return (rows // TILE[0]) * (columns // TILE[1])


def is_upper(width):
    return iota((TILE[0], width), 0) < TILE[0] // 2


def swapped(first, second, axis):
    count = lax.axis_size(axis)
    outer = [(i, (i + 1 if i % 2 else i - 1) % count) for i in range(count)]
    inner = [(i, i ^ 1) for i in range(count)]
    if axis == "gy":
        inner, outer = outer, inner
    return lax.ppermute(first, axis, inner), lax.ppermute(second, axis, outer)


def shifted(value, axis, step):
    count = lax.axis_size(axis)
    return lax.ppermute(value, axis, [(i, (i + step) % count) for i in range(count)])


def pack_kernel(
    ini_in, src_in, absorb_in, face_x_in, face_y_in, face_z_in,
    up_x, down_x, up_y, down_y, mid, low, own, sems,
):
    copies = []
    for field, ref in enumerate((ini_in, src_in, absorb_in, face_x_in, face_y_in, face_z_in)):
        copies.append(pltpu.make_async_copy(ref, own.at[field], sems.at[field]))
        copies[-1].start()
    for copy in copies:
        copy.wait()
    fields = tuple(own.at[field] for field in range(6))
    ini, src, absorb, face_x, face_y, face_z = fields
    size_x, size_y, size_z = ini.shape
    mid_x = size_x // 2
    for block in range(mid_x):
        one, two = 2 * block, 2 * block + 1
        mid[block] = merge(absorb[one] + absorb[two]) * 0.125
        mid[mid_x + block] = merge(face_x[one]) * 0.25
        mid[2 * mid_x + block] = merge(face_y[one] + face_y[two], row_pairs=False) * 0.25
        mid[3 * mid_x + block] = merge(face_z[one] + face_z[two], lane_pairs=False) * 0.25

    def coarser(array, planes, row_pairs=True, lane_pairs=True):
        parts = []
        for block in range(0, mid_x, 2):
            total = None
            for plane in range(planes):
                part = mid[array * mid_x + block + plane]
                total = part if total is None else total + part
            parts.append(total)
        tile = rows_merge(*parts, row_pairs)
        return lanes_merge(tile, tile, lane_pairs)

    left = iota(TILE, 1) < TILE[1] // 2
    low[0] = jnp.where(left, coarser(2, 2, row_pairs=False), coarser(3, 2, lane_pairs=False)) * 0.25
    low[1] = jnp.where(left, coarser(0, 2) * 0.125, coarser(1, 1) * 0.25)

    tops, bottoms = Writer(up_x), Writer(down_x)
    for ref, count in zip(fields, UP_PLANES):
        for plane in range(size_x - count, size_x):
            tops.put(ref[plane])
    for ref, count in zip(fields, DOWN_PLANES):
        for plane in range(count):
            bottoms.put(ref[plane])

    upper = is_upper(size_z)
    tops_y, bottoms_y = Writer(up_y), Writer(down_y)
    for ref in fields:
        for pair in range(0, size_x, 2):
            one, two = ref[pair], ref[pair + 1]
            tops_y.put(jnp.where(upper, roll(one[size_y - 8 :], 4, 0), two[size_y - 8 :]))
            bottoms_y.put(jnp.where(upper, one[:8], roll(two[:8], 4, 0)))
    tops_y.put(ini[:, size_y - 5, :])
    bottoms_y.put(ini[:, 4, :])
    bottoms_y.put(face_y[:, 4, :])
    for writer in (tops_y, bottoms_y):
        for tile in range(2):
            writer.put(low[tile])
    upper = is_upper(TILE[1])
    for array in range(4):
        for pair in range(0, mid_x, 2):
            one, two = mid[array * mid_x + pair], mid[array * mid_x + pair + 1]
            for writer in (tops_y, bottoms_y):
                writer.put(jnp.where(upper, roll(one, -2, 0), roll(two, 2, 0)))


def corner_of(low_y, high_y, plane, upper, first_tile=0):
    width = upper.shape[1]
    at = first_tile + (plane // 2) * tiles_of(8, width)
    low = Reader(low_y, at).get(8, width)
    high = Reader(high_y, at).get(8, width)
    if plane % 2 == 0:
        return jnp.where(upper, low, roll(high, 4, 0))
    return jnp.where(upper, roll(low, 4, 0), high)


def mix(near, far):
    row = iota(near.shape, 0)
    return jnp.where((row >= 2) & (row < 6), near, roll(far, 3, 0))


def put_corners(writer, low_y, high_y, planes, upper, first_tile):
    parts = [corner_of(low_y, high_y, plane, upper, first_tile) for plane in planes]
    for part in parts[:-2]:
        writer.put(part)
    writer.put(mix(*parts[-2:]))


def mid_beside(ref, array, plane, low):
    pairs = (ref.shape[0] - 4 * STRIP - 2) // 12
    at = ((2 + array) * pairs + plane) * 2
    halves = []
    for side in range(2):
        total = ref[at + side]
        if array != 1:
            total = total + roll(total, 4, 0)
        if array != 2:
            total = total + roll(total, -1, 0)
        halves.append(take(total, (2 * iota(TILE, 0) + (4 if low else 0)) % TILE[0], 0))
    return lanes_merge(*halves, array != 3) * (0.125 if array == 0 else 0.25)


def mid_strip(ref, array, plane, low):
    far = roll(ref[ref.shape[0] - 4 * STRIP + array * STRIP + plane // 2], 2 if plane % 2 == 0 else -2, 0)
    row = iota(TILE, 0)
    return jnp.where((row >= 2) & (row < 6), far, mid_beside(ref, array, plane, low))


def corner_kernel(size_x, size_z, low_y, high_y, mid, low_faces, first, second):
    place = here()
    upper = is_upper(size_z)
    per_field = (size_x // 2) * tiles_of(8, size_z)
    tops, bottoms = Tiles(), Tiles()
    for field in range(6):
        start = field * per_field
        planes = [size_x - 1 - plane for plane in range(UP_CORNER[field])]
        put_corners(tops, low_y, high_y, planes, upper, start)
        put_corners(bottoms, low_y, high_y, range(DOWN_CORNER[field]), upper, start)
    mid_x = size_x // 2
    upper = is_upper(TILE[1])
    for _ in range(len(bottoms.tiles) - len(tops.tiles)):
        tops.put(low_faces[0])
    for writer, near, next_plane in ((tops, mid_x - 1, mid_x - 2), (bottoms, 0, 1)):
        wanted = [(array, near) for array in range(4)] + [(1, next_plane)]
        for array, plane in wanted:
            writer.put(
                jnp.where(upper, mid_beside(high_y, array, plane, False), mid_beside(low_y, array, plane, True))
            )
        for array, plane in wanted:
            writer.put(mid[array * mid_x + plane])
        for tiles in ((low_faces[0], low_faces[1]), low_tiles_of(low_y), low_tiles_of(high_y)):
            for tile in tiles:
                writer.put(tile)
    send(first, second, place[0] % 2 == 0, tops, bottoms)


def low_tiles_of(ref):
    end = ref.shape[0] - 4 * STRIP
    return ref[end - 2], ref[end - 1]


class Planes:
    def __init__(self, *parts):
        self.parts = parts
        self.shape = parts[0][2].shape

    def find(self, i):
        for start, stop, ref, offset, lead in self.parts:
            if start <= i < stop:
                return ref, lead + (i - start + offset,)
        raise IndexError(i)

    def __getitem__(self, i):
        ref, index = self.find(i)
        return ref[index]


class Stack:
    def __init__(self, *parts):
        self.parts = parts

    def of(self, kind):
        return Planes(*((a, b, ref, offset, (kind,)) for a, b, ref, offset in self.parts))

    def __getitem__(self, index):
        return self.of(index[0])[index[1]]

    def __setitem__(self, index, value):
        ref, place = self.of(index[0]).find(index[1])
        ref[place] = value


def scale_coeffs(scale, absorb, face_x, face_y, face_z, coeffs, planes, target=None, diagonal=None):
    rows, lanes = absorb.shape[-2:]
    lane = iota((rows, lanes), 1)

    def body(i, carry):
        xl, xh = face_x[i], face_x[i + 1]
        yl, zl = face_y[i], face_z[i]
        yh = roll(yl, -1, 0)
        zh = jnp.where(lane == lanes - 1, 0.0, roll(zl, -1, 1))
        diag = absorb[i] + scale * (xl + xh + yl + yh + zl + zh)
        inverse = 1.0 / diag
        scaled = scale * inverse
        coeffs[0, i] = scaled * xl
        coeffs[1, i] = scaled * xh
        coeffs[2, i] = scaled * yl
        coeffs[3, i] = scaled * yh
        coeffs[4, i] = jnp.where(lane == 0, 0.0, scaled * zl)
        coeffs[5, i] = scaled * zh
        if target is not None:
            coeffs[6, i] = target[i] * inverse
        else:
            coeffs[6, i] = inverse
        if diagonal is not None:
            coeffs[7, i] = diag
        return carry

    each(*planes, body)


def scaled_remain(coeffs, i, below, here, above, goal=None):
    along_z = coeffs[4, i] * roll(here, 1, 1) + coeffs[5, i] * roll(here, -1, 1)
    along_y = coeffs[2, i] * roll(here, 1, 0) + coeffs[3, i] * roll(here, -1, 0)
    along_x = coeffs[0, i] * below + coeffs[1, i] * above
    return ((coeffs[6, i] if goal is None else goal[i]) - here + along_x) + (along_y + along_z)


def sweep_window(iterate, update, coeffs, planes, pair, first, goal=None, source=None):
    start, stop = planes
    source = iterate if source is None else source

    def body(i, carry):
        below, here = carry
        above = source[i + 1]
        step = pair[1] * scaled_remain(coeffs, i, below, here, above, goal)
        if not first:
            step = step + pair[0] * update[i]
        update[i] = step
        iterate[i] = here + step
        return here, above

    each(start, stop, body, (source[start - 1], source[start]))


def assemble_own(window, own, low_y, high_y, low_start, high_start):
    size_x, size_y, size_z = own.shape
    high = PAD + size_y
    low_reader, high_reader = Reader(low_y, low_start), Reader(high_y, high_start)
    for pair in range(0, size_x, 2):
        window[pair, PAD:high] = own[pair]
        window[pair + 1, PAD:high] = own[pair + 1]
        tile = low_reader.get(8, size_z)
        window[pair, 0:8] = roll(tile, 4, 0)
        window[pair + 1, 0:8] = tile
        tile = high_reader.get(8, size_z)
        window[pair, high : high + 8] = tile
        window[pair + 1, high : high + 8] = roll(tile, 4, 0)


def assemble_side(window, first, count, rows, planes, plane_start, corners, corner_start, corner_count, from_end):
    size_y, size_z = rows
    high = PAD + size_y
    reader = Reader(planes, plane_start)
    for plane in range(count):
        window[first + plane, PAD:high] = reader.get(size_y, size_z)
    reader = Reader(corners, corner_start)
    tiles = [roll(reader.get(8, size_z), 4, 0) for _ in range(corner_count - 1)]
    tiles.append(roll(tiles[-1], -3, 0))
    for plane, tile in enumerate(tiles):
        at = first + count - 1 - plane if from_end else first + plane
        window[at, 0:8] = tile
        window[at, high : high + 8] = tile


def assemble_owns(windows, own, low_y, high_y):
    size_x, size_y, size_z = own.shape[1:]
    per_field = (size_x // 2) * tiles_of(8, size_z)
    for field in range(6):
        assemble_own(windows.at[field], own.at[field], low_y, high_y, field * per_field, field * per_field)
    low_line = Reader(low_y, 6 * per_field).get(8, size_z)
    high_reader = Reader(high_y, 6 * per_field)
    high_line = high_reader.get(8, size_z)
    face_line = high_reader.get(8, size_z)
    high = PAD + size_y
    for plane in range(size_x):
        windows[0, plane, 3:4] = low_line[plane : plane + 1]
        windows[0, plane, high + 4 : high + 5] = high_line[plane : plane + 1]
        windows[4, plane, high + 4 : high + 5] = face_line[plane : plane + 1]


def assemble_sides(side_windows, rows, low_x, high_x, low_c, high_c):
    plane_tiles, strip_tiles = tiles_of(*rows), tiles_of(8, rows[1])
    starts = [0] * 4
    for field in range(6):
        up, down, up_c, down_c = (
            kinds[field] for kinds in (UP_PLANES, DOWN_PLANES, UP_CORNER, DOWN_CORNER)
        )
        window = side_windows.at[field]
        assemble_side(
            window, FINE - up, up, rows, low_x, starts[0], low_c, starts[2], up_c, True
        )
        assemble_side(
            window, FINE, down, rows, high_x, starts[1], high_c, starts[3], down_c, False
        )
        starts[0] += up * plane_tiles
        starts[1] += down * plane_tiles
        starts[2] += (up_c - 1) * strip_tiles
        starts[3] += (down_c - 1) * strip_tiles


def own_kernel(own, low_y, high_y, windows, coeffs, up_corner, down_corner, strips):
    assemble_owns(windows, own, low_y, high_y)
    fields = [windows.at[field] for field in range(6)]
    scale_coeffs(1.0, *fields[2:], coeffs, (0, own.shape[1] - 1), fields[1], True)
    mid_x = own.shape[1] // 2
    tops, bottoms = Writer(up_corner), Writer(down_corner)
    upper = is_upper(TILE[1])
    for side, (ref, low) in enumerate(((low_y, True), (high_y, False))):
        for array in range(4):
            for plane in range(mid_x):
                strips[(side * 4 + array) * mid_x + plane] = mid_strip(ref, array, plane, low)
    for writer, first, step in ((tops, mid_x - 1, -1), (bottoms, 0, 1)):
        for array in range(4):
            for q in range(2):
                for side in range(2):
                    writer.put(strips[(side * 4 + array) * mid_x + first + q * step])
        for array in range(4):
            for q in range(2, 4):
                one, two = (roll(strips[(side * 4 + array) * mid_x + first + q * step], 4, 0) for side in range(2))
                writer.put(jnp.where(upper, one, two))


def fine_kernel(
    own_windows, own_coeffs, up_corner, down_corner, mid, low_x, high_x, first_c, second_c,
    iterate_out, mid_target, first_x, second_x, first_y, second_y,
    side_windows, side_coeffs, iterate, update,
):
    size_x, size_z = own_windows.shape[1], own_windows.shape[3]
    size_y = own_windows.shape[2] - 2 * PAD
    place = here()
    even = place[0] % 2 == 0
    low_c, high_c = got(first_c, second_c, even)
    assemble_sides(side_windows, (size_y, size_z), low_x, high_x, low_c, high_c)
    end = FINE + size_x
    last = end + FINE - 1
    windows = Stack(
        (0, FINE, side_windows, 0), (FINE, end, own_windows, 0), (end, last + 1, side_windows, FINE)
    )
    coeffs = Stack(
        (0, FINE, side_coeffs, 0), (FINE, end - 1, own_coeffs, 0), (end - 1, last + 1, side_coeffs, FINE)
    )
    fields = [windows.of(field) for field in range(6)]
    scale_coeffs(1.0, *fields[2:], coeffs, (1, FINE), fields[1], True)
    scale_coeffs(1.0, *fields[2:], coeffs, (end - 1, last), fields[1], True)
    for sweep, pair in enumerate(chebyshev_weights(SWEEPS)):
        sweep_window(
            iterate, update, coeffs, (1 + sweep, last - sweep), pair, sweep == 0,
            source=fields[0] if sweep == 0 else None,
        )
    mid_x, mid_y = size_x // 2, size_y // 2
    coarse = []
    for block in range(mid_x):
        total = None
        for plane in (FINE + 2 * block, FINE + 2 * block + 1):
            remain = scaled_remain(coeffs, plane, iterate[plane - 1], iterate[plane], iterate[plane + 1])
            remain = (remain * coeffs[7, plane])[PAD : PAD + size_y]
            total = remain if total is None else total + remain
        coarse.append(merge(total) * 0.125)
        mid_target[block] = coarse[block]
    for plane in range(size_x):
        iterate_out[plane] = iterate[FINE + plane, PAD : PAD + size_y]

    tops, bottoms = Tiles(), Tiles()
    for plane in range(size_x - 4, size_x):
        tops.put(iterate_out[plane])
    for plane in range(4):
        bottoms.put(iterate_out[plane])
    upper = is_upper(size_z)
    tops_y, bottoms_y = Tiles(), Tiles()
    for pair in range(0, size_x, 2):
        one, two = iterate_out[pair], iterate_out[pair + 1]
        tops_y.put(jnp.where(upper, roll(one[size_y - 8 :], 4, 0), two[size_y - 8 :]))
        bottoms_y.put(jnp.where(upper, one[:8], roll(two[:8], 4, 0)))
    for writer in (tops, bottoms, tops_y, bottoms_y):
        for tile in coarse:
            writer.put(tile)
    for writer, ref in ((tops, up_corner), (bottoms, down_corner)):
        for tile in range(MID_CORNER):
            writer.put(ref[tile])
    for writer in (tops, bottoms):
        for tile in range(mid.shape[0]):
            writer.put(mid[tile])
    for writer, corners in ((tops, low_c), (bottoms, high_c)):
        for tile in range(corners.shape[0] - PASSED - 10, corners.shape[0]):
            writer.put(corners[tile])
    send(first_x, second_x, even, tops, bottoms)
    send(first_y, second_y, place[1] % 2 == 1, tops_y, bottoms_y)


MID_CORNER = 24
PASSED = 6


def whole_corner(ref, start, array, q, side):
    return ref[start + (array * 2 + q) * 2 + side]


def part_corner(ref, start, array, q):
    return ref[start + 16 + array * 2 + q - 2]


def corner_two_kernel(size_x, size_z, first_y, second_y, first, second):
    place = here()
    upper = is_upper(size_z)
    low_y, high_y = got(first_y, second_y, place[1] % 2 == 1)
    tops, bottoms = Tiles(), Tiles()
    put_corners(tops, low_y, high_y, [size_x - 1, size_x - 2, size_x - 3], upper, 0)
    put_corners(bottoms, low_y, high_y, range(3), upper, 0)
    for writer in (tops, bottoms):
        for ref in (low_y, high_y):
            for tile in range(ref.shape[0] - size_x // 2, ref.shape[0]):
                writer.put(ref[tile])
    send(first, second, place[0] % 2 == 0, tops, bottoms)


def level_two_near(near, low, low_y, high_y, low_c, high_c, low_x2, high_x2):
    known = {(0, 0): (low[0], low[1]), (0, -1): low_tiles_of(low_y), (0, 1): low_tiles_of(high_y)}
    for step, ref, distance in ((-1, low_c, 1), (1, high_c, 1), (-1, low_x2, 2), (1, high_x2, 2)):
        start = ref.shape[0] - PASSED
        for at, dy in enumerate((0, -1, 1)):
            known[step * distance, dy] = (ref[start + 2 * at], ref[start + 2 * at + 1])
    for (dx, dy), tiles in known.items():
        for kind in range(2):
            near[((dx + 2) * 3 + dy + 1) * 2 + kind] = tiles[kind]


def mid_coeffs_kernel(
    mid, low, strips, low_y, high_y, first_c, second_c, first_x2, second_x2, coeffs, near, window
):
    place = here()
    low_x2, high_x2 = got(first_x2, second_x2, place[0] % 2 == 0)
    low_c, high_c = got(first_c, second_c, place[0] % 2 == 0)
    level_two_near(near, low, low_y, high_y, low_c, high_c, low_x2, high_x2)
    mid_y, mid_z = mid.shape[1:]
    mid_x = mid.shape[0] // 4
    mids = 4 * mid_x
    first = MID - mid_x
    corner = 4 * tiles_of(2 * mid_y, 2 * mid_z) + mid_x
    passed = corner + MID_CORNER
    for ref, start, block in ((low_x2, passed, 0), (mid, 0, 1), (high_x2, passed, 2)):
        for array in range(4):
            for plane in range(mid_x):
                window[array, first + block * mid_x + plane, mid_y : 2 * mid_y] = ref[start + array * mid_x + plane]
    for array in range(4):
        for plane in range(mid_x):
            window[array, MID + plane, :mid_y] = strips[array * mid_x + plane]
            window[array, MID + plane, 2 * mid_y :] = strips[(4 + array) * mid_x + plane]
    passed += mids
    far = 3 * mid_x + first
    for ref, start, step, end in ((low_x2, MID - 1, -1, first - 1), (high_x2, MID + mid_x, 1, far)):
        for array in range(4):
            for q in range(mid_x):
                if q < 2:
                    one, two = (whole_corner(ref, corner, array, q, side) for side in range(2))
                else:
                    one = two = roll(part_corner(ref, corner, array, q), 4, 0)
                window[array, start + q * step, :mid_y] = one
                window[array, start + q * step, 2 * mid_y :] = two
        for at in range(5):
            array, plane = (at, end) if at < 4 else (1, end + step)
            window[array, plane, :mid_y] = ref[passed + at]
            window[array, plane, 2 * mid_y :] = ref[passed + at]
            window[array, plane, mid_y : 2 * mid_y] = ref[passed + 5 + at]
    scale_coeffs(0.25, *(window.at[array] for array in range(4)), coeffs, (first - 1, far + 1), None, True)


def mid_kernel(
    count_x, count_y, low, mid_target, coeffs, first_x2, second_x2, first_y2, second_y2, first_c2, second_c2, unused,
    goal, slots, target, iterate, update,
):
    mid_x, mid_y, mid_z = mid_target.shape
    first = MID - mid_x
    far = 3 * mid_x + first
    fine_tiles = 4 * tiles_of(2 * mid_y, 2 * mid_z)
    place = here()
    even = place[0] % 2 == 0
    low_x2, high_x2 = got(first_x2, second_x2, even)
    low_y2, high_y2 = got(first_y2, second_y2, place[1] % 2 == 1)
    low_c2, high_c2 = got(first_c2, second_c2, even)
    blocks = {
        (0, 0): (low_c2, low_c2.shape[0] - 2 * mid_x), (0, 1): (low_x2, fine_tiles),
        (0, 2): (low_c2, low_c2.shape[0] - mid_x), (1, 0): (low_y2, low_y2.shape[0] - mid_x),
        (1, 2): (high_y2, high_y2.shape[0] - mid_x),
        (2, 0): (high_c2, high_c2.shape[0] - 2 * mid_x), (2, 1): (high_x2, fine_tiles),
        (2, 2): (high_c2, high_c2.shape[0] - mid_x),
    }
    for plane in range(mid_x):
        target[MID + plane, mid_y : 2 * mid_y] = mid_target[plane]
    for (bx, by), (ref, start) in blocks.items():
        for plane in range(mid_x):
            target[first + bx * mid_x + plane, by * mid_y : (by + 1) * mid_y] = ref[start + plane]

    weights = chebyshev_weights(SWEEPS)

    def start_sweep(i, carry):
        value = target[i] * coeffs[6, i]
        goal[i] = value
        update[i] = weights[0][1] * value
        iterate[i] = weights[0][1] * value
        return carry

    each(first, far, start_sweep)
    for sweep in range(1, SWEEPS):
        sweep_window(iterate, update, coeffs, (first + sweep, far - sweep), weights[sweep], False, goal)
    parts = []
    for block in range(0, mid_x, 2):
        total = None
        for plane in (MID + block, MID + block + 1):
            remain = scaled_remain(coeffs, plane, iterate[plane - 1], iterate[plane], iterate[plane + 1], goal)
            remain = (remain * coeffs[7, plane])[mid_y : 2 * mid_y]
            total = remain if total is None else total + remain
        parts.append(total)
    coarse = rows_merge(*parts)
    coarse = lanes_merge(coarse, coarse) * 0.125
    left = iota(TILE, 1) < TILE[1] // 2
    x1 = [iterate[MID + plane, mid_y : 2 * mid_y] for plane in range(mid_x)]
    low_one, low_two = low[0], low[1]
    pairs = count_x // 2
    own = place[0] // 2
    above, below = lax.rem(own + 1, pairs), lax.rem(own + pairs - 1, pairs)
    odd = jnp.logical_not(even)

    def fill(i, carry):
        up, down = i == above, i == below
        edge = jnp.where(up, mid_target[mid_x - 1], mid_target[0])
        edge_left, edge_right = jnp.where(left, coarse, roll(edge, TILE[1] // 2, 1)), jnp.where(left, coarse, edge)
        near_pair = up | down | (i == own)
        for j in range(count_y):
            me = place[1]
            beside = (j == me) | (j == lax.rem(me + 1, count_y)) | (j == lax.rem(me + count_y - 1, count_y))
            far = jnp.logical_not(near_pair & beside)
            one, two = 2 * i * count_y + j, (2 * i + 1) * count_y + j
            slots[one, 0] = edge_left
            slots[two, 0] = edge_right
            for at, tile in ((1, low_one), (2, low_two)):
                slots[one, at] = jnp.where(far | (down & odd), tile, jnp.where(up & even, x1[at + 1], x1[at - 1]))
                slots[two, at] = jnp.where(far | (up & even), tile, jnp.where(down & odd, x1[at - 1], x1[at + 1]))
        return carry

    each(0, pairs, fill)


def low_kernel(count_x, count_y, own_half, near, iterate, gathered, fields, coeffs, update):
    planes, size_y, lanes = iterate.shape
    low_x, low_y = 2 * planes // count_x, size_y // count_y
    low_z = lanes // 2
    me_x, me_y = here()

    def take_all(i, carry):
        for kind in range(3):
            gathered[i, kind] = own_half[i, kind]
        return carry

    each(0, count_x * count_y, take_all)
    for dy in (-1, 0, 1):
        for dx in range(-2, 3):
            source = lax.rem(me_x + dx + count_x, count_x) * count_y + lax.rem(me_y + dy + count_y, count_y)
            for kind in range(2):
                gathered[source, 1 + kind] = near[((dx + 2) * 3 + dy + 1) * 2 + kind]

    left = iota(TILE, 1) < low_z

    def place(i, carry):
        for j in range(count_y):
            one = [gathered[i * count_y + j, kind] for kind in range(3)]
            two = [gathered[(i + count_x // 2) * count_y + j, kind] for kind in range(3)]
            parts = [jnp.where(left, low, roll(high, low_z, 1)) for low, high in zip(one, two)]
            parts += [jnp.where(left, roll(low, low_z, 1), high) for low, high in zip(one[1:], two[1:])]
            for kind, tile in enumerate(parts):
                for plane in range(low_x):
                    fields[kind, i * low_x + plane, j * low_y : (j + 1) * low_y] = tile[
                        plane * low_y : (plane + 1) * low_y
                    ]
        return carry

    each(0, count_x // 2, place)
    lane = iota((size_y, lanes), 1) % low_z
    scale = 0.0625
    weights = chebyshev_weights(COARSE_SWEEPS)

    def next_plane(ref, i, first):
        if isinstance(i, int):
            return roll(first, low_z, 1) if i == planes - 1 else ref[i + 1]
        return jnp.where(i == planes - 1, roll(first, low_z, 1), ref[jnp.minimum(i + 1, planes - 1)])

    def prepare(i, carry):
        goal, yl, diag, zl, xl = (fields[kind, i] for kind in range(5))
        xh = next_plane(fields.at[4], i, fields[4, 0])
        yh = roll(yl, -1, 0)
        zh = jnp.where(lane == low_z - 1, 0.0, roll(zl, -1, 1))
        inverse = 1.0 / (diag + scale * (xl + xh + yl + yh + zl + zh))
        scaled = scale * inverse
        coeffs[0, i] = scaled * xl
        coeffs[1, i] = scaled * xh
        coeffs[2, i] = scaled * yl
        coeffs[3, i] = scaled * yh
        coeffs[4, i] = jnp.where(lane == 0, 0.0, scaled * zl)
        coeffs[5, i] = scaled * zh
        goal = goal * inverse
        coeffs[6, i] = goal
        update[i] = weights[0][1] * goal
        iterate[i] = weights[0][1] * goal
        return carry

    each(0, planes, prepare)
    for pair in weights[1:]:
        start = iterate[0]

        def body(i, carry, pair=pair, start=start):
            below, here = carry
            above = next_plane(iterate, i, start)
            step = pair[1] * scaled_remain(coeffs, i, below, here, above) + pair[0] * update[i]
            update[i] = step
            iterate[i] = here + step
            return here, above

        each(0, planes, body, (roll(iterate[planes - 1], low_z, 1), start))


def fine_coeffs_kernel(fields_own, low_x, high_x, low_y, high_y, first_c, second_c, coeffs, own_windows, side_windows):
    size_x, size_y, size_z = fields_own.shape[1:]
    low_c, high_c = got(first_c, second_c, here()[0] % 2 == 0)
    assemble_owns(own_windows, fields_own, low_y, high_y)
    assemble_sides(side_windows, (size_y, size_z), low_x, high_x, low_c, high_c)
    end = FINE + size_x
    windows = Stack(
        (0, FINE, side_windows, 0), (FINE, end, own_windows, 0), (end, end + FINE, side_windows, FINE)
    )
    fields = [windows.of(field) for field in range(6)]
    scale_coeffs(1.0, *fields[2:], Stack((2, end + 3, coeffs, 0)), (2, end + 3), fields[1])


def window_kernel(own, first_x, second_x, first_y, second_y, first_c, second_c, window):
    size_x, size_y, size_z = own.shape
    place = here()
    even = place[0] % 2 == 0
    low_x, high_x = got(first_x, second_x, even)
    low_y, high_y = got(first_y, second_y, place[1] % 2 == 1)
    low_c, high_c = got(first_c, second_c, even)
    assemble_own(window.at[FINE : FINE + size_x], own, low_y, high_y, 0, 0)
    assemble_side(window, FINE - 4, 4, (size_y, size_z), low_x, 0, low_c, 0, 3, True)
    assemble_side(window, FINE + size_x, 4, (size_y, size_z), high_x, 0, high_c, 0, 3, False)


def last_kernel(
    count_x, count_y, own_half, other_half, low_iterate, mid_coeffs, goal_in, fine_coeffs, window,
    out,
    goal, mid_iterate, mid_update,
    iterate, update,
):
    size_x, size_y, size_z = out.shape
    mid_x, mid_y, mid_z = size_x // 2, size_y // 2, size_z // 2
    last = size_x + 2 * FINE - 2
    coeffs = Stack((2, last, fine_coeffs, 0))
    me_x, me_y = here()
    even = me_x % 2 == 0

    def half(which, device, tile):
        one, two = own_half[device, tile], other_half[device, tile]
        return jnp.where(even, one, two) if which == 0 else jnp.where(even, two, one)

    def device(dx, dy):
        return lax.rem(me_x + dx + count_x, count_x) * count_y + lax.rem(me_y + dy + count_y, count_y)

    first, far = MID - mid_x, MID + 2 * mid_x
    for dy in (-1, 0, 1):
        rows = slice((dy + 1) * mid_y, (dy + 2) * mid_y)
        for dx in (-1, 0, 1):
            source = device(dx, dy)
            start = MID + dx * mid_x
            for plane in range(mid_x):
                mid_iterate[start + plane, rows] = half(plane // 2, source, 1 + plane % 2)
        for plane in range(2):
            mid_iterate[plane, rows] = own_half[device(-2, dy), 1 + plane]
            mid_iterate[far + plane, rows] = own_half[device(2, dy), 1 + plane]
    low_planes, low_size_y = low_iterate.shape[:2]
    low_size_x = 2 * low_planes
    low_y = mid_y // 2
    turn = lax.rem(low_size_y - me_y * low_y + low_y, low_size_y)
    for plane in range((mid_x + 2 * MID) // 2):
        at = lax.rem(me_x * (mid_x // 2) - MID // 2 + plane + low_size_x, low_size_x)
        turned = pltpu.roll(low_iterate[lax.rem(at, low_planes)], turn, 0)
        side = at // low_planes
        one, two = lanes_spread(turned[: TILE[0]], side), lanes_spread(turned[TILE[0] : 2 * TILE[0]], side)
        part = jnp.concatenate([rows_spread(one, 0), rows_spread(one, 1), rows_spread(two, 0)], axis=0)
        mid_iterate[2 * plane] += part
        mid_iterate[2 * plane + 1] += part

    left = iota(TILE, 1) < TILE[1] // 2
    for plane in range(first, far):
        goal[plane] = goal_in[plane]
    for dy in (-1, 0, 1):
        rows = slice((dy + 1) * mid_y, (dy + 2) * mid_y)
        for plane, dx in ((first - 1, -2), (far, 2)):
            source = device(dx, dy)
            edge = jnp.where(left, roll(half(0, source, 0), TILE[1] // 2, 1), half(1, source, 0))
            goal[plane, rows] = edge * mid_coeffs[6, plane, rows]
    for sweep, pair in enumerate(chebyshev_weights(SWEEPS)):
        sweep_window(
            mid_iterate, mid_update, mid_coeffs, (first - 1 + sweep, far + 1 - sweep), pair, sweep == 0, goal
        )

    fine_low = FINE - 4
    for plane in range(mid_x + 4):
        turned = roll(mid_iterate[MID - 2 + plane], -4, 0)
        lines = []
        for r in range(2):
            tile = turned[r * TILE[0] : (r + 1) * TILE[0]]
            for side in range(2):
                line = rows_spread(tile, side)
                lines.append(jnp.concatenate([lanes_spread(line, 0), lanes_spread(line, 1)], axis=1))
        part = jnp.concatenate(lines, axis=0)
        for at in (fine_low + 2 * plane, fine_low + 2 * plane + 1):
            iterate[at] = window[at] + part
    for sweep, pair in enumerate(chebyshev_weights(SWEEPS)):
        sweep_window(
            iterate, update, coeffs, (2 + sweep, last - sweep), pair, sweep == 0
        )
    for plane in range(size_x):
        out[plane] = iterate[FINE + plane, PAD : PAD + size_y]


def call(kernel, inputs, outs, scratch=(), scalars=0, far_in=(), far_out=(), sems=0):
    def place(i):
        return pltpu.SMEM if i < scalars else pltpu.HBM if i in far_in else pltpu.VMEM

    near = [x.shape for i, x in enumerate(inputs) if i >= scalars and i not in far_in]
    near += [shape for i, shape in enumerate(outs) if i not in far_out] + list(scratch)
    used = 4 * sum(math.prod(shape) for shape in near)
    inputs = [pltpu.with_memory_space_constraint(x, pltpu.HBM) if i in far_in else x for i, x in enumerate(inputs)]
    return pl.pallas_call(
        kernel,
        out_shape=[
            pltpu.HBM(shape, F32) if i in far_out else jax.ShapeDtypeStruct(shape, F32)
            for i, shape in enumerate(outs)
        ],
        in_specs=[pl.BlockSpec(memory_space=place(i)) for i in range(len(inputs))],
        out_specs=[
            pl.BlockSpec(memory_space=pltpu.HBM if i in far_out else pltpu.VMEM) for i in range(len(outs))
        ],
        scratch_shapes=[pltpu.VMEM(shape, F32) for shape in scratch]
        + ([pltpu.SemaphoreType.DMA((sems,))] if sems > 1 else [pltpu.SemaphoreType.DMA] * sems),
        cost_estimate=pl.CostEstimate(flops=1000, bytes_accessed=1000, transcendentals=0),
        compiler_params=pltpu.CompilerParams(vmem_limit_bytes=used + used // 4 + 2 * 1024 * 1024),
    )(*inputs)


def local(source, initial, absorption, beta_x, beta_y, beta_z):
    size_x, size_y, size_z = source.shape
    mid_x, mid_y, mid_z = size_x // 2, size_y // 2, size_z // 2
    low_x, low_y = mid_x // 2, mid_y // 2
    count_x, count_y = lax.axis_size("gx"), lax.axis_size("gy")
    devices = count_x * count_y
    plane, strip = tiles_of(size_y, size_z), tiles_of(8, size_z)
    mids = 4 * mid_x

    def tiles(count):
        return (count,) + TILE

    pairs = size_x // 2
    up_x, down_x, up_y, down_y, mid, low, own = call(
        pack_kernel,
        (initial, source, absorption, beta_x, beta_y, beta_z),
        [
            tiles(sum(UP_PLANES) * plane),
            tiles(sum(DOWN_PLANES) * plane),
            tiles((6 * pairs + 1) * strip + 2 + 4 * STRIP),
            tiles((6 * pairs + 2) * strip + 2 + 4 * STRIP),
            tiles(mids),
            tiles(2),
            (6,) + source.shape,
        ],
        far_in=range(6),
        sems=6,
    )
    low_x1, high_x1 = shifted(up_x, "gx", 1), shifted(down_x, "gx", -1)
    low_y1, high_y1 = shifted(up_y, "gy", 1), shifted(down_y, "gy", -1)
    first_c1, second_c1 = call(
        functools.partial(corner_kernel, size_x, size_z),
        (low_y1, high_y1, mid, low),
        [tiles(corner_tiles(DOWN_CORNER) * strip + 16)] * 2,
    )
    first_c1, second_c1 = swapped(first_c1, second_c1, "gx")

    tall = (size_y + 2 * PAD, size_z)
    wide = (size_x + 2 * FINE,) + tall
    own_windows, own_coeffs, up_corner, down_corner, strips = call(
        own_kernel,
        (own, low_y1, high_y1),
        [(6, size_x) + tall, (8, size_x - 1) + tall, tiles(MID_CORNER), tiles(MID_CORNER), tiles(2 * mids)],
    )
    iterate, mid_target, first_x2, second_x2, first_y2, second_y2 = call(
        fine_kernel,
        (own_windows, own_coeffs, up_corner, down_corner, mid, low_x1, high_x1, first_c1, second_c1),
        [
            source.shape,
            (mid_x, mid_y, mid_z),
            tiles(4 * plane + mid_x + MID_CORNER + mids + 10 + PASSED),
            tiles(4 * plane + mid_x + MID_CORNER + mids + 10 + PASSED),
            tiles(pairs * strip + mid_x),
            tiles(pairs * strip + mid_x),
        ],
        scratch=[(6, 2 * FINE) + tall, (8, 2 * FINE + 1) + tall, wide, wide],
    )
    first_x2, second_x2 = swapped(first_x2, second_x2, "gx")
    first_y2, second_y2 = swapped(first_y2, second_y2, "gy")
    first_c2, second_c2 = call(
        functools.partial(corner_two_kernel, size_x, size_z),
        (first_y2, second_y2),
        [tiles(2 * strip + 2 * mid_x)] * 2,
    )
    first_c2, second_c2 = swapped(first_c2, second_c2, "gx")

    mid_wide = (mid_x + 2 * MID, 3 * mid_y, mid_z)
    mid_coeffs, near = call(
        mid_coeffs_kernel,
        (mid, low, strips, low_y1, high_y1, first_c1, second_c1, first_x2, second_x2),
        [(8,) + mid_wide, tiles(30)],
        [(4,) + mid_wide],
    )
    (coeffs,) = call(
        fine_coeffs_kernel,
        (own, low_x1, high_x1, low_y1, high_y1, first_c1, second_c1),
        [(7, wide[0] - 4) + tall],
        [(6, size_x) + tall, (6, 2 * FINE) + tall],
    )
    goal, slots = call(
        functools.partial(mid_kernel, count_x, count_y),
        (low, mid_target, mid_coeffs, first_x2, second_x2, first_y2, second_y2, first_c2, second_c2, coeffs),
        [mid_wide, (devices, 3) + TILE],
        [mid_wide] * 3,
    )
    own_half = lax.all_to_all(slots, ("gx", "gy"), 0, 0)
    other_half = lax.ppermute(own_half, "gx", [(i, i ^ 1) for i in range(count_x)])

    (window,) = call(
        window_kernel, (iterate, first_x2, second_x2, first_y2, second_y2, first_c2, second_c2), [wide]
    )
    low_wide = (low_x * count_x // 2, low_y * count_y, mid_z)
    (low_iterate,) = call(
        functools.partial(low_kernel, count_x, count_y),
        (own_half, near),
        [low_wide],
        [(devices, 3) + TILE, (5,) + low_wide, (7,) + low_wide, low_wide],
    )
    (result,) = call(
        functools.partial(last_kernel, count_x, count_y),
        (own_half, other_half, low_iterate, mid_coeffs, goal, coeffs, window),
        [source.shape],
        [mid_wide, mid_wide, mid_wide]
        + [wide, wide],
    )
    return result


def solution(mesh):
    spec = P("gx", "gy", None)
    return jax.shard_map(
        local, mesh=mesh, in_specs=(spec,) * 6, out_specs=spec, check_vma=False
    )
```

```python
import functools
import math

import jax
import jax.numpy as jnp
from jax import lax
from jax.experimental import pallas as pl
from jax.experimental.pallas import tpu as pltpu
from jax.sharding import PartitionSpec as P

SWEEPS = 4
COARSE_SWEEPS = 8
F32 = jnp.float32
TILE = (8, 128)
PAD = 8
FINE = 5
MID = 6


def chebyshev_weights(sweeps):
    cheb_theta = 1.125
    cheb_delta = 0.875
    cheb_sigma = cheb_theta / cheb_delta
    rho_old = 1.0 / cheb_sigma
    weights = [(0.0, 1.0 / cheb_theta)]
    for sweep in range(1, sweeps):
        rho_new = 1.0 / (2.0 * cheb_sigma - rho_old)
        weights.append((rho_new * rho_old, 2.0 * rho_new / cheb_delta))
        rho_old = rho_new
    return weights


def iota(shape, axis):
    return lax.broadcasted_iota(jnp.int32, shape, axis)


def roll(value, shift, axis):
    return pltpu.roll(value, shift % value.shape[axis], axis)


def take(tile, index, axis):
    return jnp.take_along_axis(tile, index, axis=axis, mode="promise_in_bounds")


def rows_spread(tile, half):
    return take(tile, iota(TILE, 0) // 2 + 4 * half, 0)


def lanes_spread(tile, half):
    return take(tile, iota(TILE, 1) // 2 + 64 * half, 1)


def rows_merge(one, two, pairs=True):
    row = iota(TILE, 0)
    if pairs:
        one, two = one + roll(one, -1, 0), two + roll(two, -1, 0)
    index = (2 * row) % TILE[0]
    return jnp.where(row < TILE[0] // 2, take(one, index, 0), take(two, index, 0))


def lanes_merge(one, two, pairs=True):
    lane = iota(TILE, 1)
    if pairs:
        one, two = one + roll(one, -1, 1), two + roll(two, -1, 1)
    index = (2 * lane) % TILE[1]
    return jnp.where(lane < TILE[1] // 2, take(one, index, 1), take(two, index, 1))


def merge(plane, row_pairs=True, lane_pairs=True):
    halves = []
    for side in range(2):
        lanes = slice(side * TILE[1], (side + 1) * TILE[1])
        halves.append(rows_merge(plane[: TILE[0], lanes], plane[TILE[0] :, lanes], row_pairs))
    return lanes_merge(*halves, lane_pairs)


def each(start, stop, body, carry=0):
    if stop - start > 20:
        return lax.fori_loop(start, stop, body, carry, unroll=2)
    for i in range(start, stop):
        carry = body(i, carry)
    return carry


def here():
    return lax.axis_index("gx"), lax.axis_index("gy")


class Writer:
    def __init__(self, ref):
        self.ref, self.at = ref, 0

    def put(self, value):
        rows, columns = value.shape
        for r in range(0, rows, TILE[0]):
            for c in range(0, columns, TILE[1]):
                self.ref[self.at] = value[r : r + TILE[0], c : c + TILE[1]]
                self.at += 1


class Tiles:
    def __init__(self):
        self.tiles = []

    def put(self, value):
        rows, columns = value.shape
        for r in range(0, rows, TILE[0]):
            for c in range(0, columns, TILE[1]):
                self.tiles.append(value[r : r + TILE[0], c : c + TILE[1]])


def send(first, second, odd, up, down):
    for at, (one, two) in enumerate(zip(up.tiles, down.tiles, strict=True)):
        first[at] = jnp.where(odd, one, two)
        second[at] = jnp.where(odd, two, one)


class Got:
    def __init__(self, first, second, even, low):
        self.refs = (second, first) if low else (first, second)
        self.even, self.shape = even, first.shape

    def __getitem__(self, at):
        return jnp.where(self.even, self.refs[0][at], self.refs[1][at])


def got(first, second, even):
    return Got(first, second, even, True), Got(first, second, even, False)


class Reader:
    def __init__(self, ref, at=0):
        self.ref, self.at = ref, at

    def get(self, rows, columns):
        lines = []
        for _ in range(rows // TILE[0]):
            parts = []
            for _ in range(columns // TILE[1]):
                parts.append(self.ref[self.at])
                self.at += 1
            lines.append(parts[0] if len(parts) == 1 else jnp.concatenate(parts, axis=1))
        return lines[0] if len(lines) == 1 else jnp.concatenate(lines, axis=0)


UP_PLANES = (5, 4, 4, 4, 4, 4)
DOWN_PLANES = (5, 4, 4, 5, 4, 4)
UP_CORNER = (4, 3, 3, 3, 4, 3)
DOWN_CORNER = (4, 3, 3, 4, 4, 3)
STRIP = 2


def corner_tiles(counts):
    return sum(count - 1 for count in counts)


def tiles_of(rows, columns):
    return (rows // TILE[0]) * (columns // TILE[1])


def is_upper(width):
    return iota((TILE[0], width), 0) < TILE[0] // 2


def swapped(first, second, axis):
    count = lax.axis_size(axis)
    outer = [(i, (i + 1 if i % 2 else i - 1) % count) for i in range(count)]
    inner = [(i, i ^ 1) for i in range(count)]
    return lax.ppermute(first, axis, outer), lax.ppermute(second, axis, inner)


def shifted(value, axis, step):
    count = lax.axis_size(axis)
    return lax.ppermute(value, axis, [(i, (i + step) % count) for i in range(count)])


def pack_kernel(
    ini_in, src_in, absorb_in, face_x_in, face_y_in, face_z_in,
    up_x, down_x, up_y, down_y, mid, low, own, sems,
):
    copies = []
    for field, ref in enumerate((ini_in, src_in, absorb_in, face_x_in, face_y_in, face_z_in)):
        copies.append(pltpu.make_async_copy(ref, own.at[field], sems.at[field]))
        copies[-1].start()
    for copy in copies:
        copy.wait()
    fields = tuple(own.at[field] for field in range(6))
    ini, src, absorb, face_x, face_y, face_z = fields
    size_x, size_y, size_z = ini.shape
    mid_x = size_x // 2
    for block in range(mid_x):
        one, two = 2 * block, 2 * block + 1
        mid[block] = merge(absorb[one] + absorb[two]) * 0.125
        mid[mid_x + block] = merge(face_x[one]) * 0.25
        mid[2 * mid_x + block] = merge(face_y[one] + face_y[two], row_pairs=False) * 0.25
        mid[3 * mid_x + block] = merge(face_z[one] + face_z[two], lane_pairs=False) * 0.25

    def coarser(array, planes, row_pairs=True, lane_pairs=True):
        parts = []
        for block in range(0, mid_x, 2):
            total = None
            for plane in range(planes):
                part = mid[array * mid_x + block + plane]
                total = part if total is None else total + part
            parts.append(total)
        tile = rows_merge(*parts, row_pairs)
        return lanes_merge(tile, tile, lane_pairs)

    left = iota(TILE, 1) < TILE[1] // 2
    low[0] = jnp.where(left, coarser(2, 2, row_pairs=False), coarser(3, 2, lane_pairs=False)) * 0.25
    low[1] = jnp.where(left, coarser(0, 2) * 0.125, coarser(1, 1) * 0.25)

    tops, bottoms = Writer(up_x), Writer(down_x)
    for ref, count in zip(fields, UP_PLANES):
        for plane in range(size_x - count, size_x):
            tops.put(ref[plane])
    for ref, count in zip(fields, DOWN_PLANES):
        for plane in range(count):
            bottoms.put(ref[plane])

    upper = is_upper(size_z)
    tops_y, bottoms_y = Writer(up_y), Writer(down_y)
    for ref in fields:
        for pair in range(0, size_x, 2):
            one, two = ref[pair], ref[pair + 1]
            tops_y.put(jnp.where(upper, roll(one[size_y - 8 :], 4, 0), two[size_y - 8 :]))
            bottoms_y.put(jnp.where(upper, one[:8], roll(two[:8], 4, 0)))
    tops_y.put(ini[:, size_y - 5, :])
    bottoms_y.put(ini[:, 4, :])
    bottoms_y.put(face_y[:, 4, :])
    for writer in (tops_y, bottoms_y):
        for tile in range(2):
            writer.put(low[tile])
    upper = is_upper(TILE[1])
    for array in range(4):
        for pair in range(0, mid_x, 2):
            one, two = mid[array * mid_x + pair], mid[array * mid_x + pair + 1]
            for writer in (tops_y, bottoms_y):
                writer.put(jnp.where(upper, roll(one, -2, 0), roll(two, 2, 0)))


def corner_of(low_y, high_y, plane, upper, first_tile=0):
    width = upper.shape[1]
    at = first_tile + (plane // 2) * tiles_of(8, width)
    low = Reader(low_y, at).get(8, width)
    high = Reader(high_y, at).get(8, width)
    if plane % 2 == 0:
        return jnp.where(upper, low, roll(high, 4, 0))
    return jnp.where(upper, roll(low, 4, 0), high)


def mix(near, far):
    row = iota(near.shape, 0)
    return jnp.where((row >= 2) & (row < 6), near, roll(far, 3, 0))


def put_corners(writer, low_y, high_y, planes, upper, first_tile):
    parts = [corner_of(low_y, high_y, plane, upper, first_tile) for plane in planes]
    for part in parts[:-2]:
        writer.put(part)
    writer.put(mix(*parts[-2:]))


def mid_beside(ref, array, plane, low):
    pairs = (ref.shape[0] - 4 * STRIP - 2) // 12
    at = ((2 + array) * pairs + plane) * 2
    halves = []
    for side in range(2):
        total = ref[at + side]
        if array != 1:
            total = total + roll(total, 4, 0)
        if array != 2:
            total = total + roll(total, -1, 0)
        halves.append(take(total, (2 * iota(TILE, 0) + (4 if low else 0)) % TILE[0], 0))
    return lanes_merge(*halves, array != 3) * (0.125 if array == 0 else 0.25)


def mid_strip(ref, array, plane, low):
    far = roll(ref[ref.shape[0] - 4 * STRIP + array * STRIP + plane // 2], 2 if plane % 2 == 0 else -2, 0)
    row = iota(TILE, 0)
    return jnp.where((row >= 2) & (row < 6), far, mid_beside(ref, array, plane, low))


def corner_kernel(size_x, size_z, low_y, high_y, mid, low_faces, first, second):
    place = here()
    upper = is_upper(size_z)
    per_field = (size_x // 2) * tiles_of(8, size_z)
    tops, bottoms = Tiles(), Tiles()
    for field in range(6):
        start = field * per_field
        planes = [size_x - 1 - plane for plane in range(UP_CORNER[field])]
        put_corners(tops, low_y, high_y, planes, upper, start)
        put_corners(bottoms, low_y, high_y, range(DOWN_CORNER[field]), upper, start)
    mid_x = size_x // 2
    upper = is_upper(TILE[1])
    for _ in range(len(bottoms.tiles) - len(tops.tiles)):
        tops.put(low_faces[0])
    for writer, near, next_plane in ((tops, mid_x - 1, mid_x - 2), (bottoms, 0, 1)):
        wanted = [(array, near) for array in range(4)] + [(1, next_plane)]
        for array, plane in wanted:
            writer.put(
                jnp.where(upper, mid_beside(high_y, array, plane, False), mid_beside(low_y, array, plane, True))
            )
        for array, plane in wanted:
            writer.put(mid[array * mid_x + plane])
        for tiles in ((low_faces[0], low_faces[1]), low_tiles_of(low_y), low_tiles_of(high_y)):
            for tile in tiles:
                writer.put(tile)
    send(first, second, place[0] % 2 == 1, tops, bottoms)


def low_tiles_of(ref):
    end = ref.shape[0] - 4 * STRIP
    return ref[end - 2], ref[end - 1]


class Planes:
    def __init__(self, *parts):
        self.parts = parts
        self.shape = parts[0][2].shape

    def find(self, i):
        for start, stop, ref, offset, lead in self.parts:
            if start <= i < stop:
                return ref, lead + (i - start + offset,)
        raise IndexError(i)

    def __getitem__(self, i):
        ref, index = self.find(i)
        return ref[index]


class Stack:
    def __init__(self, *parts):
        self.parts = parts

    def of(self, kind):
        return Planes(*((a, b, ref, offset, (kind,)) for a, b, ref, offset in self.parts))

    def __getitem__(self, index):
        return self.of(index[0])[index[1]]

    def __setitem__(self, index, value):
        ref, place = self.of(index[0]).find(index[1])
        ref[place] = value


def scale_coeffs(scale, absorb, face_x, face_y, face_z, coeffs, planes, target=None, diagonal=None):
    rows, lanes = absorb.shape[-2:]
    lane = iota((rows, lanes), 1)

    def body(i, carry):
        xl, xh = face_x[i], face_x[i + 1]
        yl, zl = face_y[i], face_z[i]
        yh = roll(yl, -1, 0)
        zh = jnp.where(lane == lanes - 1, 0.0, roll(zl, -1, 1))
        diag = absorb[i] + scale * (xl + xh + yl + yh + zl + zh)
        inverse = 1.0 / diag
        scaled = scale * inverse
        coeffs[0, i] = scaled * xl
        coeffs[1, i] = scaled * xh
        coeffs[2, i] = scaled * yl
        coeffs[3, i] = scaled * yh
        coeffs[4, i] = jnp.where(lane == 0, 0.0, scaled * zl)
        coeffs[5, i] = scaled * zh
        if target is not None:
            coeffs[6, i] = target[i] * inverse
        else:
            coeffs[6, i] = inverse
        if diagonal is not None:
            coeffs[7, i] = diag
        return carry

    each(*planes, body)


def scaled_remain(coeffs, i, below, here, above, goal=None):
    along_z = coeffs[4, i] * roll(here, 1, 1) + coeffs[5, i] * roll(here, -1, 1)
    along_y = coeffs[2, i] * roll(here, 1, 0) + coeffs[3, i] * roll(here, -1, 0)
    along_x = coeffs[0, i] * below + coeffs[1, i] * above
    return ((coeffs[6, i] if goal is None else goal[i]) - here + along_x) + (along_y + along_z)


def sweep_window(iterate, update, coeffs, planes, pair, first, goal=None, source=None):
    start, stop = planes
    source = iterate if source is None else source

    def body(i, carry):
        below, here = carry
        above = source[i + 1]
        step = pair[1] * scaled_remain(coeffs, i, below, here, above, goal)
        if not first:
            step = step + pair[0] * update[i]
        update[i] = step
        iterate[i] = here + step
        return here, above

    each(start, stop, body, (source[start - 1], source[start]))


def assemble_own(window, own, low_y, high_y, low_start, high_start):
    size_x, size_y, size_z = own.shape
    high = PAD + size_y
    low_reader, high_reader = Reader(low_y, low_start), Reader(high_y, high_start)
    for pair in range(0, size_x, 2):
        window[pair, PAD:high] = own[pair]
        window[pair + 1, PAD:high] = own[pair + 1]
        tile = low_reader.get(8, size_z)
        window[pair, 0:8] = roll(tile, 4, 0)
        window[pair + 1, 0:8] = tile
        tile = high_reader.get(8, size_z)
        window[pair, high : high + 8] = tile
        window[pair + 1, high : high + 8] = roll(tile, 4, 0)


def assemble_side(window, first, count, rows, planes, plane_start, corners, corner_start, corner_count, from_end):
    size_y, size_z = rows
    high = PAD + size_y
    reader = Reader(planes, plane_start)
    for plane in range(count):
        window[first + plane, PAD:high] = reader.get(size_y, size_z)
    reader = Reader(corners, corner_start)
    tiles = [roll(reader.get(8, size_z), 4, 0) for _ in range(corner_count - 1)]
    tiles.append(roll(tiles[-1], -3, 0))
    for plane, tile in enumerate(tiles):
        at = first + count - 1 - plane if from_end else first + plane
        window[at, 0:8] = tile
        window[at, high : high + 8] = tile


def assemble_owns(windows, own, low_y, high_y):
    size_x, size_y, size_z = own.shape[1:]
    per_field = (size_x // 2) * tiles_of(8, size_z)
    for field in range(6):
        assemble_own(windows.at[field], own.at[field], low_y, high_y, field * per_field, field * per_field)
    low_line = Reader(low_y, 6 * per_field).get(8, size_z)
    high_reader = Reader(high_y, 6 * per_field)
    high_line = high_reader.get(8, size_z)
    face_line = high_reader.get(8, size_z)
    high = PAD + size_y
    for plane in range(size_x):
        windows[0, plane, 3:4] = low_line[plane : plane + 1]
        windows[0, plane, high + 4 : high + 5] = high_line[plane : plane + 1]
        windows[4, plane, high + 4 : high + 5] = face_line[plane : plane + 1]


def assemble_sides(side_windows, rows, low_x, high_x, low_c, high_c):
    plane_tiles, strip_tiles = tiles_of(*rows), tiles_of(8, rows[1])
    starts = [0] * 4
    for field in range(6):
        up, down, up_c, down_c = (
            kinds[field] for kinds in (UP_PLANES, DOWN_PLANES, UP_CORNER, DOWN_CORNER)
        )
        window = side_windows.at[field]
        assemble_side(
            window, FINE - up, up, rows, low_x, starts[0], low_c, starts[2], up_c, True
        )
        assemble_side(
            window, FINE, down, rows, high_x, starts[1], high_c, starts[3], down_c, False
        )
        starts[0] += up * plane_tiles
        starts[1] += down * plane_tiles
        starts[2] += (up_c - 1) * strip_tiles
        starts[3] += (down_c - 1) * strip_tiles


def own_kernel(own, low_y, high_y, windows, coeffs, up_corner, down_corner, strips):
    assemble_owns(windows, own, low_y, high_y)
    fields = [windows.at[field] for field in range(6)]
    scale_coeffs(1.0, *fields[2:], coeffs, (0, own.shape[1] - 1), fields[1], True)
    mid_x = own.shape[1] // 2
    tops, bottoms = Writer(up_corner), Writer(down_corner)
    upper = is_upper(TILE[1])
    for side, (ref, low) in enumerate(((low_y, True), (high_y, False))):
        for array in range(4):
            for plane in range(mid_x):
                strips[(side * 4 + array) * mid_x + plane] = mid_strip(ref, array, plane, low)
    for writer, first, step in ((tops, mid_x - 1, -1), (bottoms, 0, 1)):
        for array in range(4):
            for q in range(2):
                for side in range(2):
                    writer.put(strips[(side * 4 + array) * mid_x + first + q * step])
        for array in range(4):
            for q in range(2, 4):
                one, two = (roll(strips[(side * 4 + array) * mid_x + first + q * step], 4, 0) for side in range(2))
                writer.put(jnp.where(upper, one, two))


def fine_kernel(
    own_windows, own_coeffs, up_corner, down_corner, mid, low_x, high_x, first_c, second_c,
    iterate_out, mid_target, first_x, second_x, first_y, second_y,
    side_windows, side_coeffs, iterate, update,
):
    size_x, size_z = own_windows.shape[1], own_windows.shape[3]
    size_y = own_windows.shape[2] - 2 * PAD
    place = here()
    odd = place[0] % 2 == 1
    low_c, high_c = got(first_c, second_c, odd)
    assemble_sides(side_windows, (size_y, size_z), low_x, high_x, low_c, high_c)
    end = FINE + size_x
    last = end + FINE - 1
    windows = Stack(
        (0, FINE, side_windows, 0), (FINE, end, own_windows, 0), (end, last + 1, side_windows, FINE)
    )
    coeffs = Stack(
        (0, FINE, side_coeffs, 0), (FINE, end - 1, own_coeffs, 0), (end - 1, last + 1, side_coeffs, FINE)
    )
    fields = [windows.of(field) for field in range(6)]
    scale_coeffs(1.0, *fields[2:], coeffs, (1, FINE), fields[1], True)
    scale_coeffs(1.0, *fields[2:], coeffs, (end - 1, last), fields[1], True)
    for sweep, pair in enumerate(chebyshev_weights(SWEEPS)):
        sweep_window(
            iterate, update, coeffs, (1 + sweep, last - sweep), pair, sweep == 0,
            source=fields[0] if sweep == 0 else None,
        )
    mid_x, mid_y = size_x // 2, size_y // 2
    coarse = []
    for block in range(mid_x):
        total = None
        for plane in (FINE + 2 * block, FINE + 2 * block + 1):
            remain = scaled_remain(coeffs, plane, iterate[plane - 1], iterate[plane], iterate[plane + 1])
            remain = (remain * coeffs[7, plane])[PAD : PAD + size_y]
            total = remain if total is None else total + remain
        coarse.append(merge(total) * 0.125)
        mid_target[block] = coarse[block]
    for plane in range(size_x):
        iterate_out[plane] = iterate[FINE + plane, PAD : PAD + size_y]

    tops, bottoms = Tiles(), Tiles()
    for plane in range(size_x - 4, size_x):
        tops.put(iterate_out[plane])
    for plane in range(4):
        bottoms.put(iterate_out[plane])
    upper = is_upper(size_z)
    tops_y, bottoms_y = Tiles(), Tiles()
    for pair in range(0, size_x, 2):
        one, two = iterate_out[pair], iterate_out[pair + 1]
        tops_y.put(jnp.where(upper, roll(one[size_y - 8 :], 4, 0), two[size_y - 8 :]))
        bottoms_y.put(jnp.where(upper, one[:8], roll(two[:8], 4, 0)))
    for writer in (tops, bottoms, tops_y, bottoms_y):
        for tile in coarse:
            writer.put(tile)
    for writer, ref in ((tops, up_corner), (bottoms, down_corner)):
        for tile in range(MID_CORNER):
            writer.put(ref[tile])
    for writer in (tops, bottoms):
        for tile in range(mid.shape[0]):
            writer.put(mid[tile])
    for writer, corners in ((tops, low_c), (bottoms, high_c)):
        for tile in range(corners.shape[0] - PASSED - 10, corners.shape[0]):
            writer.put(corners[tile])
    send(first_x, second_x, odd, tops, bottoms)
    send(first_y, second_y, place[1] % 2 == 1, tops_y, bottoms_y)


MID_CORNER = 24
PASSED = 6


def whole_corner(ref, start, array, q, side):
    return ref[start + (array * 2 + q) * 2 + side]


def part_corner(ref, start, array, q):
    return ref[start + 16 + array * 2 + q - 2]


def corner_two_kernel(size_x, size_z, first_y, second_y, first, second):
    place = here()
    upper = is_upper(size_z)
    low_y, high_y = got(first_y, second_y, place[1] % 2 == 1)
    tops, bottoms = Tiles(), Tiles()
    put_corners(tops, low_y, high_y, [size_x - 1, size_x - 2, size_x - 3], upper, 0)
    put_corners(bottoms, low_y, high_y, range(3), upper, 0)
    for writer in (tops, bottoms):
        for ref in (low_y, high_y):
            for tile in range(ref.shape[0] - size_x // 2, ref.shape[0]):
                writer.put(ref[tile])
    send(first, second, place[0] % 2 == 1, tops, bottoms)


def level_two_near(near, low, low_y, high_y, low_c, high_c, low_x2, high_x2):
    known = {(0, 0): (low[0], low[1]), (0, -1): low_tiles_of(low_y), (0, 1): low_tiles_of(high_y)}
    for step, ref, distance in ((-1, low_c, 1), (1, high_c, 1), (-1, low_x2, 2), (1, high_x2, 2)):
        start = ref.shape[0] - PASSED
        for at, dy in enumerate((0, -1, 1)):
            known[step * distance, dy] = (ref[start + 2 * at], ref[start + 2 * at + 1])
    for (dx, dy), tiles in known.items():
        for kind in range(2):
            near[((dx + 2) * 3 + dy + 1) * 2 + kind] = tiles[kind]


def mid_coeffs_kernel(
    mid, low, strips, low_y, high_y, first_c, second_c, first_x2, second_x2, coeffs, near, window
):
    place = here()
    low_x2, high_x2 = got(first_x2, second_x2, place[0] % 2 == 1)
    low_c, high_c = got(first_c, second_c, place[0] % 2 == 1)
    level_two_near(near, low, low_y, high_y, low_c, high_c, low_x2, high_x2)
    mid_y, mid_z = mid.shape[1:]
    mid_x = mid.shape[0] // 4
    mids = 4 * mid_x
    first = MID - mid_x
    corner = 4 * tiles_of(2 * mid_y, 2 * mid_z) + mid_x
    passed = corner + MID_CORNER
    for ref, start, block in ((low_x2, passed, 0), (mid, 0, 1), (high_x2, passed, 2)):
        for array in range(4):
            for plane in range(mid_x):
                window[array, first + block * mid_x + plane, mid_y : 2 * mid_y] = ref[start + array * mid_x + plane]
    for array in range(4):
        for plane in range(mid_x):
            window[array, MID + plane, :mid_y] = strips[array * mid_x + plane]
            window[array, MID + plane, 2 * mid_y :] = strips[(4 + array) * mid_x + plane]
    passed += mids
    far = 3 * mid_x + first
    for ref, start, step, end in ((low_x2, MID - 1, -1, first - 1), (high_x2, MID + mid_x, 1, far)):
        for array in range(4):
            for q in range(mid_x):
                if q < 2:
                    one, two = (whole_corner(ref, corner, array, q, side) for side in range(2))
                else:
                    one = two = roll(part_corner(ref, corner, array, q), 4, 0)
                window[array, start + q * step, :mid_y] = one
                window[array, start + q * step, 2 * mid_y :] = two
        for at in range(5):
            array, plane = (at, end) if at < 4 else (1, end + step)
            window[array, plane, :mid_y] = ref[passed + at]
            window[array, plane, 2 * mid_y :] = ref[passed + at]
            window[array, plane, mid_y : 2 * mid_y] = ref[passed + 5 + at]
    scale_coeffs(0.25, *(window.at[array] for array in range(4)), coeffs, (first - 1, far + 1), None, True)


def mid_kernel(
    count_x, count_y, low, mid_target, coeffs, first_x2, second_x2, first_y2, second_y2, first_c2, second_c2, unused,
    goal, slots, target, iterate, update,
):
    mid_x, mid_y, mid_z = mid_target.shape
    first = MID - mid_x
    far = 3 * mid_x + first
    fine_tiles = 4 * tiles_of(2 * mid_y, 2 * mid_z)
    place = here()
    even = place[0] % 2 == 0
    odd = place[0] % 2 == 1
    low_x2, high_x2 = got(first_x2, second_x2, odd)
    low_y2, high_y2 = got(first_y2, second_y2, place[1] % 2 == 1)
    low_c2, high_c2 = got(first_c2, second_c2, odd)
    blocks = {
        (0, 0): (low_c2, low_c2.shape[0] - 2 * mid_x), (0, 1): (low_x2, fine_tiles),
        (0, 2): (low_c2, low_c2.shape[0] - mid_x), (1, 0): (low_y2, low_y2.shape[0] - mid_x),
        (1, 2): (high_y2, high_y2.shape[0] - mid_x),
        (2, 0): (high_c2, high_c2.shape[0] - 2 * mid_x), (2, 1): (high_x2, fine_tiles),
        (2, 2): (high_c2, high_c2.shape[0] - mid_x),
    }
    for plane in range(mid_x):
        target[MID + plane, mid_y : 2 * mid_y] = mid_target[plane]
    for (bx, by), (ref, start) in blocks.items():
        for plane in range(mid_x):
            target[first + bx * mid_x + plane, by * mid_y : (by + 1) * mid_y] = ref[start + plane]

    weights = chebyshev_weights(SWEEPS)

    def start_sweep(i, carry):
        value = target[i] * coeffs[6, i]
        goal[i] = value
        update[i] = weights[0][1] * value
        iterate[i] = weights[0][1] * value
        return carry

    each(first, far, start_sweep)
    for sweep in range(1, SWEEPS):
        sweep_window(iterate, update, coeffs, (first + sweep, far - sweep), weights[sweep], False, goal)
    parts = []
    for block in range(0, mid_x, 2):
        total = None
        for plane in (MID + block, MID + block + 1):
            remain = scaled_remain(coeffs, plane, iterate[plane - 1], iterate[plane], iterate[plane + 1], goal)
            remain = (remain * coeffs[7, plane])[mid_y : 2 * mid_y]
            total = remain if total is None else total + remain
        parts.append(total)
    coarse = rows_merge(*parts)
    coarse = lanes_merge(coarse, coarse) * 0.125
    left = iota(TILE, 1) < TILE[1] // 2
    x1 = [iterate[MID + plane, mid_y : 2 * mid_y] for plane in range(mid_x)]
    low_one, low_two = low[0], low[1]
    pairs = count_x // 2
    own = place[0] // 2
    above, below = lax.rem(own + 1, pairs), lax.rem(own + pairs - 1, pairs)

    def fill(i, carry):
        up, down = i == above, i == below
        edge = jnp.where(up, mid_target[mid_x - 1], mid_target[0])
        edge_left, edge_right = jnp.where(left, coarse, roll(edge, TILE[1] // 2, 1)), jnp.where(left, coarse, edge)
        near_pair = up | down | (i == own)
        for j in range(count_y):
            me = place[1]
            beside = (j == me) | (j == lax.rem(me + 1, count_y)) | (j == lax.rem(me + count_y - 1, count_y))
            far = jnp.logical_not(near_pair & beside)
            one, two = 2 * i * count_y + j, (2 * i + 1) * count_y + j
            slots[one, 0] = edge_left
            slots[two, 0] = edge_right
            for at, tile in ((1, low_one), (2, low_two)):
                slots[one, at] = jnp.where(far | (down & odd), tile, jnp.where(up & even, x1[at + 1], x1[at - 1]))
                slots[two, at] = jnp.where(far | (up & even), tile, jnp.where(down & odd, x1[at - 1], x1[at + 1]))
        return carry

    each(0, pairs, fill)


def low_kernel(count_x, count_y, own_half, near, iterate, gathered, fields, coeffs, update):
    planes, size_y, lanes = iterate.shape
    low_x, low_y = 2 * planes // count_x, size_y // count_y
    low_z = lanes // 2
    me_x, me_y = here()

    def take_all(i, carry):
        for kind in range(3):
            gathered[i, kind] = own_half[i, kind]
        return carry

    each(0, count_x * count_y, take_all)
    for dy in (-1, 0, 1):
        for dx in range(-2, 3):
            source = lax.rem(me_x + dx + count_x, count_x) * count_y + lax.rem(me_y + dy + count_y, count_y)
            for kind in range(2):
                gathered[source, 1 + kind] = near[((dx + 2) * 3 + dy + 1) * 2 + kind]

    left = iota(TILE, 1) < low_z

    def place(i, carry):
        for j in range(count_y):
            one = [gathered[i * count_y + j, kind] for kind in range(3)]
            two = [gathered[(i + count_x // 2) * count_y + j, kind] for kind in range(3)]
            parts = [jnp.where(left, low, roll(high, low_z, 1)) for low, high in zip(one, two)]
            parts += [jnp.where(left, roll(low, low_z, 1), high) for low, high in zip(one[1:], two[1:])]
            for kind, tile in enumerate(parts):
                for plane in range(low_x):
                    fields[kind, i * low_x + plane, j * low_y : (j + 1) * low_y] = tile[
                        plane * low_y : (plane + 1) * low_y
                    ]
        return carry

    each(0, count_x // 2, place)
    lane = iota((size_y, lanes), 1) % low_z
    scale = 0.0625
    weights = chebyshev_weights(COARSE_SWEEPS)

    def next_plane(ref, i, first):
        if isinstance(i, int):
            return roll(first, low_z, 1) if i == planes - 1 else ref[i + 1]
        return jnp.where(i == planes - 1, roll(first, low_z, 1), ref[jnp.minimum(i + 1, planes - 1)])

    def prepare(i, carry):
        goal, yl, diag, zl, xl = (fields[kind, i] for kind in range(5))
        xh = next_plane(fields.at[4], i, fields[4, 0])
        yh = roll(yl, -1, 0)
        zh = jnp.where(lane == low_z - 1, 0.0, roll(zl, -1, 1))
        inverse = 1.0 / (diag + scale * (xl + xh + yl + yh + zl + zh))
        scaled = scale * inverse
        coeffs[0, i] = scaled * xl
        coeffs[1, i] = scaled * xh
        coeffs[2, i] = scaled * yl
        coeffs[3, i] = scaled * yh
        coeffs[4, i] = jnp.where(lane == 0, 0.0, scaled * zl)
        coeffs[5, i] = scaled * zh
        goal = goal * inverse
        coeffs[6, i] = goal
        update[i] = weights[0][1] * goal
        iterate[i] = weights[0][1] * goal
        return carry

    each(0, planes, prepare)
    for pair in weights[1:]:
        start = iterate[0]

        def body(i, carry, pair=pair, start=start):
            below, here = carry
            above = next_plane(iterate, i, start)
            step = pair[1] * scaled_remain(coeffs, i, below, here, above) + pair[0] * update[i]
            update[i] = step
            iterate[i] = here + step
            return here, above

        each(0, planes, body, (roll(iterate[planes - 1], low_z, 1), start))


def fine_coeffs_kernel(fields_own, low_x, high_x, low_y, high_y, first_c, second_c, coeffs, own_windows, side_windows):
    size_x, size_y, size_z = fields_own.shape[1:]
    low_c, high_c = got(first_c, second_c, here()[0] % 2 == 1)
    assemble_owns(own_windows, fields_own, low_y, high_y)
    assemble_sides(side_windows, (size_y, size_z), low_x, high_x, low_c, high_c)
    end = FINE + size_x
    windows = Stack(
        (0, FINE, side_windows, 0), (FINE, end, own_windows, 0), (end, end + FINE, side_windows, FINE)
    )
    fields = [windows.of(field) for field in range(6)]
    scale_coeffs(1.0, *fields[2:], Stack((2, end + 3, coeffs, 0)), (2, end + 3), fields[1])


def window_kernel(own, first_x, second_x, first_y, second_y, first_c, second_c, window):
    size_x, size_y, size_z = own.shape
    place = here()
    odd = place[0] % 2 == 1
    low_x, high_x = got(first_x, second_x, odd)
    low_y, high_y = got(first_y, second_y, place[1] % 2 == 1)
    low_c, high_c = got(first_c, second_c, odd)
    assemble_own(window.at[FINE : FINE + size_x], own, low_y, high_y, 0, 0)
    assemble_side(window, FINE - 4, 4, (size_y, size_z), low_x, 0, low_c, 0, 3, True)
    assemble_side(window, FINE + size_x, 4, (size_y, size_z), high_x, 0, high_c, 0, 3, False)


def last_kernel(
    count_x, count_y, own_half, other_half, low_iterate, mid_coeffs, goal_in, fine_coeffs, window,
    out,
    goal, mid_iterate, mid_update,
    iterate, update,
):
    size_x, size_y, size_z = out.shape
    mid_x, mid_y, mid_z = size_x // 2, size_y // 2, size_z // 2
    last = size_x + 2 * FINE - 2
    coeffs = Stack((2, last, fine_coeffs, 0))
    me_x, me_y = here()
    even = me_x % 2 == 0

    def half(which, device, tile):
        one, two = own_half[device, tile], other_half[device, tile]
        return jnp.where(even, one, two) if which == 0 else jnp.where(even, two, one)

    def device(dx, dy):
        return lax.rem(me_x + dx + count_x, count_x) * count_y + lax.rem(me_y + dy + count_y, count_y)

    first, far = MID - mid_x, MID + 2 * mid_x
    for dy in (-1, 0, 1):
        rows = slice((dy + 1) * mid_y, (dy + 2) * mid_y)
        for dx in (-1, 0, 1):
            source = device(dx, dy)
            start = MID + dx * mid_x
            for plane in range(mid_x):
                mid_iterate[start + plane, rows] = half(plane // 2, source, 1 + plane % 2)
        for plane in range(2):
            mid_iterate[plane, rows] = own_half[device(-2, dy), 1 + plane]
            mid_iterate[far + plane, rows] = own_half[device(2, dy), 1 + plane]
    low_planes, low_size_y = low_iterate.shape[:2]
    low_size_x = 2 * low_planes
    low_y = mid_y // 2
    turn = lax.rem(low_size_y - me_y * low_y + low_y, low_size_y)
    for plane in range((mid_x + 2 * MID) // 2):
        at = lax.rem(me_x * (mid_x // 2) - MID // 2 + plane + low_size_x, low_size_x)
        turned = pltpu.roll(low_iterate[lax.rem(at, low_planes)], turn, 0)
        side = at // low_planes
        one, two = lanes_spread(turned[: TILE[0]], side), lanes_spread(turned[TILE[0] : 2 * TILE[0]], side)
        part = jnp.concatenate([rows_spread(one, 0), rows_spread(one, 1), rows_spread(two, 0)], axis=0)
        mid_iterate[2 * plane] += part
        mid_iterate[2 * plane + 1] += part

    left = iota(TILE, 1) < TILE[1] // 2
    for plane in range(first, far):
        goal[plane] = goal_in[plane]
    for dy in (-1, 0, 1):
        rows = slice((dy + 1) * mid_y, (dy + 2) * mid_y)
        for plane, dx in ((first - 1, -2), (far, 2)):
            source = device(dx, dy)
            edge = jnp.where(left, roll(half(0, source, 0), TILE[1] // 2, 1), half(1, source, 0))
            goal[plane, rows] = edge * mid_coeffs[6, plane, rows]
    for sweep, pair in enumerate(chebyshev_weights(SWEEPS)):
        sweep_window(
            mid_iterate, mid_update, mid_coeffs, (first - 1 + sweep, far + 1 - sweep), pair, sweep == 0, goal
        )

    fine_low = FINE - 4
    for plane in range(mid_x + 4):
        turned = roll(mid_iterate[MID - 2 + plane], -4, 0)
        lines = []
        for r in range(2):
            tile = turned[r * TILE[0] : (r + 1) * TILE[0]]
            for side in range(2):
                line = rows_spread(tile, side)
                lines.append(jnp.concatenate([lanes_spread(line, 0), lanes_spread(line, 1)], axis=1))
        part = jnp.concatenate(lines, axis=0)
        for at in (fine_low + 2 * plane, fine_low + 2 * plane + 1):
            iterate[at] = window[at] + part
    for sweep, pair in enumerate(chebyshev_weights(SWEEPS)):
        sweep_window(
            iterate, update, coeffs, (2 + sweep, last - sweep), pair, sweep == 0
        )
    for plane in range(size_x):
        out[plane] = iterate[FINE + plane, PAD : PAD + size_y]


def call(kernel, inputs, outs, scratch=(), scalars=0, far_in=(), far_out=(), sems=0):
    def place(i):
        return pltpu.SMEM if i < scalars else pltpu.HBM if i in far_in else pltpu.VMEM

    near = [x.shape for i, x in enumerate(inputs) if i >= scalars and i not in far_in]
    near += [shape for i, shape in enumerate(outs) if i not in far_out] + list(scratch)
    used = 4 * sum(math.prod(shape) for shape in near)
    inputs = [pltpu.with_memory_space_constraint(x, pltpu.HBM) if i in far_in else x for i, x in enumerate(inputs)]
    return pl.pallas_call(
        kernel,
        out_shape=[
            pltpu.HBM(shape, F32) if i in far_out else jax.ShapeDtypeStruct(shape, F32)
            for i, shape in enumerate(outs)
        ],
        in_specs=[pl.BlockSpec(memory_space=place(i)) for i in range(len(inputs))],
        out_specs=[
            pl.BlockSpec(memory_space=pltpu.HBM if i in far_out else pltpu.VMEM) for i in range(len(outs))
        ],
        scratch_shapes=[pltpu.VMEM(shape, F32) for shape in scratch]
        + ([pltpu.SemaphoreType.DMA((sems,))] if sems > 1 else [pltpu.SemaphoreType.DMA] * sems),
        cost_estimate=pl.CostEstimate(flops=1000, bytes_accessed=1000, transcendentals=0),
        compiler_params=pltpu.CompilerParams(vmem_limit_bytes=used + used // 4 + 2 * 1024 * 1024),
    )(*inputs)


def local(source, initial, absorption, beta_x, beta_y, beta_z):
    size_x, size_y, size_z = source.shape
    mid_x, mid_y, mid_z = size_x // 2, size_y // 2, size_z // 2
    low_x, low_y = mid_x // 2, mid_y // 2
    count_x, count_y = lax.axis_size("gx"), lax.axis_size("gy")
    devices = count_x * count_y
    plane, strip = tiles_of(size_y, size_z), tiles_of(8, size_z)
    mids = 4 * mid_x

    def tiles(count):
        return (count,) + TILE

    pairs = size_x // 2
    up_x, down_x, up_y, down_y, mid, low, own = call(
        pack_kernel,
        (initial, source, absorption, beta_x, beta_y, beta_z),
        [
            tiles(sum(UP_PLANES) * plane),
            tiles(sum(DOWN_PLANES) * plane),
            tiles((6 * pairs + 1) * strip + 2 + 4 * STRIP),
            tiles((6 * pairs + 2) * strip + 2 + 4 * STRIP),
            tiles(mids),
            tiles(2),
            (6,) + source.shape,
        ],
        far_in=range(6),
        sems=6,
    )
    low_x1, high_x1 = shifted(up_x, "gx", 1), shifted(down_x, "gx", -1)
    low_y1, high_y1 = shifted(up_y, "gy", 1), shifted(down_y, "gy", -1)
    first_c1, second_c1 = call(
        functools.partial(corner_kernel, size_x, size_z),
        (low_y1, high_y1, mid, low),
        [tiles(corner_tiles(DOWN_CORNER) * strip + 16)] * 2,
    )
    first_c1, second_c1 = swapped(first_c1, second_c1, "gx")

    tall = (size_y + 2 * PAD, size_z)
    wide = (size_x + 2 * FINE,) + tall
    own_windows, own_coeffs, up_corner, down_corner, strips = call(
        own_kernel,
        (own, low_y1, high_y1),
        [(6, size_x) + tall, (8, size_x - 1) + tall, tiles(MID_CORNER), tiles(MID_CORNER), tiles(2 * mids)],
    )
    iterate, mid_target, first_x2, second_x2, first_y2, second_y2 = call(
        fine_kernel,
        (own_windows, own_coeffs, up_corner, down_corner, mid, low_x1, high_x1, first_c1, second_c1),
        [
            source.shape,
            (mid_x, mid_y, mid_z),
            tiles(4 * plane + mid_x + MID_CORNER + mids + 10 + PASSED),
            tiles(4 * plane + mid_x + MID_CORNER + mids + 10 + PASSED),
            tiles(pairs * strip + mid_x),
            tiles(pairs * strip + mid_x),
        ],
        scratch=[(6, 2 * FINE) + tall, (8, 2 * FINE + 1) + tall, wide, wide],
    )
    first_x2, second_x2 = swapped(first_x2, second_x2, "gx")
    first_y2, second_y2 = swapped(first_y2, second_y2, "gy")
    first_c2, second_c2 = call(
        functools.partial(corner_two_kernel, size_x, size_z),
        (first_y2, second_y2),
        [tiles(2 * strip + 2 * mid_x)] * 2,
    )
    first_c2, second_c2 = swapped(first_c2, second_c2, "gx")

    mid_wide = (mid_x + 2 * MID, 3 * mid_y, mid_z)
    mid_coeffs, near = call(
        mid_coeffs_kernel,
        (mid, low, strips, low_y1, high_y1, first_c1, second_c1, first_x2, second_x2),
        [(8,) + mid_wide, tiles(30)],
        [(4,) + mid_wide],
    )
    (coeffs,) = call(
        fine_coeffs_kernel,
        (own, low_x1, high_x1, low_y1, high_y1, first_c1, second_c1),
        [(7, wide[0] - 4) + tall],
        [(6, size_x) + tall, (6, 2 * FINE) + tall],
    )
    goal, slots = call(
        functools.partial(mid_kernel, count_x, count_y),
        (low, mid_target, mid_coeffs, first_x2, second_x2, first_y2, second_y2, first_c2, second_c2, coeffs),
        [mid_wide, (devices, 3) + TILE],
        [mid_wide] * 3,
    )
    own_half = lax.all_to_all(slots, ("gx", "gy"), 0, 0)
    other_half = lax.ppermute(own_half, "gx", [(i, i ^ 1) for i in range(count_x)])

    (window,) = call(
        window_kernel, (iterate, first_x2, second_x2, first_y2, second_y2, first_c2, second_c2), [wide]
    )
    low_wide = (low_x * count_x // 2, low_y * count_y, mid_z)
    (low_iterate,) = call(
        functools.partial(low_kernel, count_x, count_y),
        (own_half, near),
        [low_wide],
        [(devices, 3) + TILE, (5,) + low_wide, (7,) + low_wide, low_wide],
    )
    (result,) = call(
        functools.partial(last_kernel, count_x, count_y),
        (own_half, other_half, low_iterate, mid_coeffs, goal, coeffs, window),
        [source.shape],
        [mid_wide, mid_wide, mid_wide]
        + [wide, wide],
    )
    return result


def solution(mesh):
    spec = P("gx", "gy", None)
    return jax.shard_map(
        local, mesh=mesh, in_specs=(spec,) * 6, out_specs=spec, check_vma=False
    )
```

```python
import functools
import math

import jax
import jax.numpy as jnp
from jax import lax
from jax.experimental import pallas as pl
from jax.experimental.pallas import tpu as pltpu
from jax.sharding import PartitionSpec as P

SWEEPS = 4
COARSE_SWEEPS = 8
F32 = jnp.float32
TILE = (8, 128)
PAD = 8
FINE = 5
MID = 6


def chebyshev_weights(sweeps):
    cheb_theta = 1.125
    cheb_delta = 0.875
    cheb_sigma = cheb_theta / cheb_delta
    rho_old = 1.0 / cheb_sigma
    weights = [(0.0, 1.0 / cheb_theta)]
    for sweep in range(1, sweeps):
        rho_new = 1.0 / (2.0 * cheb_sigma - rho_old)
        weights.append((rho_new * rho_old, 2.0 * rho_new / cheb_delta))
        rho_old = rho_new
    return weights


def iota(shape, axis):
    return lax.broadcasted_iota(jnp.int32, shape, axis)


def roll(value, shift, axis):
    return pltpu.roll(value, shift % value.shape[axis], axis)


def take(tile, index, axis):
    return jnp.take_along_axis(tile, index, axis=axis, mode="promise_in_bounds")


def rows_spread(tile, half):
    return take(tile, iota(TILE, 0) // 2 + 4 * half, 0)


def lanes_spread(tile, half):
    return take(tile, iota(TILE, 1) // 2 + 64 * half, 1)


def rows_merge(one, two, pairs=True):
    row = iota(TILE, 0)
    if pairs:
        one, two = one + roll(one, -1, 0), two + roll(two, -1, 0)
    index = (2 * row) % TILE[0]
    return jnp.where(row < TILE[0] // 2, take(one, index, 0), take(two, index, 0))


def lanes_merge(one, two, pairs=True):
    lane = iota(TILE, 1)
    if pairs:
        one, two = one + roll(one, -1, 1), two + roll(two, -1, 1)
    index = (2 * lane) % TILE[1]
    return jnp.where(lane < TILE[1] // 2, take(one, index, 1), take(two, index, 1))


def merge(plane, row_pairs=True, lane_pairs=True):
    halves = []
    for side in range(2):
        lanes = slice(side * TILE[1], (side + 1) * TILE[1])
        halves.append(rows_merge(plane[: TILE[0], lanes], plane[TILE[0] :, lanes], row_pairs))
    return lanes_merge(*halves, lane_pairs)


def each(start, stop, body, carry=0):
    if stop - start > 20:
        return lax.fori_loop(start, stop, body, carry, unroll=2)
    for i in range(start, stop):
        carry = body(i, carry)
    return carry


def here():
    return lax.axis_index("gx"), lax.axis_index("gy")


class Writer:
    def __init__(self, ref):
        self.ref, self.at = ref, 0

    def put(self, value):
        rows, columns = value.shape
        for r in range(0, rows, TILE[0]):
            for c in range(0, columns, TILE[1]):
                self.ref[self.at] = value[r : r + TILE[0], c : c + TILE[1]]
                self.at += 1


class Tiles:
    def __init__(self):
        self.tiles = []

    def put(self, value):
        rows, columns = value.shape
        for r in range(0, rows, TILE[0]):
            for c in range(0, columns, TILE[1]):
                self.tiles.append(value[r : r + TILE[0], c : c + TILE[1]])


def send(first, second, odd, up, down):
    for at, (one, two) in enumerate(zip(up.tiles, down.tiles, strict=True)):
        first[at] = jnp.where(odd, one, two)
        second[at] = jnp.where(odd, two, one)


class Got:
    def __init__(self, first, second, even, low):
        self.refs = (second, first) if low else (first, second)
        self.even, self.shape = even, first.shape

    def __getitem__(self, at):
        return jnp.where(self.even, self.refs[0][at], self.refs[1][at])


def got(first, second, even):
    return Got(first, second, even, True), Got(first, second, even, False)


class Reader:
    def __init__(self, ref, at=0):
        self.ref, self.at = ref, at

    def get(self, rows, columns):
        lines = []
        for _ in range(rows // TILE[0]):
            parts = []
            for _ in range(columns // TILE[1]):
                parts.append(self.ref[self.at])
                self.at += 1
            lines.append(parts[0] if len(parts) == 1 else jnp.concatenate(parts, axis=1))
        return lines[0] if len(lines) == 1 else jnp.concatenate(lines, axis=0)


UP_PLANES = (5, 4, 4, 4, 4, 4)
DOWN_PLANES = (5, 4, 4, 5, 4, 4)
UP_CORNER = (4, 3, 3, 3, 4, 3)
DOWN_CORNER = (4, 3, 3, 4, 4, 3)
STRIP = 2


def corner_tiles(counts):
    return sum(count - 1 for count in counts)


def tiles_of(rows, columns):
    return (rows // TILE[0]) * (columns // TILE[1])


def is_upper(width):
    return iota((TILE[0], width), 0) < TILE[0] // 2


def swapped(first, second, axis):
    count = lax.axis_size(axis)
    outer = [(i, (i + 1 if i % 2 else i - 1) % count) for i in range(count)]
    inner = [(i, i ^ 1) for i in range(count)]
    return lax.ppermute(first, axis, outer), lax.ppermute(second, axis, inner)


def shifted(value, axis, step):
    count = lax.axis_size(axis)
    return lax.ppermute(value, axis, [(i, (i + step) % count) for i in range(count)])


def pack_kernel(
    ini_in, src_in, absorb_in, face_x_in, face_y_in, face_z_in,
    up_x, down_x, up_y, down_y, mid, low, own, sems,
):
    copies = []
    for field, ref in enumerate((ini_in, src_in, absorb_in, face_x_in, face_y_in, face_z_in)):
        copies.append(pltpu.make_async_copy(ref, own.at[field], sems.at[field]))
        copies[-1].start()
    for copy in copies:
        copy.wait()
    fields = tuple(own.at[field] for field in range(6))
    ini, src, absorb, face_x, face_y, face_z = fields
    size_x, size_y, size_z = ini.shape
    mid_x = size_x // 2
    for block in range(mid_x):
        one, two = 2 * block, 2 * block + 1
        mid[block] = merge(absorb[one] + absorb[two]) * 0.125
        mid[mid_x + block] = merge(face_x[one]) * 0.25
        mid[2 * mid_x + block] = merge(face_y[one] + face_y[two], row_pairs=False) * 0.25
        mid[3 * mid_x + block] = merge(face_z[one] + face_z[two], lane_pairs=False) * 0.25

    def coarser(array, planes, row_pairs=True, lane_pairs=True):
        parts = []
        for block in range(0, mid_x, 2):
            total = None
            for plane in range(planes):
                part = mid[array * mid_x + block + plane]
                total = part if total is None else total + part
            parts.append(total)
        tile = rows_merge(*parts, row_pairs)
        return lanes_merge(tile, tile, lane_pairs)

    left = iota(TILE, 1) < TILE[1] // 2
    low[0] = jnp.where(left, coarser(2, 2, row_pairs=False), coarser(3, 2, lane_pairs=False)) * 0.25
    low[1] = jnp.where(left, coarser(0, 2) * 0.125, coarser(1, 1) * 0.25)

    tops, bottoms = Writer(up_x), Writer(down_x)
    for ref, count in zip(fields, UP_PLANES):
        for plane in range(size_x - count, size_x):
            tops.put(ref[plane])
    for ref, count in zip(fields, DOWN_PLANES):
        for plane in range(count):
            bottoms.put(ref[plane])

    upper = is_upper(size_z)
    tops_y, bottoms_y = Writer(up_y), Writer(down_y)
    for ref in fields:
        for pair in range(0, size_x, 2):
            one, two = ref[pair], ref[pair + 1]
            tops_y.put(jnp.where(upper, roll(one[size_y - 8 :], 4, 0), two[size_y - 8 :]))
            bottoms_y.put(jnp.where(upper, one[:8], roll(two[:8], 4, 0)))
    tops_y.put(ini[:, size_y - 5, :])
    bottoms_y.put(ini[:, 4, :])
    bottoms_y.put(face_y[:, 4, :])
    for writer in (tops_y, bottoms_y):
        for tile in range(2):
            writer.put(low[tile])
    upper = is_upper(TILE[1])
    for array in range(4):
        for pair in range(0, mid_x, 2):
            one, two = mid[array * mid_x + pair], mid[array * mid_x + pair + 1]
            for writer in (tops_y, bottoms_y):
                writer.put(jnp.where(upper, roll(one, -2, 0), roll(two, 2, 0)))


def corner_of(low_y, high_y, plane, upper, first_tile=0):
    width = upper.shape[1]
    at = first_tile + (plane // 2) * tiles_of(8, width)
    low = Reader(low_y, at).get(8, width)
    high = Reader(high_y, at).get(8, width)
    if plane % 2 == 0:
        return jnp.where(upper, low, roll(high, 4, 0))
    return jnp.where(upper, roll(low, 4, 0), high)


def mix(near, far):
    row = iota(near.shape, 0)
    return jnp.where((row >= 2) & (row < 6), near, roll(far, 3, 0))


def put_corners(writer, low_y, high_y, planes, upper, first_tile):
    parts = [corner_of(low_y, high_y, plane, upper, first_tile) for plane in planes]
    for part in parts[:-2]:
        writer.put(part)
    writer.put(mix(*parts[-2:]))


def mid_beside(ref, array, plane, low):
    pairs = (ref.shape[0] - 4 * STRIP - 2) // 12
    at = ((2 + array) * pairs + plane) * 2
    halves = []
    for side in range(2):
        total = ref[at + side]
        if array != 1:
            total = total + roll(total, 4, 0)
        if array != 2:
            total = total + roll(total, -1, 0)
        halves.append(take(total, (2 * iota(TILE, 0) + (4 if low else 0)) % TILE[0], 0))
    return lanes_merge(*halves, array != 3) * (0.125 if array == 0 else 0.25)


def mid_strip(ref, array, plane, low):
    far = roll(ref[ref.shape[0] - 4 * STRIP + array * STRIP + plane // 2], 2 if plane % 2 == 0 else -2, 0)
    row = iota(TILE, 0)
    return jnp.where((row >= 2) & (row < 6), far, mid_beside(ref, array, plane, low))


def corner_kernel(size_x, size_z, low_y, high_y, mid, low_faces, first, second):
    place = here()
    upper = is_upper(size_z)
    per_field = (size_x // 2) * tiles_of(8, size_z)
    tops, bottoms = Tiles(), Tiles()
    for field in range(6):
        start = field * per_field
        planes = [size_x - 1 - plane for plane in range(UP_CORNER[field])]
        put_corners(tops, low_y, high_y, planes, upper, start)
        put_corners(bottoms, low_y, high_y, range(DOWN_CORNER[field]), upper, start)
    mid_x = size_x // 2
    upper = is_upper(TILE[1])
    for _ in range(len(bottoms.tiles) - len(tops.tiles)):
        tops.put(low_faces[0])
    for writer, near, next_plane in ((tops, mid_x - 1, mid_x - 2), (bottoms, 0, 1)):
        wanted = [(array, near) for array in range(4)] + [(1, next_plane)]
        for array, plane in wanted:
            writer.put(
                jnp.where(upper, mid_beside(high_y, array, plane, False), mid_beside(low_y, array, plane, True))
            )
        for array, plane in wanted:
            writer.put(mid[array * mid_x + plane])
        for tiles in ((low_faces[0], low_faces[1]), low_tiles_of(low_y), low_tiles_of(high_y)):
            for tile in tiles:
                writer.put(tile)
    send(first, second, place[0] % 2 == 1, tops, bottoms)


def low_tiles_of(ref):
    end = ref.shape[0] - 4 * STRIP
    return ref[end - 2], ref[end - 1]


class Planes:
    def __init__(self, *parts):
        self.parts = parts
        self.shape = parts[0][2].shape

    def find(self, i):
        for start, stop, ref, offset, lead in self.parts:
            if start <= i < stop:
                return ref, lead + (i - start + offset,)
        raise IndexError(i)

    def __getitem__(self, i):
        ref, index = self.find(i)
        return ref[index]


class Stack:
    def __init__(self, *parts):
        self.parts = parts

    def of(self, kind):
        return Planes(*((a, b, ref, offset, (kind,)) for a, b, ref, offset in self.parts))

    def __getitem__(self, index):
        return self.of(index[0])[index[1]]

    def __setitem__(self, index, value):
        ref, place = self.of(index[0]).find(index[1])
        ref[place] = value


def scale_coeffs(scale, absorb, face_x, face_y, face_z, coeffs, planes, target=None, diagonal=None):
    rows, lanes = absorb.shape[-2:]
    lane = iota((rows, lanes), 1)

    def body(i, carry):
        xl, xh = face_x[i], face_x[i + 1]
        yl, zl = face_y[i], face_z[i]
        yh = roll(yl, -1, 0)
        zh = jnp.where(lane == lanes - 1, 0.0, roll(zl, -1, 1))
        diag = absorb[i] + scale * (xl + xh + yl + yh + zl + zh)
        inverse = 1.0 / diag
        scaled = scale * inverse
        coeffs[0, i] = scaled * xl
        coeffs[1, i] = scaled * xh
        coeffs[2, i] = scaled * yl
        coeffs[3, i] = scaled * yh
        coeffs[4, i] = jnp.where(lane == 0, 0.0, scaled * zl)
        coeffs[5, i] = scaled * zh
        if target is not None:
            coeffs[6, i] = target[i] * inverse
        else:
            coeffs[6, i] = inverse
        if diagonal is not None:
            coeffs[7, i] = diag
        return carry

    each(*planes, body)


def scaled_remain(coeffs, i, below, here, above, goal=None):
    along_z = coeffs[4, i] * roll(here, 1, 1) + coeffs[5, i] * roll(here, -1, 1)
    along_y = coeffs[2, i] * roll(here, 1, 0) + coeffs[3, i] * roll(here, -1, 0)
    along_x = coeffs[0, i] * below + coeffs[1, i] * above
    return ((coeffs[6, i] if goal is None else goal[i]) - here + along_x) + (along_y + along_z)


def sweep_window(iterate, update, coeffs, planes, pair, first, goal=None, source=None):
    start, stop = planes
    source = iterate if source is None else source

    def body(i, carry):
        below, here = carry
        above = source[i + 1]
        step = pair[1] * scaled_remain(coeffs, i, below, here, above, goal)
        if not first:
            step = step + pair[0] * update[i]
        update[i] = step
        iterate[i] = here + step
        return here, above

    each(start, stop, body, (source[start - 1], source[start]))


def assemble_own(window, own, low_y, high_y, low_start, high_start):
    size_x, size_y, size_z = own.shape
    high = PAD + size_y
    low_reader, high_reader = Reader(low_y, low_start), Reader(high_y, high_start)
    for pair in range(0, size_x, 2):
        window[pair, PAD:high] = own[pair]
        window[pair + 1, PAD:high] = own[pair + 1]
        tile = low_reader.get(8, size_z)
        window[pair, 0:8] = roll(tile, 4, 0)
        window[pair + 1, 0:8] = tile
        tile = high_reader.get(8, size_z)
        window[pair, high : high + 8] = tile
        window[pair + 1, high : high + 8] = roll(tile, 4, 0)


def assemble_side(window, first, count, rows, planes, plane_start, corners, corner_start, corner_count, from_end):
    size_y, size_z = rows
    high = PAD + size_y
    reader = Reader(planes, plane_start)
    for plane in range(count):
        window[first + plane, PAD:high] = reader.get(size_y, size_z)
    reader = Reader(corners, corner_start)
    tiles = [roll(reader.get(8, size_z), 4, 0) for _ in range(corner_count - 1)]
    tiles.append(roll(tiles[-1], -3, 0))
    for plane, tile in enumerate(tiles):
        at = first + count - 1 - plane if from_end else first + plane
        window[at, 0:8] = tile
        window[at, high : high + 8] = tile


def assemble_owns(windows, own, low_y, high_y):
    size_x, size_y, size_z = own.shape[1:]
    per_field = (size_x // 2) * tiles_of(8, size_z)
    for field in range(6):
        assemble_own(windows.at[field], own.at[field], low_y, high_y, field * per_field, field * per_field)
    low_line = Reader(low_y, 6 * per_field).get(8, size_z)
    high_reader = Reader(high_y, 6 * per_field)
    high_line = high_reader.get(8, size_z)
    face_line = high_reader.get(8, size_z)
    high = PAD + size_y
    for plane in range(size_x):
        windows[0, plane, 3:4] = low_line[plane : plane + 1]
        windows[0, plane, high + 4 : high + 5] = high_line[plane : plane + 1]
        windows[4, plane, high + 4 : high + 5] = face_line[plane : plane + 1]


def assemble_sides(side_windows, rows, low_x, high_x, low_c, high_c):
    plane_tiles, strip_tiles = tiles_of(*rows), tiles_of(8, rows[1])
    starts = [0] * 4
    for field in range(6):
        up, down, up_c, down_c = (
            kinds[field] for kinds in (UP_PLANES, DOWN_PLANES, UP_CORNER, DOWN_CORNER)
        )
        window = side_windows.at[field]
        assemble_side(
            window, FINE - up, up, rows, low_x, starts[0], low_c, starts[2], up_c, True
        )
        assemble_side(
            window, FINE, down, rows, high_x, starts[1], high_c, starts[3], down_c, False
        )
        starts[0] += up * plane_tiles
        starts[1] += down * plane_tiles
        starts[2] += (up_c - 1) * strip_tiles
        starts[3] += (down_c - 1) * strip_tiles


def own_kernel(own, low_y, high_y, windows, coeffs, up_corner, down_corner, strips):
    assemble_owns(windows, own, low_y, high_y)
    fields = [windows.at[field] for field in range(6)]
    scale_coeffs(1.0, *fields[2:], coeffs, (0, own.shape[1] - 1), fields[1], True)
    mid_x = own.shape[1] // 2
    tops, bottoms = Writer(up_corner), Writer(down_corner)
    upper = is_upper(TILE[1])
    for side, (ref, low) in enumerate(((low_y, True), (high_y, False))):
        for array in range(4):
            for plane in range(mid_x):
                strips[(side * 4 + array) * mid_x + plane] = mid_strip(ref, array, plane, low)
    for writer, first, step in ((tops, mid_x - 1, -1), (bottoms, 0, 1)):
        for array in range(4):
            for q in range(2):
                for side in range(2):
                    writer.put(strips[(side * 4 + array) * mid_x + first + q * step])
        for array in range(4):
            for q in range(2, 4):
                one, two = (roll(strips[(side * 4 + array) * mid_x + first + q * step], 4, 0) for side in range(2))
                writer.put(jnp.where(upper, one, two))


def fine_kernel(
    own_windows, own_coeffs, up_corner, down_corner, mid, low_x, high_x, first_c, second_c,
    iterate_out, mid_target, first_x, second_x, first_y, second_y,
    side_windows, side_coeffs, iterate, update,
):
    size_x, size_z = own_windows.shape[1], own_windows.shape[3]
    size_y = own_windows.shape[2] - 2 * PAD
    place = here()
    odd = place[0] % 2 == 1
    low_c, high_c = got(first_c, second_c, odd)
    assemble_sides(side_windows, (size_y, size_z), low_x, high_x, low_c, high_c)
    end = FINE + size_x
    last = end + FINE - 1
    windows = Stack(
        (0, FINE, side_windows, 0), (FINE, end, own_windows, 0), (end, last + 1, side_windows, FINE)
    )
    coeffs = Stack(
        (0, FINE, side_coeffs, 0), (FINE, end - 1, own_coeffs, 0), (end - 1, last + 1, side_coeffs, FINE)
    )
    fields = [windows.of(field) for field in range(6)]
    scale_coeffs(1.0, *fields[2:], coeffs, (1, FINE), fields[1], True)
    scale_coeffs(1.0, *fields[2:], coeffs, (end - 1, last), fields[1], True)
    for sweep, pair in enumerate(chebyshev_weights(SWEEPS)):
        sweep_window(
            iterate, update, coeffs, (1 + sweep, last - sweep), pair, sweep == 0,
            source=fields[0] if sweep == 0 else None,
        )
    mid_x, mid_y = size_x // 2, size_y // 2
    coarse = []
    for block in range(mid_x):
        total = None
        for plane in (FINE + 2 * block, FINE + 2 * block + 1):
            remain = scaled_remain(coeffs, plane, iterate[plane - 1], iterate[plane], iterate[plane + 1])
            remain = (remain * coeffs[7, plane])[PAD : PAD + size_y]
            total = remain if total is None else total + remain
        coarse.append(merge(total) * 0.125)
        mid_target[block] = coarse[block]
    for plane in range(size_x):
        iterate_out[plane] = iterate[FINE + plane, PAD : PAD + size_y]

    tops, bottoms = Tiles(), Tiles()
    for plane in range(size_x - 4, size_x):
        tops.put(iterate_out[plane])
    for plane in range(4):
        bottoms.put(iterate_out[plane])
    upper = is_upper(size_z)
    tops_y, bottoms_y = Tiles(), Tiles()
    for pair in range(0, size_x, 2):
        one, two = iterate_out[pair], iterate_out[pair + 1]
        tops_y.put(jnp.where(upper, roll(one[size_y - 8 :], 4, 0), two[size_y - 8 :]))
        bottoms_y.put(jnp.where(upper, one[:8], roll(two[:8], 4, 0)))
    for writer in (tops, bottoms, tops_y, bottoms_y):
        for tile in coarse:
            writer.put(tile)
    for writer, ref in ((tops, up_corner), (bottoms, down_corner)):
        for tile in range(MID_CORNER):
            writer.put(ref[tile])
    for writer in (tops, bottoms):
        for tile in range(mid.shape[0]):
            writer.put(mid[tile])
    for writer, corners in ((tops, low_c), (bottoms, high_c)):
        for tile in range(corners.shape[0] - PASSED - 10, corners.shape[0]):
            writer.put(corners[tile])
    send(first_x, second_x, odd, tops, bottoms)
    send(first_y, second_y, place[1] % 2 == 1, tops_y, bottoms_y)


MID_CORNER = 24
PASSED = 6


def whole_corner(ref, start, array, q, side):
    return ref[start + (array * 2 + q) * 2 + side]


def part_corner(ref, start, array, q):
    return ref[start + 16 + array * 2 + q - 2]


def corner_two_kernel(size_x, size_z, first_y, second_y, first, second):
    place = here()
    upper = is_upper(size_z)
    low_y, high_y = got(first_y, second_y, place[1] % 2 == 1)
    tops, bottoms = Tiles(), Tiles()
    put_corners(tops, low_y, high_y, [size_x - 1, size_x - 2, size_x - 3], upper, 0)
    put_corners(bottoms, low_y, high_y, range(3), upper, 0)
    mid_x = size_x // 2
    upper = is_upper(TILE[1])
    start = low_y.shape[0] - mid_x
    for writer, near, step in ((tops, mid_x - 1, -1), (bottoms, 0, 1)):
        writer.put(low_y[start + near])
        writer.put(high_y[start + near])
        for q in range(1, mid_x):
            at = start + near + q * step
            writer.put(jnp.where(upper, roll(low_y[at], 4, 0), roll(high_y[at], 4, 0)))
    send(first, second, place[0] % 2 == 1, tops, bottoms)


def level_two_near(near, low, low_y, high_y, low_c, high_c, low_x2, high_x2):
    known = {(0, 0): (low[0], low[1]), (0, -1): low_tiles_of(low_y), (0, 1): low_tiles_of(high_y)}
    for step, ref, distance in ((-1, low_c, 1), (1, high_c, 1), (-1, low_x2, 2), (1, high_x2, 2)):
        start = ref.shape[0] - PASSED
        for at, dy in enumerate((0, -1, 1)):
            known[step * distance, dy] = (ref[start + 2 * at], ref[start + 2 * at + 1])
    for (dx, dy), tiles in known.items():
        for kind in range(2):
            near[((dx + 2) * 3 + dy + 1) * 2 + kind] = tiles[kind]


def mid_coeffs_kernel(
    mid, low, strips, low_y, high_y, first_c, second_c, first_x2, second_x2, coeffs, near, window
):
    place = here()
    low_x2, high_x2 = got(first_x2, second_x2, place[0] % 2 == 1)
    low_c, high_c = got(first_c, second_c, place[0] % 2 == 1)
    level_two_near(near, low, low_y, high_y, low_c, high_c, low_x2, high_x2)
    mid_y, mid_z = mid.shape[1:]
    mid_x = mid.shape[0] // 4
    mids = 4 * mid_x
    first = MID - mid_x
    corner = 4 * tiles_of(2 * mid_y, 2 * mid_z) + mid_x
    passed = corner + MID_CORNER
    for ref, start, block in ((low_x2, passed, 0), (mid, 0, 1), (high_x2, passed, 2)):
        for array in range(4):
            for plane in range(mid_x):
                window[array, first + block * mid_x + plane, mid_y : 2 * mid_y] = ref[start + array * mid_x + plane]
    for array in range(4):
        for plane in range(mid_x):
            window[array, MID + plane, :mid_y] = strips[array * mid_x + plane]
            window[array, MID + plane, 2 * mid_y :] = strips[(4 + array) * mid_x + plane]
    passed += mids
    far = 3 * mid_x + first
    for ref, start, step, end in ((low_x2, MID - 1, -1, first - 1), (high_x2, MID + mid_x, 1, far)):
        for array in range(4):
            for q in range(mid_x):
                if q < 2:
                    one, two = (whole_corner(ref, corner, array, q, side) for side in range(2))
                else:
                    one = two = roll(part_corner(ref, corner, array, q), 4, 0)
                window[array, start + q * step, :mid_y] = one
                window[array, start + q * step, 2 * mid_y :] = two
        for at in range(5):
            array, plane = (at, end) if at < 4 else (1, end + step)
            window[array, plane, :mid_y] = ref[passed + at]
            window[array, plane, 2 * mid_y :] = ref[passed + at]
            window[array, plane, mid_y : 2 * mid_y] = ref[passed + 5 + at]
    scale_coeffs(0.25, *(window.at[array] for array in range(4)), coeffs, (first - 1, far + 1), None, True)


def mid_kernel(
    count_x, count_y, low, mid_target, coeffs, first_x2, second_x2, first_y2, second_y2, first_c2, second_c2, unused,
    goal, slots, target, iterate, update,
):
    mid_x, mid_y, mid_z = mid_target.shape
    first = MID - mid_x
    far = 3 * mid_x + first
    fine_tiles = 4 * tiles_of(2 * mid_y, 2 * mid_z)
    place = here()
    even = place[0] % 2 == 0
    odd = place[0] % 2 == 1
    low_x2, high_x2 = got(first_x2, second_x2, odd)
    low_y2, high_y2 = got(first_y2, second_y2, place[1] % 2 == 1)
    low_c2, high_c2 = got(first_c2, second_c2, odd)
    blocks = {
        (0, 1): (low_x2, fine_tiles),
        (1, 0): (low_y2, low_y2.shape[0] - mid_x),
        (1, 2): (high_y2, high_y2.shape[0] - mid_x),
        (2, 1): (high_x2, fine_tiles),
    }
    for plane in range(mid_x):
        target[MID + plane, mid_y : 2 * mid_y] = mid_target[plane]
    for (bx, by), (ref, start) in blocks.items():
        for plane in range(mid_x):
            target[first + bx * mid_x + plane, by * mid_y : (by + 1) * mid_y] = ref[start + plane]

    for ref, near, step in ((low_c2, MID - 1, -1), (high_c2, MID + mid_x, 1)):
        start = ref.shape[0] - mid_x - 1
        for q in range(mid_x):
            one, two = (ref[start], ref[start + 1]) if q == 0 else [roll(ref[start + 1 + q], 4, 0)] * 2
            target[near + q * step, :mid_y] = one
            target[near + q * step, 2 * mid_y :] = two
    weights = chebyshev_weights(SWEEPS)

    def start_sweep(i, carry):
        value = target[i] * coeffs[6, i]
        goal[i] = value
        update[i] = weights[0][1] * value
        iterate[i] = weights[0][1] * value
        return carry

    each(first, far, start_sweep)
    for sweep in range(1, SWEEPS):
        sweep_window(iterate, update, coeffs, (first + sweep, far - sweep), weights[sweep], False, goal)
    parts = []
    for block in range(0, mid_x, 2):
        total = None
        for plane in (MID + block, MID + block + 1):
            remain = scaled_remain(coeffs, plane, iterate[plane - 1], iterate[plane], iterate[plane + 1], goal)
            remain = (remain * coeffs[7, plane])[mid_y : 2 * mid_y]
            total = remain if total is None else total + remain
        parts.append(total)
    coarse = rows_merge(*parts)
    coarse = lanes_merge(coarse, coarse) * 0.125
    left = iota(TILE, 1) < TILE[1] // 2
    x1 = [iterate[MID + plane, mid_y : 2 * mid_y] for plane in range(mid_x)]
    low_one, low_two = low[0], low[1]
    pairs = count_x // 2
    own = place[0] // 2
    above, below = lax.rem(own + 1, pairs), lax.rem(own + pairs - 1, pairs)

    def fill(i, carry):
        up, down = i == above, i == below
        edge = jnp.where(up, mid_target[mid_x - 1], mid_target[0])
        edge_left, edge_right = jnp.where(left, coarse, roll(edge, TILE[1] // 2, 1)), jnp.where(left, coarse, edge)
        near_pair = up | down | (i == own)
        for j in range(count_y):
            me = place[1]
            beside = (j == me) | (j == lax.rem(me + 1, count_y)) | (j == lax.rem(me + count_y - 1, count_y))
            far = jnp.logical_not(near_pair & beside)
            one, two = 2 * i * count_y + j, (2 * i + 1) * count_y + j
            slots[one, 0] = edge_left
            slots[two, 0] = edge_right
            for at, tile in ((1, low_one), (2, low_two)):
                slots[one, at] = jnp.where(far | (down & odd), tile, jnp.where(up & even, x1[at + 1], x1[at - 1]))
                slots[two, at] = jnp.where(far | (up & even), tile, jnp.where(down & odd, x1[at - 1], x1[at + 1]))
        return carry

    each(0, pairs, fill)


def low_kernel(count_x, count_y, own_half, near, iterate, gathered, fields, coeffs, update):
    planes, size_y, lanes = iterate.shape
    low_x, low_y = 2 * planes // count_x, size_y // count_y
    low_z = lanes // 2
    me_x, me_y = here()

    def take_all(i, carry):
        for kind in range(3):
            gathered[i, kind] = own_half[i, kind]
        return carry

    each(0, count_x * count_y, take_all)
    for dy in (-1, 0, 1):
        for dx in range(-2, 3):
            source = lax.rem(me_x + dx + count_x, count_x) * count_y + lax.rem(me_y + dy + count_y, count_y)
            for kind in range(2):
                gathered[source, 1 + kind] = near[((dx + 2) * 3 + dy + 1) * 2 + kind]

    left = iota(TILE, 1) < low_z

    def place(i, carry):
        for j in range(count_y):
            one = [gathered[i * count_y + j, kind] for kind in range(3)]
            two = [gathered[(i + count_x // 2) * count_y + j, kind] for kind in range(3)]
            parts = [jnp.where(left, low, roll(high, low_z, 1)) for low, high in zip(one, two)]
            parts += [jnp.where(left, roll(low, low_z, 1), high) for low, high in zip(one[1:], two[1:])]
            for kind, tile in enumerate(parts):
                for plane in range(low_x):
                    fields[kind, i * low_x + plane, j * low_y : (j + 1) * low_y] = tile[
                        plane * low_y : (plane + 1) * low_y
                    ]
        return carry

    each(0, count_x // 2, place)
    lane = iota((size_y, lanes), 1) % low_z
    scale = 0.0625
    weights = chebyshev_weights(COARSE_SWEEPS)

    def next_plane(ref, i, first):
        if isinstance(i, int):
            return roll(first, low_z, 1) if i == planes - 1 else ref[i + 1]
        return jnp.where(i == planes - 1, roll(first, low_z, 1), ref[jnp.minimum(i + 1, planes - 1)])

    def prepare(i, carry):
        goal, yl, diag, zl, xl = (fields[kind, i] for kind in range(5))
        xh = next_plane(fields.at[4], i, fields[4, 0])
        yh = roll(yl, -1, 0)
        zh = jnp.where(lane == low_z - 1, 0.0, roll(zl, -1, 1))
        inverse = 1.0 / (diag + scale * (xl + xh + yl + yh + zl + zh))
        scaled = scale * inverse
        coeffs[0, i] = scaled * xl
        coeffs[1, i] = scaled * xh
        coeffs[2, i] = scaled * yl
        coeffs[3, i] = scaled * yh
        coeffs[4, i] = jnp.where(lane == 0, 0.0, scaled * zl)
        coeffs[5, i] = scaled * zh
        goal = goal * inverse
        coeffs[6, i] = goal
        update[i] = weights[0][1] * goal
        iterate[i] = weights[0][1] * goal
        return carry

    each(0, planes, prepare)
    for pair in weights[1:]:
        start = iterate[0]

        def body(i, carry, pair=pair, start=start):
            below, here = carry
            above = next_plane(iterate, i, start)
            step = pair[1] * scaled_remain(coeffs, i, below, here, above) + pair[0] * update[i]
            update[i] = step
            iterate[i] = here + step
            return here, above

        each(0, planes, body, (roll(iterate[planes - 1], low_z, 1), start))


def fine_coeffs_kernel(fields_own, low_x, high_x, low_y, high_y, first_c, second_c, coeffs, own_windows, side_windows):
    size_x, size_y, size_z = fields_own.shape[1:]
    low_c, high_c = got(first_c, second_c, here()[0] % 2 == 1)
    assemble_owns(own_windows, fields_own, low_y, high_y)
    assemble_sides(side_windows, (size_y, size_z), low_x, high_x, low_c, high_c)
    end = FINE + size_x
    windows = Stack(
        (0, FINE, side_windows, 0), (FINE, end, own_windows, 0), (end, end + FINE, side_windows, FINE)
    )
    fields = [windows.of(field) for field in range(6)]
    scale_coeffs(1.0, *fields[2:], Stack((2, end + 3, coeffs, 0)), (2, end + 3), fields[1])


def window_kernel(own, first_x, second_x, first_y, second_y, first_c, second_c, window):
    size_x, size_y, size_z = own.shape
    place = here()
    odd = place[0] % 2 == 1
    low_x, high_x = got(first_x, second_x, odd)
    low_y, high_y = got(first_y, second_y, place[1] % 2 == 1)
    low_c, high_c = got(first_c, second_c, odd)
    assemble_own(window.at[FINE : FINE + size_x], own, low_y, high_y, 0, 0)
    assemble_side(window, FINE - 4, 4, (size_y, size_z), low_x, 0, low_c, 0, 3, True)
    assemble_side(window, FINE + size_x, 4, (size_y, size_z), high_x, 0, high_c, 0, 3, False)


def last_kernel(
    count_x, count_y, own_half, other_half, low_iterate, mid_coeffs, goal_in, fine_coeffs, window,
    out,
    goal, mid_iterate, mid_update,
    iterate, update,
):
    size_x, size_y, size_z = out.shape
    mid_x, mid_y, mid_z = size_x // 2, size_y // 2, size_z // 2
    last = size_x + 2 * FINE - 2
    coeffs = Stack((2, last, fine_coeffs, 0))
    me_x, me_y = here()
    even = me_x % 2 == 0

    def half(which, device, tile):
        one, two = own_half[device, tile], other_half[device, tile]
        return jnp.where(even, one, two) if which == 0 else jnp.where(even, two, one)

    def device(dx, dy):
        return lax.rem(me_x + dx + count_x, count_x) * count_y + lax.rem(me_y + dy + count_y, count_y)

    first, far = MID - mid_x, MID + 2 * mid_x
    for dy in (-1, 0, 1):
        rows = slice((dy + 1) * mid_y, (dy + 2) * mid_y)
        for dx in (-1, 0, 1):
            source = device(dx, dy)
            start = MID + dx * mid_x
            for plane in range(mid_x):
                mid_iterate[start + plane, rows] = half(plane // 2, source, 1 + plane % 2)
        for plane in range(2):
            mid_iterate[plane, rows] = own_half[device(-2, dy), 1 + plane]
            mid_iterate[far + plane, rows] = own_half[device(2, dy), 1 + plane]
    low_planes, low_size_y = low_iterate.shape[:2]
    low_size_x = 2 * low_planes
    low_y = mid_y // 2
    turn = lax.rem(low_size_y - me_y * low_y + low_y, low_size_y)
    for plane in range((mid_x + 2 * MID) // 2):
        at = lax.rem(me_x * (mid_x // 2) - MID // 2 + plane + low_size_x, low_size_x)
        turned = pltpu.roll(low_iterate[lax.rem(at, low_planes)], turn, 0)
        side = at // low_planes
        one, two = lanes_spread(turned[: TILE[0]], side), lanes_spread(turned[TILE[0] : 2 * TILE[0]], side)
        part = jnp.concatenate([rows_spread(one, 0), rows_spread(one, 1), rows_spread(two, 0)], axis=0)
        mid_iterate[2 * plane] += part
        mid_iterate[2 * plane + 1] += part

    left = iota(TILE, 1) < TILE[1] // 2
    for plane in range(first, far):
        goal[plane] = goal_in[plane]
    for dy in (-1, 0, 1):
        rows = slice((dy + 1) * mid_y, (dy + 2) * mid_y)
        for plane, dx in ((first - 1, -2), (far, 2)):
            source = device(dx, dy)
            edge = jnp.where(left, roll(half(0, source, 0), TILE[1] // 2, 1), half(1, source, 0))
            goal[plane, rows] = edge * mid_coeffs[6, plane, rows]
    for sweep, pair in enumerate(chebyshev_weights(SWEEPS)):
        sweep_window(
            mid_iterate, mid_update, mid_coeffs, (first - 1 + sweep, far + 1 - sweep), pair, sweep == 0, goal
        )

    fine_low = FINE - 4
    for plane in range(mid_x + 4):
        turned = roll(mid_iterate[MID - 2 + plane], -4, 0)
        lines = []
        for r in range(2):
            tile = turned[r * TILE[0] : (r + 1) * TILE[0]]
            for side in range(2):
                line = rows_spread(tile, side)
                lines.append(jnp.concatenate([lanes_spread(line, 0), lanes_spread(line, 1)], axis=1))
        part = jnp.concatenate(lines, axis=0)
        for at in (fine_low + 2 * plane, fine_low + 2 * plane + 1):
            iterate[at] = window[at] + part
    for sweep, pair in enumerate(chebyshev_weights(SWEEPS)):
        sweep_window(
            iterate, update, coeffs, (2 + sweep, last - sweep), pair, sweep == 0
        )
    for plane in range(size_x):
        out[plane] = iterate[FINE + plane, PAD : PAD + size_y]


def call(kernel, inputs, outs, scratch=(), scalars=0, far_in=(), far_out=(), sems=0):
    def place(i):
        return pltpu.SMEM if i < scalars else pltpu.HBM if i in far_in else pltpu.VMEM

    near = [x.shape for i, x in enumerate(inputs) if i >= scalars and i not in far_in]
    near += [shape for i, shape in enumerate(outs) if i not in far_out] + list(scratch)
    used = 4 * sum(math.prod(shape) for shape in near)
    inputs = [pltpu.with_memory_space_constraint(x, pltpu.HBM) if i in far_in else x for i, x in enumerate(inputs)]
    return pl.pallas_call(
        kernel,
        out_shape=[
            pltpu.HBM(shape, F32) if i in far_out else jax.ShapeDtypeStruct(shape, F32)
            for i, shape in enumerate(outs)
        ],
        in_specs=[pl.BlockSpec(memory_space=place(i)) for i in range(len(inputs))],
        out_specs=[
            pl.BlockSpec(memory_space=pltpu.HBM if i in far_out else pltpu.VMEM) for i in range(len(outs))
        ],
        scratch_shapes=[pltpu.VMEM(shape, F32) for shape in scratch]
        + ([pltpu.SemaphoreType.DMA((sems,))] if sems > 1 else [pltpu.SemaphoreType.DMA] * sems),
        cost_estimate=pl.CostEstimate(flops=1000, bytes_accessed=1000, transcendentals=0),
        compiler_params=pltpu.CompilerParams(vmem_limit_bytes=used + used // 4 + 2 * 1024 * 1024),
    )(*inputs)


def local(source, initial, absorption, beta_x, beta_y, beta_z):
    size_x, size_y, size_z = source.shape
    mid_x, mid_y, mid_z = size_x // 2, size_y // 2, size_z // 2
    low_x, low_y = mid_x // 2, mid_y // 2
    count_x, count_y = lax.axis_size("gx"), lax.axis_size("gy")
    devices = count_x * count_y
    plane, strip = tiles_of(size_y, size_z), tiles_of(8, size_z)
    mids = 4 * mid_x

    def tiles(count):
        return (count,) + TILE

    pairs = size_x // 2
    up_x, down_x, up_y, down_y, mid, low, own = call(
        pack_kernel,
        (initial, source, absorption, beta_x, beta_y, beta_z),
        [
            tiles(sum(UP_PLANES) * plane),
            tiles(sum(DOWN_PLANES) * plane),
            tiles((6 * pairs + 1) * strip + 2 + 4 * STRIP),
            tiles((6 * pairs + 2) * strip + 2 + 4 * STRIP),
            tiles(mids),
            tiles(2),
            (6,) + source.shape,
        ],
        far_in=range(6),
        sems=6,
    )
    low_x1, high_x1 = shifted(up_x, "gx", 1), shifted(down_x, "gx", -1)
    low_y1, high_y1 = shifted(up_y, "gy", 1), shifted(down_y, "gy", -1)
    first_c1, second_c1 = call(
        functools.partial(corner_kernel, size_x, size_z),
        (low_y1, high_y1, mid, low),
        [tiles(corner_tiles(DOWN_CORNER) * strip + 16)] * 2,
    )
    first_c1, second_c1 = swapped(first_c1, second_c1, "gx")

    tall = (size_y + 2 * PAD, size_z)
    wide = (size_x + 2 * FINE,) + tall
    own_windows, own_coeffs, up_corner, down_corner, strips = call(
        own_kernel,
        (own, low_y1, high_y1),
        [(6, size_x) + tall, (8, size_x - 1) + tall, tiles(MID_CORNER), tiles(MID_CORNER), tiles(2 * mids)],
    )
    iterate, mid_target, first_x2, second_x2, first_y2, second_y2 = call(
        fine_kernel,
        (own_windows, own_coeffs, up_corner, down_corner, mid, low_x1, high_x1, first_c1, second_c1),
        [
            source.shape,
            (mid_x, mid_y, mid_z),
            tiles(4 * plane + mid_x + MID_CORNER + mids + 10 + PASSED),
            tiles(4 * plane + mid_x + MID_CORNER + mids + 10 + PASSED),
            tiles(pairs * strip + mid_x),
            tiles(pairs * strip + mid_x),
        ],
        scratch=[(6, 2 * FINE) + tall, (8, 2 * FINE + 1) + tall, wide, wide],
    )
    first_x2, second_x2 = swapped(first_x2, second_x2, "gx")
    first_y2, second_y2 = swapped(first_y2, second_y2, "gy")
    first_c2, second_c2 = call(
        functools.partial(corner_two_kernel, size_x, size_z),
        (first_y2, second_y2),
        [tiles(2 * strip + mid_x + 1)] * 2,
    )
    first_c2, second_c2 = swapped(first_c2, second_c2, "gx")

    mid_wide = (mid_x + 2 * MID, 3 * mid_y, mid_z)
    mid_coeffs, near = call(
        mid_coeffs_kernel,
        (mid, low, strips, low_y1, high_y1, first_c1, second_c1, first_x2, second_x2),
        [(8,) + mid_wide, tiles(30)],
        [(4,) + mid_wide],
    )
    (coeffs,) = call(
        fine_coeffs_kernel,
        (own, low_x1, high_x1, low_y1, high_y1, first_c1, second_c1),
        [(7, wide[0] - 4) + tall],
        [(6, size_x) + tall, (6, 2 * FINE) + tall],
    )
    goal, slots = call(
        functools.partial(mid_kernel, count_x, count_y),
        (low, mid_target, mid_coeffs, first_x2, second_x2, first_y2, second_y2, first_c2, second_c2, coeffs),
        [mid_wide, (devices, 3) + TILE],
        [mid_wide] * 3,
    )
    own_half = lax.all_to_all(slots, ("gx", "gy"), 0, 0)
    other_half = lax.ppermute(own_half, "gx", [(i, i ^ 1) for i in range(count_x)])

    (window,) = call(
        window_kernel, (iterate, first_x2, second_x2, first_y2, second_y2, first_c2, second_c2), [wide]
    )
    low_wide = (low_x * count_x // 2, low_y * count_y, mid_z)
    (low_iterate,) = call(
        functools.partial(low_kernel, count_x, count_y),
        (own_half, near),
        [low_wide],
        [(devices, 3) + TILE, (5,) + low_wide, (7,) + low_wide, low_wide],
    )
    (result,) = call(
        functools.partial(last_kernel, count_x, count_y),
        (own_half, other_half, low_iterate, mid_coeffs, goal, coeffs, window),
        [source.shape],
        [mid_wide, mid_wide, mid_wide]
        + [wide, wide],
    )
    return result


def solution(mesh):
    spec = P("gx", "gy", None)
    return jax.shard_map(
        local, mesh=mesh, in_specs=(spec,) * 6, out_specs=spec, check_vma=False
    )
```
